128 devices in a mesh: hullx: 8 (over y, z_lo), hully: 16 (over z_hi, x, core).
Axes of the slice: x: 4, y: 4, z: 4 (z_hi: 2, z_lo: 2; z = z_hi * 2 + z_lo), core: 2. Of those that a mesh axis runs over, the one named last changes fastest.
Arguments:
- velocity: float32 [3, 128, 768, 128], P(None, 'hullx', 'hully'), may hold values from -6 to 6
- pressure: float32 [128, 768, 128], P('hullx', 'hully'), may hold values from -6 to 6
- mom_source: float32 [3, 128, 768, 128], P(None, 'hullx', 'hully'), may hold values from -6 to 6
- mom_diag: float32 [128, 768, 128], P('hullx', 'hully'), may hold values from 0.5 to 8
- press_diag: float32 [128, 768, 128], P('hullx', 'hully'), may hold values from 0.05 to 2
- agglomeration: int32 [128, 768, 128], P('hullx', 'hully'), may hold values from 0 to 32767, as said below
- coarse_blocks: float32 [256, 2, 128, 128], P('hully'), as said below
- coarse_columns: int32 [256, 2], P('hully'), may hold values from 0 to 255, as said below
- wake_cells: int32 [32768], P(('hullx', 'hully')), may hold values from 0 to 98303
- wake_sections: int32 [32768], P(('hullx', 'hully')), may hold values from 0 to 1023
- wake_weights: float32 [32768], P(('hullx', 'hully')), may hold values from 0 to 0.3
- chord: float32 [1024], P(('hullx', 'hully')), may hold values from 0.2 to 1
- radius: float32 [1024], P(('hullx', 'hully')), may hold values from 0.2 to 1
- influence: float32 [1024, 1024], P(('hullx', 'hully')), may hold values from -0.1875 to 0.1875
- resistance: float32 [1], replicated, may hold values from 0.2 to 1.2
- body_cells: int32 [65536], P(('hullx', 'hully')), may hold values from 0 to 98303
- body_sections: int32 [65536], P(('hullx', 'hully')), may hold values from 0 to 1023
- body_weights: float32 [65536], P(('hullx', 'hully')), may hold values from 0.5 to 2
Outputs:
- velocity_new: float32 [3, 128, 768, 128], P(None, 'hullx', 'hully')
- pressure_new: float32 [128, 768, 128], P('hullx', 'hully')
- section_force: float32 [1024], P(('hullx', 'hully'))
The draws below stay inside these ranges and needn't reach their ends.
Inputs may be any that keep to these rules, and one draw needn't show every extreme that they name: The agglomeration of the cell (i, j, k) differs by at most 3 from ((i * 768 + j) * 128 + k) // 384. coarse_columns[r][0] = r and coarse_columns[r][1] is another block row. coarse_blocks[r][0] holds the diagonal block of block row r.
All inputs are finite; a program needn't handle non-finite values.
Results may differ from the reference program's by a relative error of at most 0.00011.
Values sent between devices are 32-bit elements; how exact they have to be, the bound alone decides.
No kernel may reach another device: no remote copies, remote signals or barrier semaphores. Data moves between devices by JAX's collectives and lax.ppermute only.
A program may use at most 128 MiB of HBM per device.

```python
import math
import jax
import jax.numpy as jnp
from jax import lax

CX = 16
CY = 48
CZ = 128
KB = 2
WS = 256
BF = 512
TRIM = 2
NX = 128
NY = 768
CELLS_DEV = 98304
NCB = 256
NC = 32768
NSEC = 1024
N_HULLY = 16
DEVICES = 128


def draw_agglomeration(key, part):
    key = jax.random.fold_in(key, 11)
    first_key, second_key = jax.random.split(key)
    total = NX * NY * CZ
    group = total // NC
    flat = jnp.arange(total, dtype=jnp.int32)
    base = flat // group
    moved = jax.random.randint(first_key, (total,), -3, 4, dtype=jnp.int32)
    picked = jax.random.randint(second_key, (total,), 0, 4, dtype=jnp.int32)
    shifted = jnp.clip(base + moved, 0, NC - 1)
    return jnp.where(picked == 0, shifted, base).reshape(NX, NY, CZ).astype(jnp.int32)


def draw_coarse_blocks(key, part):
    key = jax.random.fold_in(key, 21)
    noise_key, diag_key, couple_key = jax.random.split(key, 3)
    noise = jax.random.uniform(noise_key, (NCB, KB, 128, 128), jnp.float32, -0.5 / 128.0, 0.5 / 128.0)
    couple = jax.random.uniform(couple_key, (NCB, KB, 128, 128), jnp.float32, 0.5, 1.0)
    diagonal = jax.random.uniform(diag_key, (NCB, 128), jnp.float32, 5.5, 9.0)
    rows = jnp.arange(128, dtype=jnp.int32)[:, None]
    cols = jnp.arange(128, dtype=jnp.int32)[None, :]
    identity = (rows == cols).astype(jnp.float32)
    own_band = ((cols == (rows + 1) % 128) | (cols == (rows + 127) % 128)).astype(jnp.float32)
    other_band = ((cols == rows) | (cols == (rows + 37) % 128)).astype(jnp.float32)
    leading = noise[:, 0] * (1.0 - identity) - couple[:, 0] * own_band + diagonal[:, :, None] * identity
    trailing = noise[:, 1] - couple[:, 1] * other_band
    return jnp.stack([leading, trailing], axis=1).astype(jnp.float32)


def draw_coarse_columns(key, part):
    key = jax.random.fold_in(key, 31)
    rows = jnp.arange(NCB, dtype=jnp.int32)
    offset = jax.random.randint(key, (NCB,), 1, NCB, dtype=jnp.int32)
    return jnp.stack([rows, (rows + offset) % NCB], axis=1).astype(jnp.int32)


def plant(drawn, stream_key, least, high):
    longest = drawn.shape.index(max(drawn.shape))
    spots = []
    for shift in (0, 1):
        where = [jax.random.randint(jax.random.fold_in(stream_key, axis), (), 0, length) for axis, length in enumerate(drawn.shape)]
        where[longest] = (where[longest] + shift) % drawn.shape[longest]
        spots.append(tuple(where))
    return drawn.at[spots[0]].set(least).at[spots[1]].set(high)


def block_scale(key, shape, cuts, low, largest):
    level, own = 1.0, jax.random.fold_in(key, 6)
    for dim, shards_of in cuts:
        draws = jnp.exp(jax.random.uniform(jax.random.fold_in(own, dim), (shards_of,), jnp.float32, low / len(cuts), largest / len(cuts)))
        level = level * jnp.repeat(draws, shape[dim] // shards_of).reshape([-1 if axis == dim else 1 for axis in range(len(shape))])
    return level


def centred(rng, shape, width, reach, shards=(), kind=jnp.bfloat16):
    array = jax.random.normal(rng, shape, jnp.float32) * width
    if len(shards) > 0:
        array = block_scale(rng, shape, shards, -0.22, 0.18) * array
    return jnp.clip(array, min=-reach, max=reach).astype(kind)


def setup_inputs(seed: int = 0) -> dict:
    splits = jax.random.split(jax.random.key(seed), 19)
    return {
        "velocity": centred(splits[0], (3, NX, NY, CZ), 1.0, 6.0, ((1, 8), (2, 16)), jnp.float32),
        "pressure": centred(splits[1], (NX, NY, CZ), 1.0, 6.0, ((0, 8), (1, 16)), jnp.float32),
        "mom_source": centred(splits[2], (3, NX, NY, CZ), 1.0, 6.0, ((1, 8), (2, 16)), jnp.float32),
        "mom_diag": jnp.clip(jnp.exp(math.log(8.0) - 2.7725887 * jax.random.uniform(splits[3], (NX, NY, CZ), jnp.float32) ** block_scale(splits[3], (NX, NY, CZ), ((0, 8), (1, 16)), -0.2, 0.2)), 0.5, 8.0),
        "press_diag": jnp.clip(jnp.exp(math.log(2.0) - 3.6888794 * jax.random.uniform(splits[4], (NX, NY, CZ), jnp.float32) ** block_scale(splits[4], (NX, NY, CZ), ((0, 8), (1, 16)), -0.2, 0.2)), 0.05, 2.0),
        "agglomeration": draw_agglomeration(jax.random.fold_in(splits[18], 71), 0),
        "coarse_blocks": draw_coarse_blocks(jax.random.fold_in(splits[18], 71), 0),
        "coarse_columns": draw_coarse_columns(jax.random.fold_in(splits[18], 71), 0),
        "wake_cells": plant(jax.random.randint(splits[8], (DEVICES * WS,), 0, CELLS_DEV), jax.random.fold_in(splits[8], 1), 0, CELLS_DEV - 1).astype(jnp.int32),
        "wake_sections": plant(jax.random.randint(splits[9], (DEVICES * WS,), 0, NSEC), jax.random.fold_in(splits[9], 1), 0, NSEC - 1).astype(jnp.int32),
        "wake_weights": jnp.clip(0.3 * jax.random.uniform(splits[10], (DEVICES * WS,), jnp.float32) ** block_scale(splits[10], (DEVICES * WS,), ((0, 128),), -0.2, 0.2), 0.0, 0.3),
        "chord": jnp.clip(jnp.exp(math.log(1.0) - 1.609438 * jax.random.uniform(splits[11], (NSEC,), jnp.float32) ** block_scale(splits[11], (NSEC,), ((0, 128),), -0.2, 0.2)), 0.2, 1.0),
        "radius": jnp.clip(0.2 + 0.8 * jax.random.uniform(splits[12], (NSEC,), jnp.float32) ** block_scale(splits[12], (NSEC,), ((0, 128),), -0.2, 0.2), 0.2, 1.0),
        "influence": centred(splits[13], (NSEC, NSEC), NSEC ** -0.5, 0.1875, ((0, 128),), jnp.float32),
        "resistance": jnp.clip(jax.random.uniform(splits[14], (1,), jnp.float32, 0.2, 1.2), 0.2, 1.2),
        "body_cells": plant(jax.random.randint(splits[15], (DEVICES * BF,), 0, CELLS_DEV), jax.random.fold_in(splits[15], 1), 0, CELLS_DEV - 1).astype(jnp.int32),
        "body_sections": plant(jax.random.randint(splits[16], (DEVICES * BF,), 0, NSEC), jax.random.fold_in(splits[16], 1), 0, NSEC - 1).astype(jnp.int32),
        "body_weights": jnp.clip(0.5 + 1.5 * jax.random.uniform(splits[17], (DEVICES * BF,), jnp.float32) ** block_scale(splits[17], (DEVICES * BF,), ((0, 128),), -0.2, 0.2), 0.5, 2.0),
    }


jacobi_weight = 0.8
trim_gain = 0.5
pressure_relax = 0.7


def neighbour_sum(padded):
    total = padded[..., 2:, 1:-1, 1:-1] + padded[..., :-2, 1:-1, 1:-1]
    total = total + padded[..., 1:-1, 2:, 1:-1] + padded[..., 1:-1, :-2, 1:-1]
    return total + padded[..., 1:-1, 1:-1, 2:] + padded[..., 1:-1, 1:-1, :-2]


def gradient(padded):
    along_x = 0.5 * (padded[2:, 1:-1, 1:-1] - padded[:-2, 1:-1, 1:-1])
    along_y = 0.5 * (padded[1:-1, 2:, 1:-1] - padded[1:-1, :-2, 1:-1])
    along_z = 0.5 * (padded[1:-1, 1:-1, 2:] - padded[1:-1, 1:-1, :-2])
    return jnp.stack([along_x, along_y, along_z])


def divergence(padded):
    total = 0.5 * (padded[0, 2:, 1:-1, 1:-1] - padded[0, :-2, 1:-1, 1:-1])
    total = total + 0.5 * (padded[1, 1:-1, 2:, 1:-1] - padded[1, 1:-1, :-2, 1:-1])
    return total + 0.5 * (padded[2, 1:-1, 1:-1, 2:] - padded[2, 1:-1, 1:-1, :-2])


def coarse_apply(blocks, columns, vector):
    pieces = vector.reshape(-1, 128)[columns]
    return jnp.einsum("rkij,rkj->ri", blocks, pieces, precision=lax.Precision.HIGHEST).reshape(-1)


def coarse_diagonal(blocks):
    identity = jnp.eye(128, dtype=jnp.float32)
    return jnp.sum(blocks[:, 0] * identity, axis=2).reshape(-1)


def smooth(correction, padded, target, denominator):
    applied = denominator * correction - neighbour_sum(padded)
    return correction + jacobi_weight * (target - applied) / denominator


def pad_scalar(field):
    return jnp.pad(field, 1)


def pad_vector(field):
    return jnp.pad(field, ((0, 0), (1, 1), (1, 1), (1, 1)))


def place(cells, count):
    device = jnp.arange(cells.shape[0], dtype=jnp.int32) // count
    row_x = (device // N_HULLY) * CX + cells // (CY * CZ)
    row_y = (device % N_HULLY) * CY + (cells // CZ) % CY
    return row_x, row_y, cells % CZ


def reference(velocity, pressure, mom_source, mom_diag, press_diag, agglomeration, coarse_blocks, coarse_columns, wake_cells, wake_sections, wake_weights, chord, radius, influence, resistance, body_cells, body_sections, body_weights):
    wake_x, wake_y, wake_z = place(wake_cells, WS)
    samples = velocity[0][wake_x, wake_y, wake_z] * wake_weights
    wake = jax.ops.segment_sum(samples, wake_sections, num_segments=NSEC)
    omega = jnp.ones((), jnp.float32)
    induced = jnp.zeros((NSEC,), jnp.float32)
    for step in range(TRIM):
        circulation = chord * (omega * radius - wake - induced)
        thrust = jnp.sum(circulation * radius) / NSEC
        omega = omega + trim_gain * (resistance[0] - thrust)
        induced = jnp.dot(influence, circulation, precision=lax.Precision.HIGHEST)
    circulation = chord * (omega * radius - wake - induced)
    section_force = circulation * omega * radius
    body_x, body_y, body_z = place(body_cells, BF)
    body_force = jnp.zeros((NX, NY, CZ), jnp.float32).at[body_x, body_y, body_z].add(body_weights * section_force[body_sections])
    source = mom_source - gradient(pad_scalar(pressure))
    source = source.at[0].add(body_force)
    denominator = 6.0 + mom_diag
    predicted = velocity
    for step in range(2):
        predicted = (source + neighbour_sum(pad_vector(predicted))) / denominator
    target = -divergence(pad_vector(predicted))
    press_denominator = 6.0 + press_diag
    correction = jacobi_weight * target / press_denominator
    correction = smooth(correction, pad_scalar(correction), target, press_denominator)
    residual = target - (press_denominator * correction - neighbour_sum(pad_scalar(correction)))
    rescale = (NX * NY * CZ / NC) ** -0.5
    coarse_residual = jax.ops.segment_sum(residual.reshape(-1), agglomeration.reshape(-1), num_segments=NC) * rescale
    diagonal = coarse_diagonal(coarse_blocks)
    first = jacobi_weight * coarse_residual / diagonal
    second = first + jacobi_weight * (coarse_residual - coarse_apply(coarse_blocks, coarse_columns, first)) / diagonal
    correction = correction + second[agglomeration]
    for step in range(2):
        correction = smooth(correction, pad_scalar(correction), target, press_denominator)
    velocity_new = predicted - gradient(pad_scalar(correction))
    pressure_new = pressure + pressure_relax * correction
    return velocity_new, pressure_new, section_force
```

```python
import numpy as np
import jax
import jax.numpy as jnp
from jax import lax
from jax.experimental import pallas as pl
from jax.experimental.pallas import tpu as pltpu
from jax.sharding import PartitionSpec as P

HX, HY = 8, 16
CX, CY, CZ = 16, 48, 128
NSEC = 1024
BOTH = ("hullx", "hully")
F32, BF16, I32 = jnp.float32, jnp.bfloat16, jnp.int32
HIGH = lax.Precision.HIGHEST
YE = 64
EN = 9 * 512

VM = pl.BlockSpec(memory_space=pltpu.VMEM)
SM = pl.BlockSpec(memory_space=pltpu.SMEM)
PARAMS = pltpu.CompilerParams(vmem_limit_bytes=48 * 1024 * 1024)


def iota(shape, dim):
    return lax.broadcasted_iota(I32, shape, dim)


def split2(x):
    hi = x.astype(BF16)
    lo = (x - hi.astype(F32)).astype(BF16)
    return hi, lo


def split3(x):
    hi = x.astype(BF16)
    rest = x - hi.astype(F32)
    mid = rest.astype(BF16)
    lo = (rest - mid.astype(F32)).astype(BF16)
    return hi, mid, lo


def nt(a, b, precision=None):
    return lax.dot_general(a, b, (((1,), (1,)), ((), ())), precision=precision, preferred_element_type=F32)


def mm(a, b, precision=None):
    return lax.dot_general(a, b, (((1,), (0,)), ((), ())), precision=precision, preferred_element_type=F32)


def lane_row(column, start):
    spot = iota((8, 128), 1) == iota((8, 128), 0) + start
    return jnp.sum(jnp.where(spot, column, 0.0), axis=0, keepdims=True)


def total(x):
    return jnp.sum(jnp.sum(x, axis=1, keepdims=True), axis=0, keepdims=True)


def zdiff_parts(v):
    lane = iota(v.shape, 1)
    before = jnp.where(lane == 0, 0.0, pltpu.roll(v, 1, 1))
    after = jnp.where(lane == CZ - 1, 0.0, pltpu.roll(v, CZ - 1, 1))
    return before, after


def y_parts(v):
    return pltpu.roll(v, 1, 0), pltpu.roll(v, v.shape[0] - 1, 0)


def s_yz(v):
    a, b = y_parts(v)
    c, d = zdiff_parts(v)
    return (a + b) + (c + d)


def wake_kernel(ids, cols, v_ref, wc, ws, ww, chord, radius, ab, out, row):
    hx, hy = ids[0], ids[1]
    cells = wc[...]
    place = cells >> 7
    spot = (iota((768, 256), 0) == place).astype(BF16)
    picked = jnp.zeros((128, 256), F32)
    for part in split3(v_ref[0]):
        picked = picked + lax.dot_general(part, spot, (((0,), (0,)), ((), ())), preferred_element_type=F32)
    samples = jnp.sum(jnp.where(iota((128, 256), 0) == (cells & 127), picked, 0.0), axis=0, keepdims=True) * ww[...]
    sec = ws[...]
    high = jnp.where(iota((8, 256), 0) == (sec >> 7), samples, 0.0)
    low = (iota((128, 256), 0) == (sec & 127)).astype(F32)
    row[0:8, :] = nt(high, low, HIGH)
    crow = lane_row(chord[...], 8 * hy)
    rrow = lane_row(radius[...], 8 * hy)
    lane = iota((1, 128), 1)
    c0 = cols[2 * hx, 1].astype(F32)
    c1 = cols[2 * hx + 1, 1].astype(F32)
    colrow = jnp.where(lane == 0, c0, jnp.where(lane == 1, c1, 0.0))
    eye = iota((128, 128), 0) == iota((128, 128), 1)
    d0 = jnp.sum(jnp.where(eye, ab[0, 0], 0.0), axis=0, keepdims=True)
    d1 = jnp.sum(jnp.where(eye, ab[1, 0], 0.0), axis=0, keepdims=True)
    row[8:16, :] = jnp.concatenate([crow, rrow, colrow, d0, d1, jnp.zeros((3, 128), F32)], axis=0)
    out[...] = jnp.broadcast_to(row[...][None], out.shape)


def trim1_kernel(ids, recv, infl, out, state, cols, grouped):
    hy = ids[1]
    wake = jnp.sum(recv[:, 0:8, :], axis=0)
    rest = recv[:, 8:16, :]
    grouped[...] = jnp.sum(rest.reshape(HX, HY, 8, 128), axis=1)
    chord = grouped[:, 0, :]
    radius = grouped[:, 1, :]
    cols[...] = recv[:, 10, :]
    state[0] = wake
    state[1] = chord
    state[2] = radius
    circ = chord * (radius - wake)
    acc = infl[:, 0:128] * circ[0:1, :]
    for c in range(1, 8):
        acc = acc + infl[:, c * 128 : (c + 1) * 128] * circ[c : c + 1, :]
    row = lane_row(jnp.sum(acc, axis=1, keepdims=True), 8 * hy)
    out[...] = jnp.broadcast_to(row, out.shape)


def trim2_kernel(ids, res, recv, state, infl, out, force):
    hx, hy = ids[0], ids[1]
    induced = jnp.sum(recv[...].reshape(HX, HY, 128), axis=1)
    wake, chord, radius = state[0], state[1], state[2]
    circ = chord * (radius - wake)
    omega = 1.0 + 0.5 * (res[0] - total(circ * radius) * (1.0 / NSEC))
    circ = chord * (omega * radius - wake - induced)
    omega = omega + 0.5 * (res[0] - total(circ * radius) * (1.0 / NSEC))
    acc = infl[:, 0:128] * circ[0:1, :]
    for c in range(1, 8):
        acc = acc + infl[:, c * 128 : (c + 1) * 128] * circ[c : c + 1, :]
    induced2 = lane_row(jnp.sum(acc, axis=1, keepdims=True), 8 * hy)
    mine = (iota((8, 128), 0) == hx) & ((iota((8, 128), 1) >> 3) == hy)
    full = chord * (omega * radius - wake - induced2) * omega * radius
    row = jnp.sum(jnp.where(mine, full, 0.0), axis=0, keepdims=True)
    force[...] = row
    out[...] = jnp.broadcast_to(row, out.shape)


def own_s_yz(v, ylo, yhi):
    r = iota(v.shape, 0)
    up = jnp.where(r == 0, ylo, pltpu.roll(v, 1, 0))
    down = jnp.where(r == CY - 1, yhi, pltpu.roll(v, CY - 1, 0))
    c, d = zdiff_parts(v)
    return (up + down) + (c + d)


def sweep1_kernel(vel, pres, src, mdiag, xlo, xhi, ylo, yhi, pred, source, vext):
    for c in range(3):
        vext[c, 1 : CX + 1] = vel[c]
    vext[3, 1 : CX + 1] = pres[...]
    vext[:, 0:1] = xlo[...][:, None]
    vext[:, CX + 1 : CX + 2] = xhi[...][:, None]

    def body(x, carry):
        inv = 1.0 / (6.0 + mdiag[x])
        p = vext[3, x + 1]
        gx = 0.5 * (vext[3, x + 2] - vext[3, x])
        r = iota(p.shape, 0)
        up = jnp.where(r == 0, ylo[3, pl.ds(x, 1), :], pltpu.roll(p, 1, 0))
        down = jnp.where(r == CY - 1, yhi[3, pl.ds(x, 1), :], pltpu.roll(p, CY - 1, 0))
        before, after = zdiff_parts(p)
        grads = (gx, 0.5 * (down - up), 0.5 * (after - before))
        for c in range(3):
            s = src[c, x] - grads[c]
            source[c, x] = s
            v = vext[c, x + 1]
            around = vext[c, x] + vext[c, x + 2] + own_s_yz(v, ylo[c, pl.ds(x, 1), :], yhi[c, pl.ds(x, 1), :])
            pred[c, x] = (s + around) * inv
        return carry

    lax.fori_loop(0, CX, body, 0)


def sweep2_kernel(pred, source, mdiag, xlo, xhi, ylo, yhi, out, vext):
    for c in range(3):
        vext[c, 1 : CX + 1] = pred[c]
    vext[:, 0:1] = xlo[...][:, None]
    vext[:, CX + 1 : CX + 2] = xhi[...][:, None]

    def body(x, carry):
        inv = 1.0 / (6.0 + mdiag[x])
        for c in range(3):
            v = vext[c, x + 1]
            around = vext[c, x] + vext[c, x + 2] + own_s_yz(v, ylo[c, pl.ds(x, 1), :], yhi[c, pl.ds(x, 1), :])
            out[c, x] = (source[c, x] + around) * inv
        return carry

    lax.fori_loop(0, CX, body, 0)


def body_parts():
    return [(sx, sy) for sy in (0, -1, 1) for sx in (0, -1, 1)]


def body_kernel(
    ids, recv, ecell, esec, ewt, p0, p1, p2, invd, invp, pdiag, acode, cols, gfold,
    pred0, target, corr1, send,
    b, dp, pr0, corr0, acc,
):
    hx, hy = ids[0], ids[1]
    force = jnp.sum(recv[...].reshape(HX, HY, 128), axis=1)
    sec = esec[...].astype(I32)
    low = (iota((128, EN), 0) == (sec & 127)).astype(BF16)
    got = mm(jnp.concatenate(split3(force), axis=0), low)
    got = got[0:8] + got[8:16] + got[16:24]
    val = jnp.sum(jnp.where(iota((8, EN), 0) == (sec >> 7), got, 0.0), axis=0, keepdims=True) * ewt[...]
    cell = ecell[...].astype(I32)
    cz = cell & 127
    place = cell >> 7
    cx = (place * 43691) >> 21
    cy = place - 48 * cx
    zv = jnp.where(iota((128, EN), 0) == cz, val, 0.0)
    zh, zl = split2(zv)
    for k, (sx, sy) in enumerate(body_parts()):
        lanes = slice(k * 512, (k + 1) * 512)
        x, y = cx[:, lanes], cy[:, lanes]
        planes = CX if sx == 0 else 4
        first = {0: 4, -1: 0, 1: 20}[sx]
        x = x - 12 if sx < 0 else x
        inside = (x >= 0) & (x < planes)
        if sy == 0:
            r = jnp.where(inside, x * YE + y + 8, -1)
            rows = planes * YE
        else:
            y = y - 40 if sy < 0 else y
            inside = inside & (y >= 0) & (y < 8)
            r = jnp.where(inside, x * 8 + y, -1)
            rows = planes * 8
        spot = (iota((rows, 512), 0) == r).astype(BF16)
        part = nt(spot, zh[:, lanes]) + nt(spot, zl[:, lanes])
        if sy == 0:
            b[first : first + planes] = part.reshape(planes, YE, 128)
        else:
            at = 0 if sy < 0 else 56
            b[first : first + planes, at : at + 8] = b[first : first + planes, at : at + 8] + part.reshape(planes, 8, 128)

    def s1(p, carry):
        dp[p] = b[p] * invd[p]
        return carry

    lax.fori_loop(0, 24, s1, 0)

    def s2(p, carry):
        d = (b[p] + dp[p - 1] + dp[p + 1] + s_yz(dp[p])) * invd[p]
        pr0[p - 1] = p0[p - 1] + d
        return carry

    lax.fori_loop(1, 23, s2, 0)

    def s3(t, carry):
        ya, yb = y_parts(p1[t])
        za, zb = zdiff_parts(p2[t])
        tg = -0.5 * ((pr0[t + 2] - pr0[t]) + (yb - ya) + (zb - za))
        target[t] = tg
        corr0[t] = 0.8 * tg * invp[t]
        return carry

    lax.fori_loop(0, 20, s3, 0)

    def s4(c, carry):
        t = c + 1
        v = corr0[t]
        corr1[c] = 0.2 * v + 0.8 * (target[t] + corr0[t - 1] + corr0[t + 1] + s_yz(v)) * invp[t]
        return carry

    lax.fori_loop(0, 18, s4, 0)
    acc[...] = jnp.zeros(acc.shape, F32)

    def s5(x, carry):
        pred0[x] = pr0[x + 3, 8:56, :]
        v = corr1[x + 1]
        full = target[x + 2] + corr1[x] + corr1[x + 2] + s_yz(v)
        res = full[8:56] - (6.0 + pdiag[x]) * v[8:56]
        code = acode[x]
        parts = [jnp.where(code == float(d + 1), res, 0.0) for d in range(7)]
        stacked = jnp.concatenate(parts, axis=0)
        hi, lo = split2(stacked)
        both = jnp.concatenate([hi, lo], axis=1)
        pick = (iota((256, 128), 1) == x).astype(BF16)
        acc[...] += mm(both, pick)
        return carry

    lax.fori_loop(0, CX, s5, 0)
    window = mm(gfold[...], acc[...], HIGH) * float(384.0**-0.5)
    blank = jnp.zeros((32, 128), F32)
    spread = jnp.concatenate(
        [jnp.concatenate([window if j == q else blank for j in range(4)], axis=1) for q in range(4)], axis=0
    )
    m = iota((128, 1), 0)
    plane = 8 * (m & 15) + (m >> 4)
    c0 = cols[:, 0:1].astype(I32)
    c1 = cols[:, 1:2].astype(I32)
    lane = iota((128, 128), 1)
    wants = []
    for blk in (2 * plane, 2 * plane + 1, c0, c1):
        half = blk & 1
        pln = blk >> 1
        pln = pln - jnp.where((half == 0) & (hy == HY - 1), 1, 0) + jnp.where((half == 1) & (hy == 0), 1, 0)
        at = pln - CX * hx
        at = jnp.where((at >= 0) & (at < CX), at, -1)
        wants.append((lane == at).astype(F32))
    send[...] = nt(jnp.concatenate(wants, axis=1), spread, HIGH)


def coarse_kernel(ids, half, recv, ab, diag, place, fold, out):
    z = jnp.sum(recv[...].reshape(HX, HY, 128), axis=0)
    y = mm(z, place[...], HIGH)
    lane = iota((HY, 128), 1)
    hys = iota((HY, 128), 0)
    rows = []
    for q in range(4):
        slot = (lane + 4 + 128 * half[q] - 16 * hys) & 255
        a = jnp.where(slot < 16, y[:, (2 * q) * 128 : (2 * q + 1) * 128], 0.0)
        b = jnp.where((slot >= 16) & (slot < 24), y[:, (2 * q + 1) * 128 : (2 * q + 2) * 128], 0.0)
        rows.append(jnp.sum(a + b, axis=0, keepdims=True))
    res = jnp.concatenate(rows + [jnp.zeros((4, 128), F32)], axis=0)
    first = 0.8 * res / diag[...]
    seconds = []
    for i in range(2):
        applied = nt(first, ab[i, 0], HIGH)[i : i + 1] + nt(first, ab[i, 1], HIGH)[2 + i : 3 + i]
        seconds.append(first[i : i + 1] + 0.8 * (res[i : i + 1] - applied) / diag[i : i + 1, :])
    second = jnp.concatenate(seconds, axis=1)
    lane2 = iota((HY, 256), 1)
    slot = (lane2 + 4 - 16 * iota((HY, 256), 0)) & 255
    wide = jnp.broadcast_to(second, (HY, 256))
    d0 = jnp.where(slot < 16, wide, 0.0)
    d1 = jnp.where((slot >= 16) & (slot < 24), wide, 0.0)
    windows = mm(jnp.concatenate([d0, d1], axis=1), fold[...], HIGH)
    for i in range(HX):
        out[i * HY : (i + 1) * HY, :] = windows


def last_kernel(ids, recv, corr1, target, invp, acode, pred0, pred1, pred2, pres, glift, vel_out, pres_out, win, c2, s1, s2):
    hx, hy = ids[0], ids[1]
    for i in range(24):
        p = jnp.clip(CX * hx - 4 + i, 0, 127)
        m = (p & 7) * HY + (p >> 3)
        win[i : i + 1, :] = recv[pl.ds(m, 1), :]
    w = win[0:24, :]
    lane = iota((24, 128), 1)
    w = jnp.where((lane < 4) & (hy == 0), pltpu.roll(w, 1, 0), w)
    w = jnp.where((lane >= 20) & (lane < 24) & (hy == HY - 1), pltpu.roll(w, 23, 0), w)
    win[0:24, :] = w
    win[24:128, :] = jnp.zeros((104, 128), F32)
    wt = win[...].T
    win[...] = wt

    def lift(i, carry):
        column = jnp.sum(jnp.where(iota((32, 128), 1) == i + 1, win[0:32, :], 0.0), axis=1, keepdims=True)
        wide = jnp.broadcast_to(column, (32, 128))
        v = mm(glift[...], jnp.concatenate(split3(wide), axis=0))
        code = acode[i]
        lifted = jnp.zeros((YE, 128), F32)
        for d in range(7):
            lifted = jnp.where(code == float(d + 1), v[d * YE : (d + 1) * YE], lifted)
        c2[i] = corr1[i] + lifted
        return carry

    lax.fori_loop(0, 22, lift, 0)

    def sweep1(t, carry):
        v = c2[t + 1]
        s1[t] = 0.2 * v + 0.8 * (target[t] + c2[t] + c2[t + 2] + s_yz(v)) * invp[t]
        return carry

    lax.fori_loop(0, 20, sweep1, 0)

    def sweep2(c, carry):
        v = s1[c + 1]
        s2[c] = 0.2 * v + 0.8 * (target[c + 1] + s1[c] + s1[c + 2] + s_yz(v)) * invp[c + 1]
        return carry

    lax.fori_loop(0, 18, sweep2, 0)

    def finish(x, carry):
        v = s2[x + 1]
        ya, yb = y_parts(v)
        za, zb = zdiff_parts(v)
        vel_out[0, x] = pred0[x] - 0.5 * (s2[x + 2] - s2[x])[8:56]
        vel_out[1, x] = pred1[x] - 0.5 * (yb - ya)[8:56]
        vel_out[2, x] = pred2[x] - 0.5 * (zb - za)[8:56]
        pres_out[x] = pres[x] + 0.7 * v[8:56]
        return carry

    lax.fori_loop(0, CX, finish, 0)


def tables():
    y = np.arange(CY)
    gfold = np.zeros((32, 7 * CY), np.float32)
    for d in range(7):
        gfold[y // 3 + d + 1, d * CY + y] = 1.0
    glift = np.zeros((7 * YE, 96), np.float32)
    for d in range(7):
        for yy in range(YE):
            slot = (yy - 8) // 3 + d + 1
            if 0 <= slot < 32:
                for part in range(3):
                    glift[d * YE + yy, part * 32 + slot] = 1.0
    place = np.zeros((128, 1024), np.float32)
    lanes = np.arange(128)
    for q in range(4):
        s = (lanes + 4) % 16
        place[q * 32 + s, (2 * q) * 128 + lanes] = 1.0
        ok = s < 8
        place[q * 32 + 16 + s[ok], (2 * q + 1) * 128 + lanes[ok]] = 1.0
    fold = np.zeros((512, 128), np.float32)
    lanes = np.arange(256)
    s = (lanes + 4) % 16
    fold[lanes, s] = 1.0
    ok = s < 8
    fold[256 + lanes[ok], 16 + s[ok]] = 1.0
    return gfold, glift, place, fold


def shift(x, axis, by):
    n = HX if axis == "hullx" else HY
    return lax.ppermute(x, axis, [(i, i + by) for i in range(n) if 0 <= i + by < n])


def to_all(x):
    return lax.all_to_all(x, BOTH, 0, 0, tiled=True)


def shp(*dims, dtype=F32):
    return jax.ShapeDtypeStruct(dims, dtype)


def local(
    velocity, pressure, mom_source, mom_diag, press_diag, agglomeration, coarse_blocks, coarse_columns,
    wake_cells, wake_sections, wake_weights, chord, radius, influence, resistance,
    body_cells, body_sections, body_weights,
):
    hx, hy = lax.axis_index("hullx"), lax.axis_index("hully")
    ids = jnp.stack([hx, hy]).astype(I32)
    gfold, glift, place, fold = (jnp.asarray(t) for t in tables())
    ab = lax.dynamic_slice(coarse_blocks, (2 * hx, 0, 0, 0), (2, 2, 128, 128))

    payload = pl.pallas_call(
        wake_kernel,
        grid=(1,),
        out_shape=shp(128, 16, 128),
        in_specs=[SM, SM, pl.BlockSpec((1, 768, 128), lambda i: (0, 0, 0))] + [VM] * 6,
        out_specs=VM,
        scratch_shapes=[pltpu.VMEM((16, 128), F32)],
        compiler_params=PARAMS,
        name="wake",
    )(
        ids, coarse_columns, velocity.reshape(3, 768, 128), wake_cells[None], wake_sections[None], wake_weights[None],
        chord[:, None], radius[:, None], ab,
    )
    recv1 = to_all(payload)
    out1, state, cols = pl.pallas_call(
        trim1_kernel,
        out_shape=(shp(128, 128), shp(3, 8, 128), shp(128, 128)),
        in_specs=[SM, VM, VM],
        out_specs=(VM, VM, VM),
        scratch_shapes=[pltpu.VMEM((8, 8, 128), F32)],
        compiler_params=PARAMS,
        name="trim1",
    )(ids, recv1, influence)
    recv2 = to_all(out1[:, None, :])[:, 0, :]
    out2, force_row = pl.pallas_call(
        trim2_kernel,
        out_shape=(shp(128, 128), shp(1, 128)),
        in_specs=[SM, SM, VM, VM, VM],
        out_specs=(VM, VM),
        compiler_params=PARAMS,
        name="trim2",
    )(ids, resistance, recv2, state, influence)
    recv3 = to_all(out2[:, None, :])[:, 0, :]
    section_force = lax.dynamic_slice(force_row[0], (8 * hy,), (8,))

    def halo(f):
        return (
            shift(f[:, CX - 1], "hullx", 1), shift(f[:, 0], "hullx", -1),
            shift(f[:, :, CY - 1], "hully", 1), shift(f[:, :, 0], "hully", -1),
        )

    both = jnp.concatenate([velocity, pressure[None]], axis=0)
    pred1, source = pl.pallas_call(
        sweep1_kernel,
        out_shape=(shp(3, CX, CY, CZ), shp(3, CX, CY, CZ)),
        in_specs=[VM] * 8,
        out_specs=(VM, VM),
        scratch_shapes=[pltpu.VMEM((4, CX + 2, CY, CZ), F32)],
        compiler_params=PARAMS,
        name="sweep1",
    )(velocity, pressure, mom_source, mom_diag, *halo(both))
    free = pl.pallas_call(
        sweep2_kernel,
        out_shape=shp(3, CX, CY, CZ),
        in_specs=[VM] * 7,
        out_specs=VM,
        scratch_shapes=[pltpu.VMEM((3, CX + 2, CY, CZ), F32)],
        compiler_params=PARAMS,
        name="sweep2",
    )(pred1, source, mom_diag, *halo(pred1))

    def wide(fields, extra=None):
        tail = jnp.concatenate([f[CX - w :] for f, w in fields], axis=0)
        head = jnp.concatenate([f[:w] for f, w in fields], axis=0)
        rows = tail.shape[0] * CY
        tail, head = tail.reshape(rows, 128), head.reshape(rows, 128)
        if extra is not None:
            tail = jnp.concatenate([tail, extra], axis=0)
            head = jnp.concatenate([head, extra], axis=0)
        lo, hi = shift(tail, "hullx", 1), shift(head, "hullx", -1)
        lists = None if extra is None else [extra, lo[rows:], hi[rows:]]
        lo, hi = lo[:rows].reshape(-1, CY, 128), hi[:rows].reshape(-1, CY, 128)
        grown, at = [], 0
        for f, w in fields:
            grown.append(jnp.concatenate([lo[at : at + w], f, hi[at : at + w]], axis=0))
            at += w
        tail = jnp.concatenate([f[:, CY - 8 :] for f in grown], axis=0)
        head = jnp.concatenate([f[:, :8] for f in grown], axis=0)
        rows = tail.shape[0] * 8
        tail, head = tail.reshape(rows, 128), head.reshape(rows, 128)
        if extra is not None:
            tail = jnp.concatenate([tail] + lists, axis=0)
            head = jnp.concatenate([head] + lists, axis=0)
        lo, hi = shift(tail, "hully", 1), shift(head, "hully", -1)
        if extra is not None:
            n = extra.shape[0]
            for other in (lo, hi):
                lists = lists + [other[rows + i * n : rows + (i + 1) * n] for i in range(3)]
        lo, hi = lo[:rows].reshape(-1, 8, 128), hi[:rows].reshape(-1, 8, 128)
        out, at = [], 0
        for f in grown:
            out.append(jnp.concatenate([lo[at : at + f.shape[0]], f, hi[at : at + f.shape[0]]], axis=1))
            at += f.shape[0]
        return out, lists

    base = (
        (hx * CX + jnp.arange(CX, dtype=I32))[:, None] * 256 + (hy * CY + jnp.arange(CY, dtype=I32))[None, :] // 3
    )[:, :, None]
    code = (agglomeration - base + 4).astype(F32)
    entries = jnp.concatenate(
        [body_cells.astype(F32), body_sections.astype(F32), body_weights, jnp.zeros((512,), F32)]
    ).reshape(16, 128)
    (invd_e, invp_e, code_e), lists = wide(
        [(1.0 / (6.0 + mom_diag), 4), (1.0 / (6.0 + press_diag), 2), (code, 3)], entries
    )
    ecell, esec, ewt = (
        jnp.concatenate([l[4 * j : 4 * j + 4].reshape(1, 512) for l in lists], axis=1) for j in range(3)
    )
    (p0, p1, p2), _ = wide([(free[0], 3), (free[1], 2), (free[2], 2)])

    pred0, target, corr1, send = pl.pallas_call(
        body_kernel,
        out_shape=(shp(CX, CY, CZ), shp(20, YE, CZ), shp(18, YE, CZ), shp(128, 128)),
        in_specs=[SM] + [VM] * 13,
        out_specs=(VM,) * 4,
        scratch_shapes=[
            pltpu.VMEM((24, YE, CZ), F32),
            pltpu.VMEM((24, YE, CZ), F32),
            pltpu.VMEM((22, YE, CZ), F32),
            pltpu.VMEM((20, YE, CZ), F32),
            pltpu.VMEM((7 * CY, 128), F32),
        ],
        compiler_params=PARAMS,
        name="body",
    )(ids, recv3, ecell, esec, ewt, p0, p1, p2, invd_e, invp_e, press_diag, code, cols, gfold)

    recv4 = to_all(send[:, None, :])[:, 0, :]
    (corr1_e,), _ = wide([(corr1[1 : CX + 1, 8:56], 3)])

    mine = lax.dynamic_slice(coarse_columns, (2 * hx, 0), (2, 2))[:, 1]
    half = jnp.concatenate([jnp.array([0, 1], I32), mine & 1])
    diags = [lax.dynamic_slice(recv1, (hx * HY + hy, 11, 0), (1, 2, 128))[0]]
    for i in range(2):
        pln = mine[i] >> 1
        diags.append(lax.dynamic_slice(recv1, ((pln & 7) * HY + (pln >> 3), 11 + (mine[i] & 1), 0), (1, 1, 128))[0])
    diag = jnp.concatenate(diags + [jnp.ones((4, 128), F32)], axis=0)
    out5 = pl.pallas_call(
        coarse_kernel,
        out_shape=shp(128, 128),
        in_specs=[SM, SM] + [VM] * 5,
        out_specs=VM,
        compiler_params=PARAMS,
        name="coarse",
    )(ids, half, recv4, ab, diag, place, fold)
    recv5 = to_all(out5[:, None, :])[:, 0, :]

    vel_new, pres_new = pl.pallas_call(
        last_kernel,
        out_shape=(shp(3, CX, CY, CZ), shp(CX, CY, CZ)),
        in_specs=[SM] + [VM] * 10,
        out_specs=(VM, VM),
        scratch_shapes=[
            pltpu.VMEM((128, 128), F32),
            pltpu.VMEM((22, YE, CZ), F32),
            pltpu.VMEM((20, YE, CZ), F32),
            pltpu.VMEM((18, YE, CZ), F32),
        ],
        compiler_params=PARAMS,
        name="last",
    )(ids, recv5, corr1_e, target, invp_e, code_e, pred0, free[1], free[2], pressure, glift.astype(BF16))
    return vel_new, pres_new, section_force


def solution(mesh):
    fine = P("hullx", "hully", None)
    vector = P(None, "hullx", "hully", None)
    flat = P(BOTH)
    in_specs = (
        vector, fine, vector, fine, fine, fine,
        P("hully", None, None, None), P("hully", None),
        flat, flat, flat, flat, flat, P(BOTH, None), P(), flat, flat, flat,
    )
    return jax.shard_map(local, mesh=mesh, in_specs=in_specs, out_specs=(vector, fine, flat), check_vma=False)
```

```python
import numpy as np
import jax
import jax.numpy as jnp
from jax import lax
from jax.experimental import pallas as pl
from jax.experimental.pallas import tpu as pltpu
from jax.sharding import PartitionSpec as P

HX, HY = 8, 16
CX, CY, CZ = 16, 48, 128
NSEC = 1024
BOTH = ("hullx", "hully")
ROWS = (2, 4, 4)
F32, BF16, I32 = jnp.float32, jnp.bfloat16, jnp.int32
HIGH = lax.Precision.HIGHEST
YE = 64
EN = 9 * 512

VM = pl.BlockSpec(memory_space=pltpu.VMEM)
SM = pl.BlockSpec(memory_space=pltpu.SMEM)
AN = pl.BlockSpec(memory_space=pl.ANY)
PARAMS = pltpu.CompilerParams(vmem_limit_bytes=67000000)


def here():
    return lax.axis_index("hullx"), lax.axis_index("hully")


def iota(shape, dim):
    return lax.broadcasted_iota(I32, shape, dim)


def split2(x):
    hi = x.astype(BF16)
    lo = (x - hi.astype(F32)).astype(BF16)
    return hi, lo


def split3(x):
    hi = x.astype(BF16)
    rest = x - hi.astype(F32)
    mid = rest.astype(BF16)
    lo = (rest - mid.astype(F32)).astype(BF16)
    return hi, mid, lo


def nt(a, b, precision=None):
    return lax.dot_general(a, b, (((1,), (1,)), ((), ())), precision=precision, preferred_element_type=F32)


def mm(a, b, precision=None):
    return lax.dot_general(a, b, (((1,), (0,)), ((), ())), precision=precision, preferred_element_type=F32)


def lane_row(column, start):
    spot = iota((8, 128), 1) == iota((8, 128), 0) + start
    return jnp.sum(jnp.where(spot, column, 0.0), axis=0, keepdims=True)


def total(x):
    return jnp.sum(jnp.sum(x, axis=1, keepdims=True), axis=0, keepdims=True)


def zdiff_parts(v):
    lane = iota(v.shape, 1)
    before = jnp.where(lane == 0, 0.0, pltpu.roll(v, 1, 1))
    after = jnp.where(lane == CZ - 1, 0.0, pltpu.roll(v, CZ - 1, 1))
    return before, after


def y_parts(v):
    return pltpu.roll(v, 1, 0), pltpu.roll(v, v.shape[0] - 1, 0)


def s_yz(v):
    a, b = y_parts(v)
    c, d = zdiff_parts(v)
    return (a + b) + (c + d)


def wake_kernel(cols, chord, radius, vel, wc, ws, ww, blocks, keep, give, row, ab, sem):
    hx, hy = here()
    copies = [pltpu.make_async_copy(blocks.at[2 * hx + i, 0], ab.at[i], sem.at[i]) for i in range(2)]
    for c in copies:
        c.start()
    cells = wc[...]
    place = cells >> 7
    spot = (iota((768, 256), 0) == place).astype(BF16)
    picked = jnp.zeros((128, 256), F32)
    for part in split3(vel[0].reshape(768, 128)):
        picked = picked + lax.dot_general(part, spot, (((0,), (0,)), ((), ())), preferred_element_type=F32)
    samples = jnp.sum(jnp.where(iota((128, 256), 0) == (cells & 127), picked, 0.0), axis=0, keepdims=True) * ww[...]
    sec = ws[...]
    high = jnp.where(iota((8, 256), 0) == (sec >> 7), samples, 0.0)
    low = (iota((128, 256), 0) == (sec & 127)).astype(F32)
    row[...] = nt(high, low, HIGH)
    lane = iota((1, 128), 1)
    crow = rrow = jnp.zeros((1, 128), F32)
    for k in range(8):
        crow = jnp.where(lane == 8 * hy + k, chord[k], crow)
        rrow = jnp.where(lane == 8 * hy + k, radius[k], rrow)
    c0 = cols[1, 2 * hx].astype(F32)
    c1 = cols[1, 2 * hx + 1].astype(F32)
    colrow = jnp.where(lane == 0, c0, jnp.where(lane == 1, c1, 0.0))
    eye = iota((128, 128), 0) == iota((128, 128), 1)
    even = (hy & 1) == 0
    first, second = row[0:4, :], row[4:8, :]
    for c in copies:
        c.wait()
    d0 = jnp.sum(jnp.where(eye, ab[0], 0.0), axis=0, keepdims=True)
    d1 = jnp.sum(jnp.where(eye, ab[1], 0.0), axis=0, keepdims=True)
    keep[...] = jnp.concatenate([jnp.where(even, first, second), jnp.where(even, crow, rrow), d0, d1, colrow], axis=0)
    give[...] = jnp.concatenate(
        [jnp.where(even, second, first), jnp.where(even, rrow, crow), jnp.zeros((3, 128), F32)], axis=0
    )


def join_kernel(keep, got, out):
    out[...] = jnp.broadcast_to((keep[...] + got[...])[None], out.shape)


def trim1_kernel(recv, infl, out, state, table, grouped):
    hx, hy = here()
    by_core = recv[...].reshape(HX, HY // 2, 2, 8, 128)
    for core in range(2):
        grouped[core] = jnp.sum(by_core[:, :, core], axis=1)
    wake = jnp.concatenate([jnp.sum(grouped[0], axis=0)[0:4], jnp.sum(grouped[1], axis=0)[0:4]], axis=0)
    chord = grouped[0, :, 4, :]
    radius = grouped[1, :, 4, :]
    table[0] = recv[:, 7, :]
    table[1] = recv[:, 5, :]
    table[2] = recv[:, 6, :]
    state[0] = wake
    state[1] = chord
    state[2] = radius
    circ = chord * (radius - wake)
    acc = infl[:, 0:128] * circ[0:1, :]
    for c in range(1, 8):
        acc = acc + infl[:, c * 128 : (c + 1) * 128] * circ[c : c + 1, :]
    row = lane_row(jnp.sum(acc, axis=1, keepdims=True), 8 * hy)
    out[...] = jnp.broadcast_to(row[None], out.shape)


def trim2_kernel(res, recv, state, infl, out, force):
    hx, hy = here()
    induced = jnp.sum(recv[:, 0, :].reshape(HX, HY, 128), axis=1)
    wake, chord, radius = state[0], state[1], state[2]
    circ = chord * (radius - wake)
    omega = 1.0 + 0.5 * (res[0] - total(circ * radius) * (1.0 / NSEC))
    circ = chord * (omega * radius - wake - induced)
    omega = omega + 0.5 * (res[0] - total(circ * radius) * (1.0 / NSEC))
    acc = infl[:, 0:128] * circ[0:1, :]
    for c in range(1, 8):
        acc = acc + infl[:, c * 128 : (c + 1) * 128] * circ[c : c + 1, :]
    induced2 = lane_row(jnp.sum(acc, axis=1, keepdims=True), 8 * hy)
    mine = (iota((8, 128), 0) == hx) & ((iota((8, 128), 1) >> 3) == hy)
    full = chord * (omega * radius - wake - induced2) * omega * radius
    row = jnp.sum(jnp.where(mine, full, 0.0), axis=0, keepdims=True)
    force[...] = pltpu.roll(row, lax.rem(128 - 8 * hy, 128), 1)[:, 0:8]
    out[...] = jnp.broadcast_to(row[None], out.shape)


MID = slice(8, 8 + CY)


def run(pairs, sems):
    copies = [pltpu.make_async_copy(src, dst, sems.at[i]) for i, (src, dst) in enumerate(pairs)]
    for c in copies:
        c.start()
    return copies


def finish_all(copies):
    for c in copies:
        c.wait()


def codes_of(agg, hx, hy, y0):
    rows = agg.shape[1]
    plane = iota(agg.shape, 0) + CX * hx
    group = lax.div(iota((1, rows, 128), 1) + y0, 3) + 16 * hy
    return (agg - plane * 256 - group + 4).astype(F32)


def widen(low, middle, high):
    return jnp.concatenate([low, middle, high], axis=0)


def load_kernel(
    vel, src, pres, mdiag, pdiag, agg, bc, bs, bw,
    v, s, pr, invd, invp, codes, lists, tail, head,
    ag, ints, sems,
):
    hx, hy = here()
    copies = run(
        [(mdiag, invd), (pdiag, invp), (bc, ints.at[0]), (bs, ints.at[1]), (bw, lists.at[8:12]), (pres, pr), (vel, v), (agg, ag), (src, s)],
        sems,
    )
    lists[12:16, :] = jnp.zeros((4, 128), F32)
    finish_all(copies[:5])
    lists[0:4, :] = ints[0].astype(F32)
    lists[4:8, :] = ints[1].astype(F32)
    invd[...] = 1.0 / (6.0 + invd[...])
    invp[...] = 1.0 / (6.0 + invp[...])
    tail[4:8] = invd[CX - 4 : CX]
    head[4:8] = invd[0:4]
    tail[8:10] = invp[CX - 2 : CX]
    head[8:10] = invp[0:2]
    for out in (tail, head):
        out[10, 0:16] = lists[...]
        out[10, 16:48] = jnp.zeros((32, 128), F32)
    finish_all(copies[5:8])
    for x, out in ((CX - 1, tail), (0, head)):
        out[0:3] = v[:, x]
        out[3] = pr[x]
    codes[...] = codes_of(ag[...], hx, hy, 0)
    finish_all(copies[8:])


def packy_kernel(v, s, pr, invd, invp, codes, lists, xlo, xhi, token, tail_a, head_a, tail_b, head_b):
    for row, a, out in ((CY - 8, tail_a, tail_b), (0, head_a, head_b)):
        rows = slice(row, row + 8)
        for c in range(3):
            a[CX * c : CX * c + CX] = v[c, :, rows, :]
            a[48 + CX * c : 64 + CX * c] = s[c, :, rows, :]
        for k, f in enumerate((pr, invd, invp, codes)):
            out[CX * k : CX * k + CX] = f[:, rows, :]
        out[64:74] = xlo[0:10, rows, :]
        out[74:84] = xhi[0:10, rows, :]
        for j in range(2):
            part = slice(8 * j, 8 * j + 8)
            out[84 + j] = lists[part, :]
            out[86 + j] = xlo[10, part, :]
            out[88 + j] = xhi[10, part, :]


def sweep1_kernel(
    vel, src, pres, invd_own, invp_own, codes_own, yalo, yahi, ylo, yhi, xlo, xhi, token,
    pred, source, invd, invp, codes, tail, head,
    v,
):
    for n, (side, at) in enumerate(((xlo, 64), (xhi, 74))):
        for k in range(4):
            v[k, (CX + 1) * n] = widen(ylo[at + k], side[k], yhi[at + k])
        for k in range(4):
            invd[20 * n + k] = widen(ylo[at + 4 + k], side[4 + k], yhi[at + 4 + k])
        for k in range(2):
            invp[18 * n + k] = widen(ylo[at + 8 + k], side[8 + k], yhi[at + 8 + k])

    def grow(x, carry):
        for k in range(3):
            v[k, x + 1] = widen(yalo[CX * k + x], vel[k, x], yahi[CX * k + x])
        v[3, x + 1] = widen(ylo[x], pres[x], yhi[x])
        invd[x + 4] = widen(ylo[16 + x], invd_own[x], yhi[16 + x])
        invp[x + 2] = widen(ylo[32 + x], invp_own[x], yhi[32 + x])
        codes[x] = widen(ylo[48 + x], codes_own[x], yhi[48 + x])
        return carry

    lax.fori_loop(0, CX, grow, 0, unroll=2)

    def body(x, carry):
        inv = invd[x + 4]
        p = v[3, x + 1]
        ya, yb = y_parts(p)
        za, zb = zdiff_parts(p)
        for c, grad in enumerate((v[3, x + 2] - v[3, x], yb - ya, zb - za)):
            sc = widen(yalo[48 + CX * c + x], src[c, x], yahi[48 + CX * c + x]) - 0.5 * grad
            source[c, x] = sc
            pred[c, x] = (sc + v[c, x] + v[c, x + 2] + s_yz(v[c, x + 1])) * inv
        return carry

    lax.fori_loop(0, CX, body, 0, unroll=2)
    tail[0:3] = pred[:, CX - 1]
    head[0:3] = pred[:, 0]


def sweep2_kernel(pred, source, invd, xlo, xhi, token, out, tail, head):
    def at(x, before, here_, after):
        inv = invd[x + 4]
        for c in range(3):
            out[c, x] = (source[c, x] + before(c) + after(c) + s_yz(here_(c))) * inv

    def body(x, carry):
        at(x, lambda c: pred[c, x - 1], lambda c: pred[c, x], lambda c: pred[c, x + 1])
        return carry

    at(0, lambda c: xlo[c], lambda c: pred[c, 0], lambda c: pred[c, 1])
    lax.fori_loop(1, CX - 1, body, 0, unroll=2)
    at(CX - 1, lambda c: pred[c, CX - 2], lambda c: pred[c, CX - 1], lambda c: xhi[c])
    to = 0
    for c, w in enumerate((3, 2, 2)):
        tail[to : to + w] = out[c, CX - w : CX]
        head[to : to + w] = out[c, 0:w]
        to += w


def body_parts():
    return [(sx, sy) for sy in (0, -1, 1) for sx in (0, -1, 1)]


def force_kernel(recv, lists, ylo, yhi, x1lo, x1hi, b, listed, sems):
    listed[0:16, :] = lists[...]
    early = [(x1lo.at[10, 0:16], listed.at[16:32]), (x1hi.at[10, 0:16], listed.at[32:48])]
    for n, buf in enumerate((ylo, yhi)):
        for j in range(6):
            at = 48 + 48 * n + 8 * j
            early.append((buf.at[84 + j], listed.at[at : at + 8]))
    finish_all(run(early, sems))
    force = jnp.sum(recv[:, 0, :].reshape(HX, HY, 128), axis=1)

    def entries(j):
        rows = [listed[16 * k + 4 * j + i : 16 * k + 4 * j + i + 1, :] for k in range(9) for i in range(4)]
        return jnp.concatenate(rows, axis=1)

    ecell, esec, ewt = entries(0), entries(1), entries(2)
    sec = esec.astype(I32)
    low = (iota((128, EN), 0) == (sec & 127)).astype(BF16)
    got = mm(jnp.concatenate(split3(force), axis=0), low)
    got = got[0:8] + got[8:16] + got[16:24]
    val = jnp.sum(jnp.where(iota((8, EN), 0) == (sec >> 7), got, 0.0), axis=0, keepdims=True) * ewt
    cell = ecell.astype(I32)
    cz = cell & 127
    place = cell >> 7
    cx = (place * 43691) >> 21
    cy = place - 48 * cx
    zv = jnp.where(iota((128, EN), 0) == cz, val, 0.0)
    zh, zl = split2(zv)
    for k, (sx, sy) in enumerate(body_parts()):
        lanes = slice(k * 512, (k + 1) * 512)
        x, y = cx[:, lanes], cy[:, lanes]
        planes = CX if sx == 0 else 4
        first = {0: 4, -1: 0, 1: 20}[sx]
        x = x - 12 if sx < 0 else x
        inside = (x >= 0) & (x < planes)
        if sy == 0:
            r = jnp.where(inside, x * YE + y + 8, -1)
            rows = planes * YE
        else:
            y = y - 40 if sy < 0 else y
            inside = inside & (y >= 0) & (y < 8)
            r = jnp.where(inside, x * 8 + y, -1)
            rows = planes * 8
        spot = (iota((rows, 512), 0) == r).astype(BF16)
        part = nt(spot, zh[:, lanes]) + nt(spot, zl[:, lanes])
        if sy == 0:
            b[first : first + planes] = part.reshape(planes, YE, 128)
        else:
            at = 0 if sy < 0 else 56
            b[first : first + planes, at : at + 8] = b[first : first + planes, at : at + 8] + part.reshape(planes, 8, 128)


def three(n, w, fn):
    for i in range(w):
        fn(i, 0, i)

    def own(j, carry):
        fn(j + w, 1, j)
        return carry

    lax.fori_loop(0, CX, own, 0, unroll=4)
    for i in range(n - CX - w):
        fn(CX + w + i, 2, i)


def body_kernel(
    b, x3lo, x3hi, free, invd, invp, codes, table, gfold,
    pr0, target, corr1, tail, head, send,
    dp, corr0, acc,
):
    hx, hy = here()
    u = lambda c, at, part, j: (x3lo[at + j] if part == 0 else x3hi[at + j]) if part != 1 else free[c, j]

    def s1(p, part, j):
        dp[p] = b[p] * invd[p]

    def s2(i, part, j):
        p = i + 1
        pr0[i] = u(0, 0, part, j) + (b[p] + dp[p - 1] + dp[p + 1] + s_yz(dp[p])) * invd[p]

    def s3(t, part, j):
        ya, yb = y_parts(u(1, 3, part, j))
        za, zb = zdiff_parts(u(2, 5, part, j))
        tg = -0.5 * ((pr0[t + 2] - pr0[t]) + (yb - ya) + (zb - za))
        target[t] = tg
        corr0[t] = 0.8 * tg * invp[t]

    def s4(c, part, j):
        t = c + 1
        v = corr0[t]
        corr1[c] = 0.2 * v + 0.8 * (target[t] + corr0[t - 1] + corr0[t + 1] + s_yz(v)) * invp[t]

    three(24, 4, s1)
    three(22, 3, s2)
    three(20, 2, s3)
    three(18, 1, s4)

    def s5(g, carry):
        halves, picks = [], []
        for k in range(4):
            x = 4 * g + k
            v = corr1[x + 1]
            full = target[x + 2] + corr1[x] + corr1[x + 2] + s_yz(v)
            res = full[8:56] - v[8:56] / invp[x + 2, MID, :]
            code = codes[x, MID, :]
            hi, lo = split2(jnp.concatenate([jnp.where(code == float(n + 1), res, 0.0) for n in range(7)], axis=0))
            halves += [hi, lo]
            picks += [(iota((256, 128), 1) == x).astype(BF16)]
        part = mm(jnp.concatenate(halves, axis=1), jnp.concatenate(picks, axis=0))
        acc[...] = jnp.where(g == 0, part, acc[...] + part)
        return carry

    acc[...] = jnp.zeros(acc.shape, F32)
    lax.fori_loop(0, CX // 4, s5, 0)
    tail[0:3] = corr1[CX - 2 : CX + 1]
    tail[3:6] = codes[CX - 3 : CX]
    head[0:3] = corr1[1:4]
    head[3:6] = codes[0:3]
    window = mm(gfold[...], acc[...], HIGH) * float(384.0**-0.5)
    blank = jnp.zeros((32, 128), F32)
    spread = jnp.concatenate(
        [jnp.concatenate([window if j == q else blank for j in range(4)], axis=1) for q in range(4)], axis=0
    )
    m = iota((128, 1), 0)
    plane = 8 * (m & 15) + (m >> 4)
    c0 = table[0, :, 0:1].astype(I32)
    c1 = table[0, :, 1:2].astype(I32)
    lane = iota((128, 128), 1)
    wants = []
    for blk in (2 * plane, 2 * plane + 1, c0, c1):
        half = blk & 1
        pln = blk >> 1
        pln = pln - jnp.where((half == 0) & (hy == HY - 1), 1, 0) + jnp.where((half == 1) & (hy == 0), 1, 0)
        at = pln - CX * hx
        at = jnp.where((at >= 0) & (at < CX), at, -1)
        wants.append((lane == at).astype(F32))
    send[...] = jnp.broadcast_to(nt(jnp.concatenate(wants, axis=1), spread, HIGH)[:, None, :], send.shape)


def coarse_kernel(cols, recv, blocks, table, out, ab, diag, sem):
    hx, hy = here()
    copy = pltpu.make_async_copy(blocks.at[pl.ds(2 * hx, 2)], ab, sem)
    copy.start()
    c0, c1 = cols[1, 2 * hx], cols[1, 2 * hx + 1]
    half = (0, 1, c0 & 1, c1 & 1)
    m = hx * HY + hy
    diag[...] = jnp.ones((8, 128), F32)
    diag[0:1, :] = table[1, pl.ds(m, 1), :]
    diag[1:2, :] = table[2, pl.ds(m, 1), :]
    for i, c in enumerate((c0, c1)):
        pln = c >> 1
        diag[2 + i : 3 + i, :] = table[1 + (c & 1), pl.ds((pln & 7) * HY + (pln >> 3), 1), :]
    z = jnp.sum(recv[:, 0, :].reshape(HX, HY, 128), axis=0)
    r, c = iota((128, 1024), 0), iota((128, 1024), 1)
    later = (c >> 7) & 1
    m16 = (c + 4) & 15
    place = ((r >> 5) == (c >> 8)) & ((r & 31) == m16 + 16 * later) & ((later == 0) | (m16 < 8))
    y3 = mm(jnp.concatenate(split3(z), axis=0), place.astype(BF16))
    y = y3[0:16] + y3[16:32] + y3[32:48]
    lane = iota((HY, 128), 1)
    hys = iota((HY, 128), 0)
    rows = []
    for q in range(4):
        slot = (lane + 4 + 128 * half[q] - 16 * hys) & 255
        a = jnp.where(slot < 16, y[:, (2 * q) * 128 : (2 * q + 1) * 128], 0.0)
        b = jnp.where((slot >= 16) & (slot < 24), y[:, (2 * q + 1) * 128 : (2 * q + 2) * 128], 0.0)
        rows.append(jnp.sum(a + b, axis=0, keepdims=True))
    res = jnp.concatenate(rows + [jnp.zeros((4, 128), F32)], axis=0)
    first = 0.8 * res / diag[...]
    seconds = []
    copy.wait()
    for i in range(2):
        applied = nt(first, ab[i, 0], HIGH)[i : i + 1] + nt(first, ab[i, 1], HIGH)[2 + i : 3 + i]
        seconds.append(first[i : i + 1] + 0.8 * (res[i : i + 1] - applied) / diag[i : i + 1, :])
    second = jnp.concatenate(seconds, axis=1)
    lane2 = iota((HY, 256), 1)
    slot = (lane2 + 4 - 16 * iota((HY, 256), 0)) & 255
    wide = jnp.broadcast_to(second, (HY, 256))
    d0 = jnp.where(slot < 16, wide, 0.0)
    d1 = jnp.where((slot >= 16) & (slot < 24), wide, 0.0)
    r, c = iota((512, 128), 0), iota((512, 128), 1)
    later = r >> 8
    m16 = (r + 4) & 15
    fold = (c == m16 + 16 * later) & ((later == 0) | (m16 < 8))
    w3 = mm(jnp.concatenate(split3(jnp.concatenate([d0, d1], axis=1)), axis=0), fold.astype(BF16))
    windows = w3[0:16] + w3[16:32] + w3[32:48]
    for i in range(HX):
        out[i * HY : (i + 1) * HY, :] = windows


def last_kernel(
    recv, corr1, codes, xlo, xhi, target, invp, pr0, free, pres, glift,
    vel_out, pres_out,
    win, c2, s1, s2,
):
    hx, hy = here()
    for i in range(24):
        p = jnp.clip(CX * hx - 4 + i, 0, 127)
        m = (p & 7) * HY + (p >> 3)
        win[i : i + 1, :] = recv[pl.ds(m, 1), :]
    w = win[0:24, :]
    lane = iota((24, 128), 1)
    w = jnp.where((lane < 4) & (hy == 0), pltpu.roll(w, 1, 0), w)
    w = jnp.where((lane >= 20) & (lane < 24) & (hy == HY - 1), pltpu.roll(w, 23, 0), w)
    win[0:24, :] = w
    win[24:128, :] = jnp.zeros((104, 128), F32)
    wt = win[...].T
    win[...] = wt

    def lift(i, part, j):
        column = jnp.sum(jnp.where(iota((32, 128), 1) == i + 1, win[0:32, :], 0.0), axis=1, keepdims=True)
        wide = jnp.broadcast_to(column, (32, 128))
        v = mm(glift[...], jnp.concatenate(split3(wide), axis=0))
        side = (xlo, None, xhi)[part]
        code = codes[j] if part == 1 else side[3 + j]
        lifted = corr1[j + 1] if part == 1 else side[j]
        for n in range(7):
            lifted = jnp.where(code == float(n + 1), lifted + v[n * YE : (n + 1) * YE], lifted)
        c2[i] = lifted

    three(22, 3, lift)

    def sweep1(t, part, j):
        v = c2[t + 1]
        s1[t] = 0.2 * v + 0.8 * (target[t] + c2[t] + c2[t + 2] + s_yz(v)) * invp[t]

    def sweep2(c, part, j):
        v = s1[c + 1]
        s2[c] = 0.2 * v + 0.8 * (target[c + 1] + s1[c] + s1[c + 2] + s_yz(v)) * invp[c + 1]

    three(20, 2, sweep1)
    three(18, 1, sweep2)

    def finish(x, carry):
        v = s2[x + 1]
        ya, yb = y_parts(v)
        za, zb = zdiff_parts(v)
        vel_out[0, x] = pr0[x + 3, MID, :] - 0.5 * (s2[x + 2] - s2[x])[8:56]
        vel_out[1, x] = free[1, x, MID, :] - 0.5 * (yb - ya)[8:56]
        vel_out[2, x] = free[2, x, MID, :] - 0.5 * (zb - za)[8:56]
        pres_out[x] = pres[x] + 0.7 * v[8:56]
        return carry

    lax.fori_loop(0, CX, finish, 0, unroll=2)


def tables():
    y = np.arange(CY)
    gfold = np.zeros((32, 7 * CY), np.float32)
    for d in range(7):
        gfold[y // 3 + d + 1, d * CY + y] = 1.0
    glift = np.zeros((7 * YE, 96), np.float32)
    for d in range(7):
        for yy in range(YE):
            slot = (yy - 8) // 3 + d + 1
            if 0 <= slot < 32:
                for part in range(3):
                    glift[d * YE + yy, part * 32 + slot] = 1.0
    return gfold, glift


def shift(x, axis, by):
    n = HX if axis == "hullx" else HY
    return lax.ppermute(x, axis, [(i, i + by) for i in range(n) if 0 <= i + by < n])


def to_all(x):
    return lax.all_to_all(x, BOTH, 0, 0, tiled=True)


def pair(x):
    return lax.ppermute(x, "hully", [(i, i ^ 1) for i in range(HY)])


def fast(*dims, dtype=F32):
    return jax.ShapeDtypeStruct(dims, dtype)


def send(*dims, dtype=F32):
    return jax.ShapeDtypeStruct(dims, dtype)


def shp(*dims, dtype=F32):
    return jax.ShapeDtypeStruct(dims, dtype)


def local(
    velocity, pressure, mom_source, mom_diag, press_diag, agglomeration, coarse_blocks, coarse_columns,
    wake_cells, wake_sections, wake_weights, chord, radius, influence, resistance,
    body_cells, body_sections, body_weights,
):
    gfold, glift = (jnp.asarray(t) for t in tables())
    cols = coarse_columns.T
    block = lambda *n: pltpu.VMEM((*n, YE, CZ), F32)
    sems = lambda n: pltpu.SemaphoreType.DMA((n,))

    def call(kernel, name, outs, ins, scratch, args):
        many = isinstance(outs, tuple)
        return pl.pallas_call(
            kernel, out_shape=outs, in_specs=ins, out_specs=(VM,) * len(outs) if many else VM,
            scratch_shapes=scratch, compiler_params=PARAMS, name=name,
        )(*args)

    def slow(*arrays):
        return arrays

    v, src, pres, invd_own, invp_own, codes_own, lists, xt, xh = call(
        load_kernel, "load",
        (fast(3, CX, CY, CZ),) * 2 + (fast(CX, CY, CZ),) * 4 + (fast(16, 128),) + (send(11, CY, CZ),) * 2,
        [AN] * 9, [pltpu.VMEM((CX, CY, CZ), I32), pltpu.VMEM((2, 4, 128), I32), sems(9)],
        slow(velocity, mom_source, pressure, mom_diag, press_diag, agglomeration)
        + slow(*(a.reshape(4, 128) for a in (body_cells, body_sections, body_weights))),
    )
    x1lo, x1hi = shift(xt, "hullx", 1), shift(xh, "hullx", -1)

    keep, give = call(
        wake_kernel, "wake", (fast(8, 128), send(8, 128)), [SM, SM, SM, VM, VM, VM, VM, AN],
        [pltpu.VMEM((8, 128), F32), pltpu.VMEM((2, 128, 128), F32), sems(2)],
        (cols, chord, radius, v, wake_cells[None], wake_sections[None], wake_weights[None]) + slow(coarse_blocks),
    )
    payload = call(join_kernel, "join", send(128, 8, 128), [VM, VM], [], (keep, pair(give)))
    recv1 = to_all(payload)
    out1, state, table = call(
        trim1_kernel, "trim1", (send(128, ROWS[0], 128), fast(3, 8, 128), fast(3, 128, 128)), [VM, VM],
        [pltpu.VMEM((2, 8, 8, 128), F32)], (recv1,) + slow(influence),
    )
    recv2 = to_all(out1)

    yat, yah, yt, yh = call(
        packy_kernel, "packy", (send(96, 8, CZ),) * 2 + (send(90, 8, CZ),) * 2, [VM] * 9 + [AN], [],
        (v, src, pres, invd_own, invp_own, codes_own, lists, x1lo, x1hi, payload),
    )
    yalo, yahi = shift(yat, "hully", 1), shift(yah, "hully", -1)
    ylo, yhi = shift(yt, "hully", 1), shift(yh, "hully", -1)
    pred1, source, invd, invp, codes, xt, xh = call(
        sweep1_kernel, "sweep1",
        (fast(3, CX, YE, CZ),) * 2 + (fast(24, YE, CZ), fast(20, YE, CZ), fast(CX, YE, CZ)) + (send(3, YE, CZ),) * 2,
        [VM] * 13, [block(4, CX + 2)],
        (v, src, pres, invd_own, invp_own, codes_own, yalo, yahi, ylo, yhi, x1lo, x1hi, state),
    )
    x2lo, x2hi = shift(xt, "hullx", 1), shift(xh, "hullx", -1)

    out2, force = call(
        trim2_kernel, "trim2", (send(128, ROWS[1], 128), fast(1, 8)), [SM, VM, VM, VM], [],
        (resistance, recv2, state) + slow(influence),
    )
    recv3 = to_all(out2)
    free, xt, xh = call(
        sweep2_kernel, "sweep2", (fast(3, CX, YE, CZ),) + (send(7, YE, CZ),) * 2, [VM] * 6, [],
        (pred1, source, invd, x2lo, x2hi, force),
    )
    x3lo, x3hi = shift(xt, "hullx", 1), shift(xh, "hullx", -1)

    b = call(
        force_kernel, "force", fast(24, YE, CZ), [VM, VM] + [AN] * 4, [pltpu.VMEM((144, 128), F32), sems(14)],
        (recv3, lists, ylo, yhi, x1lo, x1hi),
    )
    pr0, target, corr1, ct, ch, out4 = call(
        body_kernel, "body",
        (fast(22, YE, CZ), fast(20, YE, CZ), fast(18, YE, CZ), send(6, YE, CZ), send(6, YE, CZ), send(128, ROWS[2], 128)),
        [VM] * 9, [block(24), block(20), pltpu.VMEM((7 * CY, 128), F32)],
        (b, x3lo, x3hi, free, invd, invp, codes, table) + slow(gfold),
    )
    recv4 = to_all(out4)
    cxlo, cxhi = shift(ct, "hullx", 1), shift(ch, "hullx", -1)
    out5 = call(
        coarse_kernel, "coarse", send(128, 128), [SM, VM, AN, VM],
        [pltpu.VMEM((2, 2, 128, 128), F32), pltpu.VMEM((8, 128), F32), pltpu.SemaphoreType.DMA],
        (cols, recv4) + slow(coarse_blocks) + (table,),
    )
    recv5 = to_all(out5[:, None, :])[:, 0, :]
    vel_new, pres_new = call(
        last_kernel, "last", (shp(3, CX, CY, CZ), shp(CX, CY, CZ)), [VM] * 11,
        [pltpu.VMEM((128, 128), F32), block(22), block(20), block(18)],
        (recv5, corr1, codes, cxlo, cxhi, target, invp, pr0, free, pres) + slow(glift.astype(BF16)),
    )
    section_force = force.reshape(8)
    return vel_new, pres_new, section_force


def solution(mesh):
    fine = P("hullx", "hully", None)
    vector = P(None, "hullx", "hully", None)
    flat = P(BOTH)
    in_specs = (
        vector, fine, vector, fine, fine, fine,
        P("hully", None, None, None), P("hully", None),
        flat, flat, flat, flat, flat, P(BOTH, None), P(), flat, flat, flat,
    )
    return jax.shard_map(local, mesh=mesh, in_specs=in_specs, out_specs=(vector, fine, flat), check_vma=False)
```

```python
import numpy as np
import jax
import jax.numpy as jnp
from jax import lax
from jax.experimental import pallas as pl
from jax.experimental.pallas import tpu as pltpu
from jax.sharding import PartitionSpec as P

HX, HY = 8, 16
CX, CY, CZ = 16, 48, 128
NSEC = 1024
BOTH = ("hullx", "hully")
ROWS = (4, 1, 4)
F32, BF16, I32 = jnp.float32, jnp.bfloat16, jnp.int32
HIGH = lax.Precision.HIGHEST
YE = 64
EN = 9 * 512

VM = pl.BlockSpec(memory_space=pltpu.VMEM)
SM = pl.BlockSpec(memory_space=pltpu.SMEM)
AN = pl.BlockSpec(memory_space=pl.ANY)
PARAMS = pltpu.CompilerParams(vmem_limit_bytes=67000000)


def here():
    return lax.axis_index("hullx"), lax.axis_index("hully")


def iota(shape, dim):
    return lax.broadcasted_iota(I32, shape, dim)


def split2(x):
    hi = x.astype(BF16)
    lo = (x - hi.astype(F32)).astype(BF16)
    return hi, lo


def split3(x):
    hi = x.astype(BF16)
    rest = x - hi.astype(F32)
    mid = rest.astype(BF16)
    lo = (rest - mid.astype(F32)).astype(BF16)
    return hi, mid, lo


def nt(a, b, precision=None):
    return lax.dot_general(a, b, (((1,), (1,)), ((), ())), precision=precision, preferred_element_type=F32)


def mm(a, b, precision=None):
    return lax.dot_general(a, b, (((1,), (0,)), ((), ())), precision=precision, preferred_element_type=F32)


def lane_row(column, start):
    spot = iota((8, 128), 1) == iota((8, 128), 0) + start
    return jnp.sum(jnp.where(spot, column, 0.0), axis=0, keepdims=True)


def total(x):
    return jnp.sum(jnp.sum(x, axis=1, keepdims=True), axis=0, keepdims=True)


def zdiff_parts(v):
    lane = iota(v.shape, 1)
    before = jnp.where(lane == 0, 0.0, pltpu.roll(v, 1, 1))
    after = jnp.where(lane == CZ - 1, 0.0, pltpu.roll(v, CZ - 1, 1))
    return before, after


def y_parts(v):
    return pltpu.roll(v, 1, 0), pltpu.roll(v, v.shape[0] - 1, 0)


def s_yz(v):
    a, b = y_parts(v)
    c, d = zdiff_parts(v)
    return (a + b) + (c + d)


def wake_kernel(cols, chord, radius, vel, wc, ws, ww, blocks, keep, give, row, ab, v, sem):
    hx, hy = here()
    copies = run([(vel.at[0], v)] + [(blocks.at[2 * hx + i, 0], ab.at[i]) for i in range(2)], sem)
    cells = wc[...]
    place = cells >> 7
    spot = (iota((768, 256), 0) == place).astype(BF16)
    picked = jnp.zeros((128, 256), F32)
    copies[0].wait()
    for part in split2(v[...].reshape(768, 128)):
        picked = picked + lax.dot_general(part, spot, (((0,), (0,)), ((), ())), preferred_element_type=F32)
    samples = jnp.sum(jnp.where(iota((128, 256), 0) == (cells & 127), picked, 0.0), axis=0, keepdims=True) * ww[...]
    sec = ws[...]
    high = jnp.where(iota((8, 256), 0) == (sec >> 7), samples, 0.0)
    low = (iota((128, 256), 0) == (sec & 127)).astype(F32)
    row[...] = nt(high, low, HIGH)
    lane = iota((1, 128), 1)
    crow = rrow = jnp.zeros((1, 128), F32)
    for k in range(8):
        crow = jnp.where(lane == 8 * hy + k, chord[k], crow)
        rrow = jnp.where(lane == 8 * hy + k, radius[k], rrow)
    c0 = cols[1, 2 * hx].astype(F32)
    c1 = cols[1, 2 * hx + 1].astype(F32)
    colrow = jnp.where(lane == 0, c0, jnp.where(lane == 1, c1, 0.0))
    eye = iota((128, 128), 0) == iota((128, 128), 1)
    even = (hy & 1) == 0
    first, second = row[0:4, :], row[4:8, :]
    finish_all(copies[1:])
    d0 = jnp.sum(jnp.where(eye, ab[0], 0.0), axis=0, keepdims=True)
    d1 = jnp.sum(jnp.where(eye, ab[1], 0.0), axis=0, keepdims=True)
    keep[...] = jnp.concatenate([jnp.where(even, first, second), jnp.where(even, crow, rrow), d0, d1, colrow], axis=0)
    give[...] = jnp.concatenate(
        [jnp.where(even, second, first), jnp.where(even, rrow, crow), jnp.zeros((3, 128), F32)], axis=0
    )


def join_kernel(keep, got, out):
    out[...] = jnp.broadcast_to((keep[...] + got[...])[None], out.shape)


def trim1_kernel(recv, infl, out, state, table, grouped):
    hx, hy = here()
    by_core = recv[...].reshape(HX, HY // 2, 2, 8, 128)
    for core in range(2):
        grouped[core] = jnp.sum(by_core[:, :, core], axis=1)
    wake = jnp.concatenate([jnp.sum(grouped[0], axis=0)[0:4], jnp.sum(grouped[1], axis=0)[0:4]], axis=0)
    chord = grouped[0, :, 4, :]
    radius = grouped[1, :, 4, :]
    table[0] = recv[:, 7, :]
    table[1] = recv[:, 5, :]
    table[2] = recv[:, 6, :]
    state[0] = wake
    state[1] = chord
    state[2] = radius
    circ = chord * (radius - wake)
    acc = infl[:, 0:128] * circ[0:1, :]
    for c in range(1, 8):
        acc = acc + infl[:, c * 128 : (c + 1) * 128] * circ[c : c + 1, :]
    row = lane_row(jnp.sum(acc, axis=1, keepdims=True), 8 * hy)
    out[...] = jnp.broadcast_to(row[None], out.shape)


def trim2_kernel(res, recv, state, infl, out, force):
    hx, hy = here()
    induced = jnp.sum(recv[:, 0, :].reshape(HX, HY, 128), axis=1)
    wake, chord, radius = state[0], state[1], state[2]
    circ = chord * (radius - wake)
    omega = 1.0 + 0.5 * (res[0] - total(circ * radius) * (1.0 / NSEC))
    circ = chord * (omega * radius - wake - induced)
    omega = omega + 0.5 * (res[0] - total(circ * radius) * (1.0 / NSEC))
    acc = infl[:, 0:128] * circ[0:1, :]
    for c in range(1, 8):
        acc = acc + infl[:, c * 128 : (c + 1) * 128] * circ[c : c + 1, :]
    induced2 = lane_row(jnp.sum(acc, axis=1, keepdims=True), 8 * hy)
    mine = (iota((8, 128), 0) == hx) & ((iota((8, 128), 1) >> 3) == hy)
    full = chord * (omega * radius - wake - induced2) * omega * radius
    row = jnp.sum(jnp.where(mine, full, 0.0), axis=0, keepdims=True)
    force[...] = pltpu.roll(row, lax.rem(128 - 8 * hy, 128), 1)[:, 0:8]
    out[...] = jnp.broadcast_to(row[None], out.shape)


MID = slice(8, 8 + CY)


def run(pairs, sems):
    copies = [pltpu.make_async_copy(src, dst, sems.at[i]) for i, (src, dst) in enumerate(pairs)]
    for c in copies:
        c.start()
    return copies


def finish_all(copies):
    for c in copies:
        c.wait()


def codes_of(agg, hx, hy, y0):
    rows = agg.shape[1]
    plane = iota(agg.shape, 0) + CX * hx
    group = lax.div(iota((1, rows, 128), 1) + y0, 3) + 16 * hy
    return (agg - plane * 256 - group + 4).astype(F32)


def widen(low, middle, high):
    return jnp.concatenate([low, middle, high], axis=0)


HALO = 17


def packx_kernel(vel, src, pres, mdiag, pdiag, bc, bs, bw, tail, head, ints, sems):
    ends = ((1, tail), (0, head))
    pairs = []
    for last, out in ends:
        end = lambda w: pl.ds(last * (CX - w), w)
        pairs += [(mdiag.at[end(4)], out.at[11:15]), (pdiag.at[end(2)], out.at[15:17])]
    pairs += [(bc, ints.at[0]), (bs, ints.at[1])]
    first = len(pairs)
    for last, out in ends:
        end = lambda w: pl.ds(last * (CX - w), w)
        pairs.append((bw, out.at[HALO, 8:12]))
        pairs.append((pres.at[end(2)], out.at[9:11]))
        for c in range(3):
            pairs.append((vel.at[c, end(2)], out.at[2 * c : 2 * c + 2]))
            pairs.append((src.at[c, end(1)], out.at[6 + c : 7 + c]))
    copies = run(pairs, sems)
    finish_all(copies[:first])
    for out in (tail, head):
        out[11:17] = 1.0 / (6.0 + out[11:17])
        out[HALO, 0:4] = ints[0].astype(F32)
        out[HALO, 4:8] = ints[1].astype(F32)
        out[HALO, 12:16] = jnp.zeros((4, 128), F32)
        out[HALO, 16:48] = jnp.zeros((32, 128), F32)
    finish_all(copies[first:])


def packy_kernel(
    vel, src, pres, mdiag, pdiag, agg, lists, xlo, xhi, token,
    near_a, far_a, near_b, far_b,
    edge, aedge, sems,
):
    hx, hy = here()
    odd = hy & 1
    ends = []
    for at, a, out in ((1 - odd, near_a, near_b), (odd, far_a, far_b)):
        row = pl.multiple_of((CY - 8) * at, 8)
        ends.append((pl.ds(row, 8), row, a, out))
    pairs = []
    for n, (rows, _, a, out) in enumerate(ends):
        pairs += [(mdiag.at[:, rows], edge.at[n, 0]), (pdiag.at[:, rows], edge.at[n, 1]), (agg.at[:, rows], aedge.at[n])]
    for rows, _, a, out in ends:
        for c in range(3):
            pairs.append((vel.at[c, :, rows], a.at[CX * c : CX * c + CX]))
            pairs.append((src.at[c, :, rows], a.at[48 + CX * c : 64 + CX * c]))
        pairs.append((pres.at[:, rows], out.at[0:CX]))
        for k, side in ((0, xlo), (1, xhi)):
            pairs.append((side.at[0:HALO, rows], out.at[pl.ds(64 + HALO * k, HALO)]))
            for j in range(2):
                pairs.append((side.at[HALO, slice(8 * j, 8 * j + 8)], out.at[100 + 2 * k + j]))
        for j in range(2):
            pairs.append((lists.at[HALO, slice(8 * j, 8 * j + 8)], out.at[98 + j]))
    copies = run(pairs, sems)
    finish_all(copies[:6])
    for n, (_, row, a, out) in enumerate(ends):
        out[16:32] = 1.0 / (6.0 + edge[n, 0])
        out[32:48] = 1.0 / (6.0 + edge[n, 1])
        out[48:64] = codes_of(aedge[n], hx, hy, row)
    finish_all(copies[6:])


def sweeps_kernel(
    vel, src, pres, mdiag, pdiag, agg, near_a, far_a, near_b, far_b, xlo, xhi, token,
    free, invd_out, invp_out, codes_out, near, far,
    v, s, q, invd, invp, codes, ya, yb, xb, sems,
):
    hx, hy = here()
    odd = hy & 1
    finish_all(
        run(
            [(near_a, ya.at[1 - odd]), (far_a, ya.at[odd]), (near_b, yb.at[1 - odd]), (far_b, yb.at[odd])]
            + [(xlo.at[0:HALO], xb.at[0]), (xhi.at[0:HALO], xb.at[1])],
            sems,
        )
    )
    yalo, yahi, ylo, yhi = ya.at[0], ya.at[1], yb.at[0], yb.at[1]
    for n in range(2):
        grown = lambda k: widen(ylo[64 + HALO * n + k], xb[n, k], yhi[64 + HALO * n + k])
        for k in range(2):
            for c in range(3):
                v[c, 18 * n + k] = grown(2 * c + k)
            v[3, 18 * n + k] = grown(9 + k)
            invp[18 * n + k] = grown(15 + k)
        for c in range(3):
            s[c, 17 * n] = grown(6 + c)
        for k in range(4):
            invd[20 * n + k] = grown(11 + k)

    def grow(x, carry):
        for c in range(3):
            v[c, x + 2] = widen(yalo[CX * c + x], vel[c, x], yahi[CX * c + x])
            s[c, x + 1] = widen(yalo[48 + CX * c + x], src[c, x], yahi[48 + CX * c + x])
        v[3, x + 2] = widen(ylo[x], pres[x], yhi[x])
        invd[x + 4] = widen(ylo[16 + x], 1.0 / (6.0 + mdiag[x]), yhi[16 + x])
        invp[x + 2] = widen(ylo[32 + x], 1.0 / (6.0 + pdiag[x]), yhi[32 + x])
        base = (CX * hx + x) * 256 + 16 * hy + lax.div(iota((CY, 128), 0), 3)
        codes[x] = widen(ylo[48 + x], (agg[x] - base + 4).astype(F32), yhi[48 + x])
        return carry

    lax.fori_loop(0, CX, grow, 0, unroll=2)

    copies = run([(invd, invd_out), (invp, invp_out), (codes, codes_out)], sems)

    def first(i, carry):
        inv = invd[i + 3]
        p = v[3, i + 1]
        ya, yb = y_parts(p)
        za, zb = zdiff_parts(p)
        for c, grad in enumerate((v[3, i + 2] - v[3, i], yb - ya, zb - za)):
            sc = s[c, i] - 0.5 * grad
            s[c, i] = sc
            q[c, i] = (sc + v[c, i] + v[c, i + 2] + s_yz(v[c, i + 1])) * inv
        return carry

    lax.fori_loop(0, CX + 2, first, 0, unroll=2)

    def second(x, carry):
        inv = invd[x + 4]
        for c in range(3):
            free[c, x] = (s[c, x + 1] + q[c, x] + q[c, x + 2] + s_yz(q[c, x + 1])) * inv
        return carry

    lax.fori_loop(0, CX, second, 0, unroll=2)
    to = 0
    for c, w in enumerate((3, 2, 2)):
        near[to : to + w] = free[c, pl.ds((1 - (hx & 1)) * (CX - w), w)]
        far[to : to + w] = free[c, pl.ds((hx & 1) * (CX - w), w)]
        to += w
    finish_all(copies)


def body_parts():
    return [(sx, sy) for sy in (0, -1, 1) for sx in (0, -1, 1)]


def three(n, w, fn):
    for i in range(w):
        fn(i, 0, i)

    def own(j, carry):
        fn(j + w, 1, j)
        return carry

    lax.fori_loop(0, CX, own, 0, unroll=4)
    for i in range(n - CX - w):
        fn(CX + w + i, 2, i)


def body_kernel(
    recv, lists, ynear, yfar, xlo, xhi, unear, ufar, free_in, invd_in, invp_in, codes_in, table_in, gfold,
    pr0, target, corr1, near, far, send,
    b, listed, dp, corr0, acc, x3, free, invd, invp, codes, table, early_sems, sems,
):
    hx, hy = here()
    early = [(lists.at[HALO, 0:16], listed.at[0:16])]
    early += [(xlo.at[HALO, 0:16], listed.at[16:32]), (xhi.at[HALO, 0:16], listed.at[32:48])]
    for n, buf in ((1 - (hy & 1), ynear), (hy & 1, yfar)):
        for j in range(6):
            at = pl.multiple_of(48 + 48 * n + 8 * j, 8)
            early.append((buf.at[98 + j], listed.at[pl.ds(at, 8)]))
    early = run(early, early_sems)
    copies = run(
        [(invd_in, invd), (unear, x3.at[1 - (hx & 1)]), (ufar, x3.at[hx & 1]), (free_in, free), (invp_in, invp), (codes_in, codes), (table_in, table)],
        sems,
    )
    finish_all(early)
    force = jnp.sum(recv[:, 0, :].reshape(HX, HY, 128), axis=1)

    def entries(j):
        rows = [listed[16 * k + 4 * j + i : 16 * k + 4 * j + i + 1, :] for k in range(9) for i in range(4)]
        return jnp.concatenate(rows, axis=1)

    ecell, esec, ewt = entries(0), entries(1), entries(2)
    sec = esec.astype(I32)
    low = (iota((128, EN), 0) == (sec & 127)).astype(BF16)
    got = mm(jnp.concatenate(split3(force), axis=0), low)
    got = got[0:8] + got[8:16] + got[16:24]
    val = jnp.sum(jnp.where(iota((8, EN), 0) == (sec >> 7), got, 0.0), axis=0, keepdims=True) * ewt
    cell = ecell.astype(I32)
    cz = cell & 127
    place = cell >> 7
    cx = (place * 43691) >> 21
    cy = place - 48 * cx
    zv = jnp.where(iota((128, EN), 0) == cz, val, 0.0)
    zh, zl = split2(zv)
    for k, (sx, sy) in enumerate(body_parts()):
        lanes = slice(k * 512, (k + 1) * 512)
        x, y = cx[:, lanes], cy[:, lanes]
        planes = CX if sx == 0 else 4
        first = {0: 4, -1: 0, 1: 20}[sx]
        x = x - 12 if sx < 0 else x
        inside = (x >= 0) & (x < planes)
        if sy == 0:
            r = jnp.where(inside, x * YE + y + 8, -1)
            rows = planes * YE
        else:
            y = y - 40 if sy < 0 else y
            inside = inside & (y >= 0) & (y < 8)
            r = jnp.where(inside, x * 8 + y, -1)
            rows = planes * 8
        spot = (iota((rows, 512), 0) == r).astype(BF16)
        part = nt(spot, zh[:, lanes]) + nt(spot, zl[:, lanes])
        if sy == 0:
            b[first : first + planes] = part.reshape(planes, YE, 128)
        else:
            at = 0 if sy < 0 else 56
            b[first : first + planes, at : at + 8] = b[first : first + planes, at : at + 8] + part.reshape(planes, 8, 128)

    finish_all(copies[:4])
    u = lambda c, at, part, j: x3[part // 2, at + j] if part != 1 else free[c, j]

    def s1(p, part, j):
        dp[p] = b[p] * invd[p]

    def s2(i, part, j):
        p = i + 1
        pr0[i] = u(0, 0, part, j) + (b[p] + dp[p - 1] + dp[p + 1] + s_yz(dp[p])) * invd[p]

    def s3(t, part, j):
        ya, yb = y_parts(u(1, 3, part, j))
        za, zb = zdiff_parts(u(2, 5, part, j))
        tg = -0.5 * ((pr0[t + 2] - pr0[t]) + (yb - ya) + (zb - za))
        target[t] = tg
        corr0[t] = 0.8 * tg * invp[t]

    def s4(c, part, j):
        t = c + 1
        v = corr0[t]
        corr1[c] = 0.2 * v + 0.8 * (target[t] + corr0[t - 1] + corr0[t + 1] + s_yz(v)) * invp[t]

    three(24, 4, s1)
    three(22, 3, s2)
    finish_all(copies[4:])
    three(20, 2, s3)
    three(18, 1, s4)

    def s5(g, carry):
        halves, picks = [], []
        for k in range(4):
            x = 4 * g + k
            v = corr1[x + 1]
            full = target[x + 2] + corr1[x] + corr1[x + 2] + s_yz(v)
            res = full[8:56] - v[8:56] / invp[x + 2, MID, :]
            code = codes[x, MID, :]
            hi, lo = split2(jnp.concatenate([jnp.where(code == float(n + 1), res, 0.0) for n in range(7)], axis=0))
            halves += [hi, lo]
            picks += [(iota((256, 128), 1) == x).astype(BF16)]
        part = mm(jnp.concatenate(halves, axis=1), jnp.concatenate(picks, axis=0))
        acc[...] = jnp.where(g == 0, part, acc[...] + part)
        return carry

    acc[...] = jnp.zeros(acc.shape, F32)
    lax.fori_loop(0, CX // 4, s5, 0)
    for last, out in ((1 - (hx & 1), near), (hx & 1, far)):
        out[0:3] = corr1[pl.ds(1 + last * (CX - 3), 3)]
        out[3:6] = codes[pl.ds(last * (CX - 3), 3)]
    window = mm(gfold[...], acc[...], HIGH) * float(384.0**-0.5)
    blank = jnp.zeros((32, 128), F32)
    spread = jnp.concatenate(
        [jnp.concatenate([window if j == q else blank for j in range(4)], axis=1) for q in range(4)], axis=0
    )
    m = iota((128, 1), 0)
    plane = 8 * (m & 15) + (m >> 4)
    c0 = table[0, :, 0:1].astype(I32)
    c1 = table[0, :, 1:2].astype(I32)
    lane = iota((128, 128), 1)
    wants = []
    for blk in (2 * plane, 2 * plane + 1, c0, c1):
        half = blk & 1
        pln = blk >> 1
        pln = pln - jnp.where((half == 0) & (hy == HY - 1), 1, 0) + jnp.where((half == 1) & (hy == 0), 1, 0)
        at = pln - CX * hx
        at = jnp.where((at >= 0) & (at < CX), at, -1)
        wants.append((lane == at).astype(F32))
    send[...] = jnp.broadcast_to(nt(jnp.concatenate(wants, axis=1), spread, HIGH)[:, None, :], send.shape)


def coarse_kernel(cols, recv, blocks, table, out, ab, diag, sem):
    hx, hy = here()
    copy = pltpu.make_async_copy(blocks.at[pl.ds(2 * hx, 2)], ab, sem)
    copy.start()
    c0, c1 = cols[1, 2 * hx], cols[1, 2 * hx + 1]
    half = (0, 1, c0 & 1, c1 & 1)
    m = hx * HY + hy
    diag[...] = jnp.ones((8, 128), F32)
    diag[0:1, :] = table[1, pl.ds(m, 1), :]
    diag[1:2, :] = table[2, pl.ds(m, 1), :]
    for i, c in enumerate((c0, c1)):
        pln = c >> 1
        diag[2 + i : 3 + i, :] = table[1 + (c & 1), pl.ds((pln & 7) * HY + (pln >> 3), 1), :]
    z = jnp.sum(recv[:, 0, :].reshape(HX, HY, 128), axis=0)
    r, c = iota((128, 1024), 0), iota((128, 1024), 1)
    later = (c >> 7) & 1
    m16 = (c + 4) & 15
    place = ((r >> 5) == (c >> 8)) & ((r & 31) == m16 + 16 * later) & ((later == 0) | (m16 < 8))
    y3 = mm(jnp.concatenate(split3(z), axis=0), place.astype(BF16))
    y = y3[0:16] + y3[16:32] + y3[32:48]
    lane = iota((HY, 128), 1)
    hys = iota((HY, 128), 0)
    rows = []
    for q in range(4):
        slot = (lane + 4 + 128 * half[q] - 16 * hys) & 255
        a = jnp.where(slot < 16, y[:, (2 * q) * 128 : (2 * q + 1) * 128], 0.0)
        b = jnp.where((slot >= 16) & (slot < 24), y[:, (2 * q + 1) * 128 : (2 * q + 2) * 128], 0.0)
        rows.append(jnp.sum(a + b, axis=0, keepdims=True))
    res = jnp.concatenate(rows + [jnp.zeros((4, 128), F32)], axis=0)
    first = 0.8 * res / diag[...]
    seconds = []
    copy.wait()
    parts = jnp.concatenate(split3(first), axis=0)

    def product(block, row):
        hi, lo = split2(block)
        both = nt(parts, hi) + nt(parts, lo)
        return both[row : row + 1] + both[8 + row : 9 + row] + both[16 + row : 17 + row]

    for i in range(2):
        applied = product(ab[i, 0], i) + product(ab[i, 1], 2 + i)
        seconds.append(first[i : i + 1] + 0.8 * (res[i : i + 1] - applied) / diag[i : i + 1, :])
    second = jnp.concatenate(seconds, axis=1)
    lane2 = iota((HY, 256), 1)
    slot = (lane2 + 4 - 16 * iota((HY, 256), 0)) & 255
    wide = jnp.broadcast_to(second, (HY, 256))
    d0 = jnp.where(slot < 16, wide, 0.0)
    d1 = jnp.where((slot >= 16) & (slot < 24), wide, 0.0)
    r, c = iota((512, 128), 0), iota((512, 128), 1)
    later = r >> 8
    m16 = (r + 4) & 15
    fold = (c == m16 + 16 * later) & ((later == 0) | (m16 < 8))
    w3 = mm(jnp.concatenate(split3(jnp.concatenate([d0, d1], axis=1)), axis=0), fold.astype(BF16))
    windows = w3[0:16] + w3[16:32] + w3[32:48]
    for i in range(HX):
        out[i * HY : (i + 1) * HY, :] = windows


def last_kernel(
    recv, corr1_in, codes_in, xnear, xfar, target_in, invp_in, pr0_in, free_in, pres_in, glift,
    vel_out, pres_out,
    win, c2, s1, s2, corr1, codes, target, invp, pr0, free, pres, xb, sems,
):
    hx, hy = here()
    mid = slice(1, CX + 1)
    copies = run(
        [(corr1_in.at[mid], corr1.at[mid]), (codes_in, codes), (xnear, xb.at[1 - (hx & 1)]), (xfar, xb.at[hx & 1])]
        + [(target_in, target), (invp_in, invp)]
        + [(pr0_in.at[3 : 3 + CX, MID], pr0), (free_in.at[1:3, :, MID], free), (pres_in, pres)],
        sems,
    )
    hx, hy = here()
    for i in range(24):
        p = jnp.clip(CX * hx - 4 + i, 0, 127)
        m = (p & 7) * HY + (p >> 3)
        win[i : i + 1, :] = recv[pl.ds(m, 1), :]
    w = win[0:24, :]
    lane = iota((24, 128), 1)
    w = jnp.where((lane < 4) & (hy == 0), pltpu.roll(w, 1, 0), w)
    w = jnp.where((lane >= 20) & (lane < 24) & (hy == HY - 1), pltpu.roll(w, 23, 0), w)
    win[0:24, :] = w
    win[24:128, :] = jnp.zeros((104, 128), F32)
    wt = win[...].T
    win[...] = wt

    def lift(i, part, j):
        column = jnp.sum(jnp.where(iota((32, 128), 1) == i + 1, win[0:32, :], 0.0), axis=1, keepdims=True)
        wide = jnp.broadcast_to(column, (32, 128))
        v = mm(glift[...], jnp.concatenate(split2(wide), axis=0))
        side = xb.at[part // 2]
        code = codes[j] if part == 1 else side[3 + j]
        lifted = corr1[j + 1] if part == 1 else side[j]
        for n in range(7):
            lifted = jnp.where(code == float(n + 1), lifted + v[n * YE : (n + 1) * YE], lifted)
        c2[i] = lifted

    finish_all(copies[:4])
    three(22, 3, lift)
    finish_all(copies[4:6])

    def sweep1(t, part, j):
        v = c2[t + 1]
        s1[t] = 0.2 * v + 0.8 * (target[t] + c2[t] + c2[t + 2] + s_yz(v)) * invp[t]

    def sweep2(c, part, j):
        v = s1[c + 1]
        s2[c] = 0.2 * v + 0.8 * (target[c + 1] + s1[c] + s1[c + 2] + s_yz(v)) * invp[c + 1]

    three(20, 2, sweep1)
    three(18, 1, sweep2)

    finish_all(copies[6:])

    def finish(x, carry):
        v = s2[x + 1]
        ya, yb = y_parts(v)
        za, zb = zdiff_parts(v)
        vel_out[0, x] = pr0[x] - 0.5 * (s2[x + 2] - s2[x])[8:56]
        vel_out[1, x] = free[0, x] - 0.5 * (yb - ya)[8:56]
        vel_out[2, x] = free[1, x] - 0.5 * (zb - za)[8:56]
        pres_out[x] = pres[x] + 0.7 * v[8:56]
        return carry

    lax.fori_loop(0, CX, finish, 0, unroll=2)


def tables():
    y = np.arange(CY)
    gfold = np.zeros((32, 7 * CY), np.float32)
    for d in range(7):
        gfold[y // 3 + d + 1, d * CY + y] = 1.0
    glift = np.zeros((7 * YE, 64), np.float32)
    for d in range(7):
        for yy in range(YE):
            slot = (yy - 8) // 3 + d + 1
            if 0 <= slot < 32:
                for part in range(2):
                    glift[d * YE + yy, part * 32 + slot] = 1.0
    return gfold, glift


def to_all(x):
    return lax.all_to_all(x, BOTH, 0, 0, tiled=True)


def pair(x, axis="hully"):
    return lax.ppermute(x, axis, [(i, i ^ 1) for i in range(HX if axis == "hullx" else HY)])


def across(x, axis="hully"):
    n = HX if axis == "hullx" else HY
    return lax.ppermute(x, axis, [(i, j) for k in range(1, n - 1, 2) for i, j in ((k, k + 1), (k + 1, k))])


def shift(x, by):
    return lax.ppermute(x, "hullx", [(i, i + by) for i in range(HX) if 0 <= i + by < HX])


def shp(*dims, dtype=F32):
    return jax.ShapeDtypeStruct(dims, dtype)


def local(
    velocity, pressure, mom_source, mom_diag, press_diag, agglomeration, coarse_blocks, coarse_columns,
    wake_cells, wake_sections, wake_weights, chord, radius, influence, resistance,
    body_cells, body_sections, body_weights,
):
    gfold, glift = (jnp.asarray(t) for t in tables())
    cols = coarse_columns.T
    block = lambda *n: pltpu.VMEM((*n, YE, CZ), F32)
    sems = lambda n: pltpu.SemaphoreType.DMA((n,))

    def call(kernel, name, outs, ins, scratch, args, out_specs=None):
        if out_specs is None:
            out_specs = (VM,) * len(outs) if isinstance(outs, tuple) else VM
        return pl.pallas_call(
            kernel, out_shape=outs, in_specs=ins, out_specs=out_specs,
            scratch_shapes=scratch, compiler_params=PARAMS, name=name,
        )(*args)

    xt, xh = call(
        packx_kernel, "packx", (shp(HALO + 1, CY, CZ),) * 2, [AN] * 8, [pltpu.VMEM((2, 4, 128), I32), sems(22)],
        (velocity, mom_source, pressure, mom_diag, press_diag)
        + tuple(a.reshape(4, 128) for a in (body_cells, body_sections, body_weights)),
    )
    x1lo, x1hi = shift(xt, 1), shift(xh, -1)

    keep, give = call(
        wake_kernel, "wake", (shp(8, 128),) * 2, [SM, SM, SM, AN, VM, VM, VM, AN],
        [pltpu.VMEM((8, 128), F32), pltpu.VMEM((2, 128, 128), F32), pltpu.VMEM((CX, CY, CZ), F32), sems(3)],
        (cols, chord, radius, velocity, wake_cells[None], wake_sections[None], wake_weights[None]) + (coarse_blocks,),
    )
    payload = call(join_kernel, "join", shp(128, 8, 128), [VM, VM], [], (keep, pair(give)))
    recv1 = to_all(payload)
    out1, state, table = call(
        trim1_kernel, "trim1", (shp(128, ROWS[0], 128), shp(3, 8, 128), shp(3, 128, 128)), [VM, VM],
        [pltpu.VMEM((2, 8, 8, 128), F32)], (recv1,) + (influence,),
    )
    recv2 = to_all(out1)

    ya_near, ya_far, yb_near, yb_far = call(
        packy_kernel, "packy", (shp(96, 8, CZ),) * 2 + (shp(104, 8, CZ),) * 2, [AN] * 10,
        [pltpu.VMEM((2, 2, CX, 8, CZ), F32), pltpu.VMEM((2, CX, 8, CZ), I32), sems(36)],
        (velocity, mom_source, pressure, mom_diag, press_diag, agglomeration, xt, x1lo, x1hi, payload),
    )
    ya_near, yb_near = pair(ya_near), pair(yb_near)
    ya_far, yb_far = across(ya_far), across(yb_far)
    free, invd, invp, codes, fxt, fxh = call(
        sweeps_kernel, "sweeps",
        (shp(3, CX, YE, CZ), shp(24, YE, CZ), shp(20, YE, CZ), shp(CX, YE, CZ)) + (shp(7, YE, CZ),) * 2,
        [VM] * 6 + [AN] * 7,
        [block(4, CX + 4), block(3, CX + 2), block(3, CX + 2), block(24), block(20), block(CX)]
        + [pltpu.VMEM((2, 96, 8, CZ), F32), pltpu.VMEM((2, 104, 8, CZ), F32), pltpu.VMEM((2, HALO, CY, CZ), F32), sems(6)],
        (velocity, mom_source, pressure, mom_diag, press_diag, agglomeration, ya_near, ya_far, yb_near, yb_far, x1lo, x1hi, state),
        (VM, AN, AN, AN, VM, VM),
    )
    x3near, x3far = pair(fxt, "hullx"), across(fxh, "hullx")

    out2, force = call(
        trim2_kernel, "trim2", (shp(128, ROWS[1], 128), shp(1, 8)), [SM, VM, VM, VM], [],
        (resistance, recv2, state, influence),
    )
    recv3 = to_all(out2)

    pr0, target, corr1, ct, ch, out4 = call(
        body_kernel, "body",
        (shp(22, YE, CZ), shp(20, YE, CZ), shp(18, YE, CZ), shp(6, YE, CZ), shp(6, YE, CZ), shp(128, ROWS[2], 128)),
        [VM] + [AN] * 12 + [VM],
        [block(24), pltpu.VMEM((144, 128), F32), block(24), block(20), pltpu.VMEM((7 * CY, 128), F32)]
        + [block(2, 7), block(3, CX), block(24), block(20), block(CX), pltpu.VMEM((3, 128, 128), F32), sems(15), sems(7)],
        (recv3, xt, yb_near, yb_far, x1lo, x1hi, x3near, x3far, free, invd, invp, codes, table, gfold),
    )
    recv4 = to_all(out4)
    cxnear, cxfar = pair(ct, "hullx"), across(ch, "hullx")
    out5 = call(
        coarse_kernel, "coarse", shp(128, 128), [SM, VM, AN, VM],
        [pltpu.VMEM((2, 2, 128, 128), F32), pltpu.VMEM((8, 128), F32), pltpu.SemaphoreType.DMA],
        (cols, recv4) + (coarse_blocks,) + (table,),
    )
    recv5 = to_all(out5[:, None, :])[:, 0, :]
    vel_new, pres_new = call(
        last_kernel, "last", (shp(3, CX, CY, CZ), shp(CX, CY, CZ)),
        [VM] + [AN] * 9 + [VM],
        [pltpu.VMEM((128, 128), F32), block(22), block(20), block(18), block(CX + 2), block(CX), block(20), block(20)]
        + [pltpu.VMEM((CX, CY, CZ), F32), pltpu.VMEM((2, CX, CY, CZ), F32), pltpu.VMEM((CX, CY, CZ), F32), block(2, 6), sems(9)],
        (recv5, corr1, codes, cxnear, cxfar, target, invp, pr0, free, pressure, glift.astype(BF16)),
    )
    section_force = force.reshape(8)
    return vel_new, pres_new, section_force


def solution(mesh):
    fine = P("hullx", "hully", None)
    vector = P(None, "hullx", "hully", None)
    flat = P(BOTH)
    in_specs = (
        vector, fine, vector, fine, fine, fine,
        P("hully", None, None, None), P("hully", None),
        flat, flat, flat, flat, flat, P(BOTH, None), P(), flat, flat, flat,
    )
    return jax.shard_map(local, mesh=mesh, in_specs=in_specs, out_specs=(vector, fine, flat), check_vma=False)
```

```python
import numpy as np
import jax
import jax.numpy as jnp
from jax import lax
from jax.experimental import pallas as pl
from jax.experimental.pallas import tpu as pltpu
from jax.sharding import PartitionSpec as P

HX, HY = 8, 16
CX, CY, CZ = 16, 48, 128
NSEC = 1024
BOTH = ("hullx", "hully")
ROWS = (4, 1, 4)
F32, BF16, I32 = jnp.float32, jnp.bfloat16, jnp.int32
HIGH = lax.Precision.HIGHEST
YE = 64
EN = 9 * 512

VM = pl.BlockSpec(memory_space=pltpu.VMEM)
SM = pl.BlockSpec(memory_space=pltpu.SMEM)
AN = pl.BlockSpec(memory_space=pl.ANY)
PARAMS = pltpu.CompilerParams(vmem_limit_bytes=67000000)


def here():
    return lax.axis_index("hullx"), lax.axis_index("hully")


def iota(shape, dim):
    return lax.broadcasted_iota(I32, shape, dim)


def split2(x):
    hi = x.astype(BF16)
    lo = (x - hi.astype(F32)).astype(BF16)
    return hi, lo


def split3(x):
    hi = x.astype(BF16)
    rest = x - hi.astype(F32)
    mid = rest.astype(BF16)
    lo = (rest - mid.astype(F32)).astype(BF16)
    return hi, mid, lo


def nt(a, b, precision=None):
    return lax.dot_general(a, b, (((1,), (1,)), ((), ())), precision=precision, preferred_element_type=F32)


def mm(a, b, precision=None):
    return lax.dot_general(a, b, (((1,), (0,)), ((), ())), precision=precision, preferred_element_type=F32)


def lane_row(column, start):
    spot = iota((8, 128), 1) == iota((8, 128), 0) + start
    return jnp.sum(jnp.where(spot, column, 0.0), axis=0, keepdims=True)


def total(x):
    return jnp.sum(jnp.sum(x, axis=1, keepdims=True), axis=0, keepdims=True)


def zdiff_parts(v):
    lane = iota(v.shape, 1)
    before = jnp.where(lane == 0, 0.0, pltpu.roll(v, 1, 1))
    after = jnp.where(lane == CZ - 1, 0.0, pltpu.roll(v, CZ - 1, 1))
    return before, after


def y_parts(v):
    return pltpu.roll(v, 1, 0), pltpu.roll(v, v.shape[0] - 1, 0)


def s_yz(v):
    a, b = y_parts(v)
    c, d = zdiff_parts(v)
    return (a + b) + (c + d)


def wake_kernel(cols, chord, radius, vel, wc_in, ws_in, ww_in, blocks, keep, give, row, ab, v, wc, ws, ww, sem):
    hx, hy = here()
    pairs = [(wc_in, wc), (ws_in, ws), (ww_in, ww), (vel.at[0], v)]
    copies = run(pairs + [(blocks.at[2 * hx + i, 0], ab.at[i]) for i in range(2)], sem)
    finish_all(copies[:3])
    cells = wc[...]
    place = cells >> 7
    spot = (iota((768, 256), 0) == place).astype(BF16)
    picked = jnp.zeros((128, 256), F32)
    copies[3].wait()
    for part in split2(v[...].reshape(768, 128)):
        picked = picked + lax.dot_general(part, spot, (((0,), (0,)), ((), ())), preferred_element_type=F32)
    samples = jnp.sum(jnp.where(iota((128, 256), 0) == (cells & 127), picked, 0.0), axis=0, keepdims=True) * ww[...]
    sec = ws[...]
    high = jnp.where(iota((8, 256), 0) == (sec >> 7), samples, 0.0)
    low = (iota((128, 256), 0) == (sec & 127)).astype(F32)
    row[...] = nt(high, low, HIGH)
    lane = iota((1, 128), 1)
    crow = rrow = jnp.zeros((1, 128), F32)
    for k in range(8):
        crow = jnp.where(lane == 8 * hy + k, chord[k], crow)
        rrow = jnp.where(lane == 8 * hy + k, radius[k], rrow)
    c0 = cols[1, 2 * hx].astype(F32)
    c1 = cols[1, 2 * hx + 1].astype(F32)
    colrow = jnp.where(lane == 0, c0, jnp.where(lane == 1, c1, 0.0))
    eye = iota((128, 128), 0) == iota((128, 128), 1)
    even = (hy & 1) == 0
    first, second = row[0:4, :], row[4:8, :]
    finish_all(copies[4:])
    d0 = jnp.sum(jnp.where(eye, ab[0], 0.0), axis=0, keepdims=True)
    d1 = jnp.sum(jnp.where(eye, ab[1], 0.0), axis=0, keepdims=True)
    keep[...] = jnp.concatenate([jnp.where(even, first, second), jnp.where(even, crow, rrow), d0, d1, colrow], axis=0)
    give[...] = jnp.concatenate(
        [jnp.where(even, second, first), jnp.where(even, rrow, crow), jnp.zeros((3, 128), F32)], axis=0
    )


def trim1_kernel(recv, infl, out, state, table, grouped):
    hx, hy = here()
    by_core = recv[...].reshape(HX, HY // 2, 2, 8, 128)
    for core in range(2):
        grouped[core] = jnp.sum(by_core[:, :, core], axis=1)
    wake = jnp.concatenate([jnp.sum(grouped[0], axis=0)[0:4], jnp.sum(grouped[1], axis=0)[0:4]], axis=0)
    chord = grouped[0, :, 4, :]
    radius = grouped[1, :, 4, :]
    table[0] = recv[:, 7, :]
    table[1] = recv[:, 5, :]
    table[2] = recv[:, 6, :]
    state[0] = wake
    state[1] = chord
    state[2] = radius
    circ = chord * (radius - wake)
    acc = infl[:, 0:128] * circ[0:1, :]
    for c in range(1, 8):
        acc = acc + infl[:, c * 128 : (c + 1) * 128] * circ[c : c + 1, :]
    row = lane_row(jnp.sum(acc, axis=1, keepdims=True), 8 * hy)
    out[...] = jnp.broadcast_to(row[None], out.shape)


def trim2_kernel(res, recv, state, infl, out, force):
    hx, hy = here()
    induced = jnp.sum(recv[:, 0, :].reshape(HX, HY, 128), axis=1)
    wake, chord, radius = state[0], state[1], state[2]
    circ = chord * (radius - wake)
    omega = 1.0 + 0.5 * (res[0] - total(circ * radius) * (1.0 / NSEC))
    circ = chord * (omega * radius - wake - induced)
    omega = omega + 0.5 * (res[0] - total(circ * radius) * (1.0 / NSEC))
    acc = infl[:, 0:128] * circ[0:1, :]
    for c in range(1, 8):
        acc = acc + infl[:, c * 128 : (c + 1) * 128] * circ[c : c + 1, :]
    induced2 = lane_row(jnp.sum(acc, axis=1, keepdims=True), 8 * hy)
    mine = (iota((8, 128), 0) == hx) & ((iota((8, 128), 1) >> 3) == hy)
    full = chord * (omega * radius - wake - induced2) * omega * radius
    row = jnp.sum(jnp.where(mine, full, 0.0), axis=0, keepdims=True)
    force[...] = pltpu.roll(row, lax.rem(128 - 8 * hy, 128), 1)[:, 0:8]
    out[...] = jnp.broadcast_to(row[None], out.shape)


MID = slice(8, 8 + CY)


def run(pairs, sems):
    copies = [pltpu.make_async_copy(src, dst, sems.at[i]) for i, (src, dst) in enumerate(pairs)]
    for c in copies:
        c.start()
    return copies


def finish_all(copies):
    for c in copies:
        c.wait()


def codes_of(agg, hx, hy, y0):
    rows = agg.shape[1]
    plane = iota(agg.shape, 0) + CX * hx
    group = lax.div(iota((1, rows, 128), 1) + y0, 3) + 16 * hy
    return (agg - plane * 256 - group + 4).astype(F32)


def widen(low, middle, high):
    return jnp.concatenate([low, middle, high], axis=0)


HALO = 17


def packx_kernel(vel, src, pres, mdiag, pdiag, bc, bs, bw, tail, head, ints, sems):
    ends = ((1, tail), (0, head))
    pairs = []
    for last, out in ends:
        end = lambda w: pl.ds(last * (CX - w), w)
        pairs += [(mdiag.at[end(4)], out.at[11:15]), (pdiag.at[end(2)], out.at[15:17])]
    pairs += [(bc, ints.at[0]), (bs, ints.at[1])]
    first = len(pairs)
    for last, out in ends:
        end = lambda w: pl.ds(last * (CX - w), w)
        pairs.append((bw, out.at[HALO, 8:12]))
        pairs.append((pres.at[end(2)], out.at[9:11]))
        for c in range(3):
            pairs.append((vel.at[c, end(2)], out.at[2 * c : 2 * c + 2]))
            pairs.append((src.at[c, end(1)], out.at[6 + c : 7 + c]))
    copies = run(pairs, sems)
    finish_all(copies[:first])
    for out in (tail, head):
        out[11:17] = 1.0 / (6.0 + out[11:17])
        out[HALO, 0:4] = ints[0].astype(F32)
        out[HALO, 4:8] = ints[1].astype(F32)
        out[HALO, 12:16] = jnp.zeros((4, 128), F32)
        out[HALO, 16:48] = jnp.zeros((32, 128), F32)
    finish_all(copies[first:])


def packy_kernel(
    vel, src, pres, mdiag, pdiag, agg, lists, xlo, xhi, token,
    near_a, far_a, near_b, far_b,
    edge, aedge, sems,
):
    hx, hy = here()
    odd = hy & 1
    ends = []
    for at, a, out in ((1 - odd, near_a, near_b), (odd, far_a, far_b)):
        row = pl.multiple_of((CY - 8) * at, 8)
        ends.append((pl.ds(row, 8), row, a, out))
    pairs = []
    for n, (rows, _, a, out) in enumerate(ends):
        pairs += [(mdiag.at[:, rows], edge.at[n, 0]), (pdiag.at[:, rows], edge.at[n, 1]), (agg.at[:, rows], aedge.at[n])]
    for rows, _, a, out in ends:
        for c in range(3):
            pairs.append((vel.at[c, :, rows], a.at[CX * c : CX * c + CX]))
            pairs.append((src.at[c, :, rows], a.at[48 + CX * c : 64 + CX * c]))
        pairs.append((pres.at[:, rows], out.at[0:CX]))
        for k, side in ((0, xlo), (1, xhi)):
            pairs.append((side.at[0:HALO, rows], out.at[pl.ds(64 + HALO * k, HALO)]))
            for j in range(2):
                pairs.append((side.at[HALO, slice(8 * j, 8 * j + 8)], out.at[100 + 2 * k + j]))
        for j in range(2):
            pairs.append((lists.at[HALO, slice(8 * j, 8 * j + 8)], out.at[98 + j]))
    copies = run(pairs, sems)
    finish_all(copies[:6])
    for n, (_, row, a, out) in enumerate(ends):
        out[16:32] = 1.0 / (6.0 + edge[n, 0])
        out[32:48] = 1.0 / (6.0 + edge[n, 1])
        out[48:64] = codes_of(aedge[n], hx, hy, row)
    finish_all(copies[6:])


def sweeps_kernel(
    vel_in, src_in, pres_in, mdiag_in, pdiag_in, agg_in, near_a, far_a, near_b, far_b, xlo, xhi, token,
    free_out, invd_out, invp_out, codes_out, near, far,
    v, s, q, invd, invp, codes, ya, yb, xb, vel, src, pres, mdiag, pdiag, agg, free, sems,
):
    hx, hy = here()
    odd = hy & 1
    finish_all(
        run(
            [(near_a, ya.at[1 - odd]), (far_a, ya.at[odd]), (near_b, yb.at[1 - odd]), (far_b, yb.at[odd])]
            + [(xlo.at[0:HALO], xb.at[0]), (xhi.at[0:HALO], xb.at[1])]
            + [(vel_in, vel), (src_in, src), (pres_in, pres), (mdiag_in, mdiag), (pdiag_in, pdiag), (agg_in, agg)],
            sems,
        )
    )
    yalo, yahi, ylo, yhi = ya.at[0], ya.at[1], yb.at[0], yb.at[1]
    for n in range(2):
        grown = lambda k: widen(ylo[64 + HALO * n + k], xb[n, k], yhi[64 + HALO * n + k])
        for k in range(2):
            for c in range(3):
                v[c, 18 * n + k] = grown(2 * c + k)
            v[3, 18 * n + k] = grown(9 + k)
            invp[18 * n + k] = grown(15 + k)
        for c in range(3):
            s[c, 17 * n] = grown(6 + c)
        for k in range(4):
            invd[20 * n + k] = grown(11 + k)

    def grow(x, carry):
        for c in range(3):
            v[c, x + 2] = widen(yalo[CX * c + x], vel[c, x], yahi[CX * c + x])
            s[c, x + 1] = widen(yalo[48 + CX * c + x], src[c, x], yahi[48 + CX * c + x])
        v[3, x + 2] = widen(ylo[x], pres[x], yhi[x])
        invd[x + 4] = widen(ylo[16 + x], 1.0 / (6.0 + mdiag[x]), yhi[16 + x])
        invp[x + 2] = widen(ylo[32 + x], 1.0 / (6.0 + pdiag[x]), yhi[32 + x])
        base = (CX * hx + x) * 256 + 16 * hy + lax.div(iota((CY, 128), 0), 3)
        codes[x] = widen(ylo[48 + x], (agg[x] - base + 4).astype(F32), yhi[48 + x])
        return carry

    lax.fori_loop(0, CX, grow, 0, unroll=2)

    copies = run([(invd, invd_out), (invp, invp_out), (codes, codes_out)], sems)

    def first(i, carry):
        inv = invd[i + 3]
        p = v[3, i + 1]
        ya, yb = y_parts(p)
        za, zb = zdiff_parts(p)
        for c, grad in enumerate((v[3, i + 2] - v[3, i], yb - ya, zb - za)):
            sc = s[c, i] - 0.5 * grad
            s[c, i] = sc
            q[c, i] = (sc + v[c, i] + v[c, i + 2] + s_yz(v[c, i + 1])) * inv
        return carry

    lax.fori_loop(0, CX + 2, first, 0, unroll=2)

    def second(x, carry):
        inv = invd[x + 4]
        for c in range(3):
            free[c, x] = (s[c, x + 1] + q[c, x] + q[c, x + 2] + s_yz(q[c, x + 1])) * inv
        return carry

    for k in range(4):
        lax.fori_loop(4 * k, 4 * k + 4, second, 0, unroll=2)
        part = slice(4 * k, 4 * k + 4)
        copy = pltpu.make_async_copy(free.at[:, part], free_out.at[:, part], sems.at[3 + k])
        copy.start()
        copies.append(copy)
    to = 0
    for c, w in enumerate((3, 2, 2)):
        near[to : to + w] = free[c, pl.ds((1 - (hx & 1)) * (CX - w), w)]
        far[to : to + w] = free[c, pl.ds((hx & 1) * (CX - w), w)]
        to += w
    finish_all(copies)


def body_parts():
    return [(sx, sy) for sy in (0, -1, 1) for sx in (0, -1, 1)]


def three(n, w, fn):
    for i in range(w):
        fn(i, 0, i)

    def own(j, carry):
        fn(j + w, 1, j)
        return carry

    lax.fori_loop(0, CX, own, 0, unroll=4)
    for i in range(n - CX - w):
        fn(CX + w + i, 2, i)


def body_kernel(
    recv, lists, ynear, yfar, xlo, xhi, unear, ufar, free_in, invd_in, invp_in, codes_in, table_in, gfold,
    pr0_out, target_out, corr1_out, near, far, send,
    pr0, target, corr1, b, listed, dp, corr0, acc, x3, free, invd, invp, codes, table, early_sems, sems,
):
    hx, hy = here()
    early = [(lists.at[HALO, 0:16], listed.at[0:16])]
    early += [(xlo.at[HALO, 0:16], listed.at[16:32]), (xhi.at[HALO, 0:16], listed.at[32:48])]
    for n, buf in ((1 - (hy & 1), ynear), (hy & 1, yfar)):
        for j in range(6):
            at = pl.multiple_of(48 + 48 * n + 8 * j, 8)
            early.append((buf.at[98 + j], listed.at[pl.ds(at, 8)]))
    early = run(early, early_sems)
    copies = run(
        [(invd_in, invd), (unear, x3.at[1 - (hx & 1)]), (ufar, x3.at[hx & 1]), (free_in, free), (invp_in, invp), (codes_in, codes), (table_in, table)],
        sems,
    )
    finish_all(early)
    force = jnp.sum(recv[:, 0, :].reshape(HX, HY, 128), axis=1)

    def entries(j):
        rows = [listed[16 * k + 4 * j + i : 16 * k + 4 * j + i + 1, :] for k in range(9) for i in range(4)]
        return jnp.concatenate(rows, axis=1)

    ecell, esec, ewt = entries(0), entries(1), entries(2)
    sec = esec.astype(I32)
    low = (iota((128, EN), 0) == (sec & 127)).astype(BF16)
    got = mm(jnp.concatenate(split3(force), axis=0), low)
    got = got[0:8] + got[8:16] + got[16:24]
    val = jnp.sum(jnp.where(iota((8, EN), 0) == (sec >> 7), got, 0.0), axis=0, keepdims=True) * ewt
    cell = ecell.astype(I32)
    cz = cell & 127
    place = cell >> 7
    cx = (place * 43691) >> 21
    cy = place - 48 * cx
    vh = val.astype(BF16).astype(F32)
    at_z = iota((128, EN), 0) == cz
    zh = jnp.where(at_z, vh, 0.0).astype(BF16)
    zl = jnp.where(at_z, val - vh, 0.0).astype(BF16)
    for k, (sx, sy) in enumerate(body_parts()):
        lanes = slice(k * 512, (k + 1) * 512)
        x, y = cx[:, lanes], cy[:, lanes]
        planes = CX if sx == 0 else 4
        first = {0: 4, -1: 0, 1: 20}[sx]
        x = x - 12 if sx < 0 else x
        inside = (x >= 0) & (x < planes)
        if sy == 0:
            r = jnp.where(inside, x * YE + y + 8, -1)
            rows = planes * YE
        else:
            y = y - 40 if sy < 0 else y
            inside = inside & (y >= 0) & (y < 8)
            r = jnp.where(inside, x * 8 + y, -1)
            rows = planes * 8
        spot = (iota((rows, 512), 0) == r).astype(BF16)
        part = nt(spot, zh[:, lanes]) + nt(spot, zl[:, lanes])
        if sy == 0:
            b[first : first + planes] = part.reshape(planes, YE, 128)
        else:
            at = 0 if sy < 0 else 56
            b[first : first + planes, at : at + 8] = b[first : first + planes, at : at + 8] + part.reshape(planes, 8, 128)

    finish_all(copies[:4])
    u = lambda c, at, part, j: x3[part // 2, at + j] if part != 1 else free[c, j]

    def s1(p, part, j):
        dp[p] = b[p] * invd[p]

    def s2(i, part, j):
        p = i + 1
        pr0[i] = u(0, 0, part, j) + (b[p] + dp[p - 1] + dp[p + 1] + s_yz(dp[p])) * invd[p]

    def s3(t, part, j):
        ya, yb = y_parts(u(1, 3, part, j))
        za, zb = zdiff_parts(u(2, 5, part, j))
        tg = -0.5 * ((pr0[t + 2] - pr0[t]) + (yb - ya) + (zb - za))
        target[t] = tg
        corr0[t] = 0.8 * tg * invp[t]

    def s4(c, part, j):
        t = c + 1
        v = corr0[t]
        corr1[c] = 0.2 * v + 0.8 * (target[t] + corr0[t - 1] + corr0[t + 1] + s_yz(v)) * invp[t]

    three(24, 4, s1)
    three(22, 3, s2)
    results = run([(pr0, pr0_out)], early_sems)
    finish_all(copies[4:])
    three(20, 2, s3)
    three(18, 1, s4)
    results += run([(target, target_out), (corr1, corr1_out)], sems)

    def s5(g, carry):
        halves, picks = [], []
        for k in range(4):
            x = 4 * g + k
            v = corr1[x + 1]
            full = target[x + 2] + corr1[x] + corr1[x + 2] + s_yz(v)
            res = full[8:56] - v[8:56] / invp[x + 2, MID, :]
            code = codes[x, MID, :]
            high = res.astype(BF16).astype(F32)
            for half in (high, res - high):
                picked = [jnp.where(code == float(n + 1), half, 0.0) for n in range(7)]
                halves.append(jnp.concatenate(picked, axis=0).astype(BF16))
            picks += [(iota((256, 128), 1) == x).astype(BF16)]
        part = mm(jnp.concatenate(halves, axis=1), jnp.concatenate(picks, axis=0))
        acc[...] = jnp.where(g == 0, part, acc[...] + part)
        return carry

    acc[...] = jnp.zeros(acc.shape, F32)
    lax.fori_loop(0, CX // 4, s5, 0)
    for last, out in ((1 - (hx & 1), near), (hx & 1, far)):
        out[0:3] = corr1[pl.ds(1 + last * (CX - 3), 3)]
        out[3:6] = codes[pl.ds(last * (CX - 3), 3)]
    window = mm(gfold[...], acc[...], HIGH) * float(384.0**-0.5)
    blank = jnp.zeros((32, 128), F32)
    spread = jnp.concatenate(
        [jnp.concatenate([window if j == q else blank for j in range(4)], axis=1) for q in range(4)], axis=0
    )
    m = iota((128, 1), 0)
    plane = 8 * (m & 15) + (m >> 4)
    c0 = table[0, :, 0:1].astype(I32)
    c1 = table[0, :, 1:2].astype(I32)
    lane = iota((128, 128), 1)
    wants = []
    for blk in (2 * plane, 2 * plane + 1, c0, c1):
        half = blk & 1
        pln = blk >> 1
        pln = pln - jnp.where((half == 0) & (hy == HY - 1), 1, 0) + jnp.where((half == 1) & (hy == 0), 1, 0)
        at = pln - CX * hx
        at = jnp.where((at >= 0) & (at < CX), at, -1)
        wants.append((lane == at).astype(F32))
    send[...] = jnp.broadcast_to(nt(jnp.concatenate(wants, axis=1), spread, HIGH)[:, None, :], send.shape)
    finish_all(results)


def coarse_kernel(cols, recv_in, blocks, table_in, out, ab, diag, recv, table, sem):
    hx, hy = here()
    copies = run([(recv_in, recv), (table_in, table), (blocks.at[pl.ds(2 * hx, 2)], ab)], sem)
    c0, c1 = cols[1, 2 * hx], cols[1, 2 * hx + 1]
    half = (0, 1, c0 & 1, c1 & 1)
    m = hx * HY + hy
    diag[...] = jnp.ones((8, 128), F32)
    finish_all(copies[:2])
    diag[0:1, :] = table[1, pl.ds(m, 1), :]
    diag[1:2, :] = table[2, pl.ds(m, 1), :]
    for i, c in enumerate((c0, c1)):
        pln = c >> 1
        diag[2 + i : 3 + i, :] = table[1 + (c & 1), pl.ds((pln & 7) * HY + (pln >> 3), 1), :]
    z = jnp.sum(recv[:, 0, :].reshape(HX, HY, 128), axis=0)
    r, c = iota((128, 1024), 0), iota((128, 1024), 1)
    later = (c >> 7) & 1
    m16 = (c + 4) & 15
    place = ((r >> 5) == (c >> 8)) & ((r & 31) == m16 + 16 * later) & ((later == 0) | (m16 < 8))
    y3 = mm(jnp.concatenate(split3(z), axis=0), place.astype(BF16))
    y = y3[0:16] + y3[16:32] + y3[32:48]
    lane = iota((HY, 128), 1)
    hys = iota((HY, 128), 0)
    rows = []
    for q in range(4):
        slot = (lane + 4 + 128 * half[q] - 16 * hys) & 255
        a = jnp.where(slot < 16, y[:, (2 * q) * 128 : (2 * q + 1) * 128], 0.0)
        b = jnp.where((slot >= 16) & (slot < 24), y[:, (2 * q + 1) * 128 : (2 * q + 2) * 128], 0.0)
        rows.append(jnp.sum(a + b, axis=0, keepdims=True))
    res = jnp.concatenate(rows + [jnp.zeros((4, 128), F32)], axis=0)
    first = 0.8 * res / diag[...]
    seconds = []
    copies[2].wait()
    parts = jnp.concatenate(split3(first), axis=0)

    def product(block, row):
        hi, lo = split2(block)
        both = nt(parts, hi) + nt(parts, lo)
        return both[row : row + 1] + both[8 + row : 9 + row] + both[16 + row : 17 + row]

    for i in range(2):
        applied = product(ab[i, 0], i) + product(ab[i, 1], 2 + i)
        seconds.append(first[i : i + 1] + 0.8 * (res[i : i + 1] - applied) / diag[i : i + 1, :])
    second = jnp.concatenate(seconds, axis=1)
    lane2 = iota((HY, 256), 1)
    slot = (lane2 + 4 - 16 * iota((HY, 256), 0)) & 255
    wide = jnp.broadcast_to(second, (HY, 256))
    d0 = jnp.where(slot < 16, wide, 0.0)
    d1 = jnp.where((slot >= 16) & (slot < 24), wide, 0.0)
    r, c = iota((512, 128), 0), iota((512, 128), 1)
    later = r >> 8
    m16 = (r + 4) & 15
    fold = (c == m16 + 16 * later) & ((later == 0) | (m16 < 8))
    w3 = mm(jnp.concatenate(split3(jnp.concatenate([d0, d1], axis=1)), axis=0), fold.astype(BF16))
    windows = w3[0:16] + w3[16:32] + w3[32:48]
    for i in range(HX):
        out[i * HY : (i + 1) * HY, :] = windows


def last_kernel(
    recv, corr1_in, codes_in, xnear, xfar, target_in, invp_in, pr0_in, free_in, pres_in, glift,
    vel_hbm, pres_hbm,
    vel_out, pres_out, win, c2, s1, s2, corr1, codes, target, invp, pr0, free, pres, xb, sems,
):
    hx, hy = here()
    mid = slice(1, CX + 1)
    copies = run(
        [(corr1_in.at[mid], corr1.at[mid]), (codes_in, codes), (xnear, xb.at[1 - (hx & 1)]), (xfar, xb.at[hx & 1])]
        + [(target_in, target), (invp_in, invp)]
        + [(pr0_in.at[3 : 3 + CX, MID], pr0), (free_in.at[1:3, :, MID], free), (pres_in, pres)],
        sems,
    )
    hx, hy = here()
    for i in range(24):
        p = jnp.clip(CX * hx - 4 + i, 0, 127)
        m = (p & 7) * HY + (p >> 3)
        win[i : i + 1, :] = recv[pl.ds(m, 1), :]
    w = win[0:24, :]
    lane = iota((24, 128), 1)
    w = jnp.where((lane < 4) & (hy == 0), pltpu.roll(w, 1, 0), w)
    w = jnp.where((lane >= 20) & (lane < 24) & (hy == HY - 1), pltpu.roll(w, 23, 0), w)
    win[0:24, :] = w
    win[24:128, :] = jnp.zeros((104, 128), F32)
    wt = win[...].T
    win[...] = wt

    def lift(i, part, j):
        column = jnp.sum(jnp.where(iota((32, 128), 1) == i + 1, win[0:32, :], 0.0), axis=1, keepdims=True)
        wide = jnp.broadcast_to(column, (32, 128))
        v = mm(glift[...], jnp.concatenate(split2(wide), axis=0))
        side = xb.at[part // 2]
        code = codes[j] if part == 1 else side[3 + j]
        lifted = corr1[j + 1] if part == 1 else side[j]
        for n in range(7):
            lifted = jnp.where(code == float(n + 1), lifted + v[n * YE : (n + 1) * YE], lifted)
        c2[i] = lifted

    finish_all(copies[:4])
    three(22, 3, lift)
    finish_all(copies[4:6])

    def sweep1(t, part, j):
        v = c2[t + 1]
        s1[t] = 0.2 * v + 0.8 * (target[t] + c2[t] + c2[t + 2] + s_yz(v)) * invp[t]

    def sweep2(c, part, j):
        v = s1[c + 1]
        s2[c] = 0.2 * v + 0.8 * (target[c + 1] + s1[c] + s1[c + 2] + s_yz(v)) * invp[c + 1]

    three(20, 2, sweep1)
    three(18, 1, sweep2)

    finish_all(copies[6:])

    def finish(x, carry):
        v = s2[x + 1]
        ya, yb = y_parts(v)
        za, zb = zdiff_parts(v)
        vel_out[0, x] = pr0[x] - 0.5 * (s2[x + 2] - s2[x])[8:56]
        vel_out[1, x] = free[0, x] - 0.5 * (yb - ya)[8:56]
        vel_out[2, x] = free[1, x] - 0.5 * (zb - za)[8:56]
        pres_out[x] = pres[x] + 0.7 * v[8:56]
        return carry

    results = []
    for k in range(4):
        lax.fori_loop(4 * k, 4 * k + 4, finish, 0, unroll=2)
        part = slice(4 * k, 4 * k + 4)
        for n, (src, dst) in enumerate(((vel_out.at[:, part], vel_hbm.at[:, part]), (pres_out.at[part], pres_hbm.at[part]))):
            copy = pltpu.make_async_copy(src, dst, sems.at[2 * k + n])
            copy.start()
            results.append(copy)
    finish_all(results)


def tables():
    y = np.arange(CY)
    gfold = np.zeros((32, 7 * CY), np.float32)
    for d in range(7):
        gfold[y // 3 + d + 1, d * CY + y] = 1.0
    glift = np.zeros((7 * YE, 64), np.float32)
    for d in range(7):
        for yy in range(YE):
            slot = (yy - 8) // 3 + d + 1
            if 0 <= slot < 32:
                for part in range(2):
                    glift[d * YE + yy, part * 32 + slot] = 1.0
    return gfold, glift


def to_all(x):
    return lax.all_to_all(x, BOTH, 0, 0, tiled=True)


def pair(x, axis="hully"):
    return lax.ppermute(x, axis, [(i, i ^ 1) for i in range(HX if axis == "hullx" else HY)])


def across(x, axis="hully"):
    n = HX if axis == "hullx" else HY
    return lax.ppermute(x, axis, [(i, j) for k in range(1, n - 1, 2) for i, j in ((k, k + 1), (k + 1, k))])


def shift(x, by):
    return lax.ppermute(x, "hullx", [(i, i + by) for i in range(HX) if 0 <= i + by < HX])


def shp(*dims, dtype=F32):
    return jax.ShapeDtypeStruct(dims, dtype)


def local(
    velocity, pressure, mom_source, mom_diag, press_diag, agglomeration, coarse_blocks, coarse_columns,
    wake_cells, wake_sections, wake_weights, chord, radius, influence, resistance,
    body_cells, body_sections, body_weights,
):
    gfold, glift = (jnp.asarray(t) for t in tables())
    cols = coarse_columns.T
    block = lambda *n: pltpu.VMEM((*n, YE, CZ), F32)
    sems = lambda n: pltpu.SemaphoreType.DMA((n,))

    def call(kernel, name, outs, ins, scratch, args, out_specs=None):
        if out_specs is None:
            out_specs = (VM,) * len(outs) if isinstance(outs, tuple) else VM
        return pl.pallas_call(
            kernel, out_shape=outs, in_specs=ins, out_specs=out_specs,
            scratch_shapes=scratch, compiler_params=PARAMS, name=name,
        )(*args)

    xt, xh = call(
        packx_kernel, "packx", (shp(HALO + 1, CY, CZ),) * 2, [AN] * 8, [pltpu.VMEM((2, 4, 128), I32), sems(22)],
        (velocity, mom_source, pressure, mom_diag, press_diag)
        + tuple(a.reshape(4, 128) for a in (body_cells, body_sections, body_weights)),
    )
    x1lo, x1hi = shift(xt, 1), shift(xh, -1)

    keep, give = call(
        wake_kernel, "wake", (shp(8, 128),) * 2, [SM, SM, SM] + [AN] * 5,
        [pltpu.VMEM((8, 128), F32), pltpu.VMEM((2, 128, 128), F32), pltpu.VMEM((CX, CY, CZ), F32)]
        + [pltpu.VMEM((1, 256), I32)] * 2 + [pltpu.VMEM((1, 256), F32), sems(6)],
        (cols, chord, radius, velocity, wake_cells[None], wake_sections[None], wake_weights[None]) + (coarse_blocks,),
    )
    payload = jnp.broadcast_to((keep + pair(give))[None], (128, 8, 128))
    recv1 = to_all(payload)
    out1, state, table = call(
        trim1_kernel, "trim1", (shp(128, ROWS[0], 128), shp(3, 8, 128), shp(3, 128, 128)), [VM, VM],
        [pltpu.VMEM((2, 8, 8, 128), F32)], (recv1,) + (influence,),
    )
    recv2 = to_all(out1)

    ya_near, ya_far, yb_near, yb_far = call(
        packy_kernel, "packy", (shp(96, 8, CZ),) * 2 + (shp(104, 8, CZ),) * 2, [AN] * 10,
        [pltpu.VMEM((2, 2, CX, 8, CZ), F32), pltpu.VMEM((2, CX, 8, CZ), I32), sems(36)],
        (velocity, mom_source, pressure, mom_diag, press_diag, agglomeration, xt, x1lo, x1hi, payload),
        (VM, VM, VM, VM),
    )
    ya_near, yb_near = pair(ya_near), pair(yb_near)
    ya_far, yb_far = across(ya_far), across(yb_far)
    free, invd, invp, codes, fxt, fxh = call(
        sweeps_kernel, "sweeps",
        (shp(3, CX, YE, CZ), shp(24, YE, CZ), shp(20, YE, CZ), shp(CX, YE, CZ)) + (shp(7, YE, CZ),) * 2,
        [AN] * 13,
        [block(4, CX + 4), block(3, CX + 2), block(3, CX + 2), block(24), block(20), block(CX)]
        + [pltpu.VMEM((2, 96, 8, CZ), F32), pltpu.VMEM((2, 104, 8, CZ), F32), pltpu.VMEM((2, HALO, CY, CZ), F32)]
        + [pltpu.VMEM((3, CX, CY, CZ), F32)] * 2 + [pltpu.VMEM((CX, CY, CZ), F32)] * 3
        + [pltpu.VMEM((CX, CY, CZ), I32), block(3, CX), sems(12)],
        (velocity, mom_source, pressure, mom_diag, press_diag, agglomeration, ya_near, ya_far, yb_near, yb_far, x1lo, x1hi, state),
        (AN, AN, AN, AN, VM, VM),
    )
    x3near, x3far = pair(fxt, "hullx"), across(fxh, "hullx")

    out2, force = call(
        trim2_kernel, "trim2", (shp(128, ROWS[1], 128), shp(1, 8)), [SM, VM, VM, VM], [],
        (resistance, recv2, state, influence),
    )
    recv3 = to_all(out2)

    pr0, target, corr1, ct, ch, out4 = call(
        body_kernel, "body",
        (shp(22, YE, CZ), shp(20, YE, CZ), shp(18, YE, CZ), shp(6, YE, CZ), shp(6, YE, CZ), shp(128, ROWS[2], 128)),
        [VM] + [AN] * 12 + [VM],
        [block(22), block(20), block(18), block(24), pltpu.VMEM((144, 128), F32), block(24), block(20), pltpu.VMEM((7 * CY, 128), F32)]
        + [block(2, 7), block(3, CX), block(24), block(20), block(CX), pltpu.VMEM((3, 128, 128), F32), sems(15), sems(7)],
        (recv3, xt, yb_near, yb_far, x1lo, x1hi, x3near, x3far, free, invd, invp, codes, table, gfold),
        (AN, AN, AN, VM, VM, VM),
    )
    recv4 = to_all(out4)
    cxnear, cxfar = pair(ct, "hullx"), across(ch, "hullx")
    out5 = call(
        coarse_kernel, "coarse", shp(128, 128), [SM, AN, AN, AN],
        [pltpu.VMEM((2, 2, 128, 128), F32), pltpu.VMEM((8, 128), F32), pltpu.VMEM((128, 4, 128), F32)]
        + [pltpu.VMEM((3, 128, 128), F32), sems(3)],
        (cols, recv4, coarse_blocks, table),
    )
    recv5 = to_all(out5[:, None, :])[:, 0, :]
    vel_new, pres_new = call(
        last_kernel, "last", (shp(3, CX, CY, CZ), shp(CX, CY, CZ)),
        [VM] + [AN] * 9 + [VM],
        [pltpu.VMEM((3, CX, CY, CZ), F32), pltpu.VMEM((CX, CY, CZ), F32)]
        + [pltpu.VMEM((128, 128), F32), block(22), block(20), block(18), block(CX + 2), block(CX), block(20), block(20)]
        + [pltpu.VMEM((CX, CY, CZ), F32), pltpu.VMEM((2, CX, CY, CZ), F32), pltpu.VMEM((CX, CY, CZ), F32), block(2, 6), sems(9)],
        (recv5, corr1, codes, cxnear, cxfar, target, invp, pr0, free, pressure, glift.astype(BF16)),
        (AN, AN),
    )
    section_force = force.reshape(8)
    return vel_new, pres_new, section_force


def solution(mesh):
    fine = P("hullx", "hully", None)
    vector = P(None, "hullx", "hully", None)
    flat = P(BOTH)
    in_specs = (
        vector, fine, vector, fine, fine, fine,
        P("hully", None, None, None), P("hully", None),
        flat, flat, flat, flat, flat, P(BOTH, None), P(), flat, flat, flat,
    )
    return jax.shard_map(local, mesh=mesh, in_specs=in_specs, out_specs=(vector, fine, flat), check_vma=False)
```

```python
import numpy as np
import jax
import jax.numpy as jnp
from jax import lax
from jax.experimental import pallas as pl
from jax.experimental.pallas import tpu as pltpu
from jax.sharding import PartitionSpec as P

HX, HY = 8, 16
CX, CY, CZ = 16, 48, 128
NSEC = 1024
BOTH = ("hullx", "hully")
ROWS = (4, 1, 4)
F32, BF16, I32 = jnp.float32, jnp.bfloat16, jnp.int32
HIGH = lax.Precision.HIGHEST
YE = 64
EN = 9 * 512

VM = pl.BlockSpec(memory_space=pltpu.VMEM)
SM = pl.BlockSpec(memory_space=pltpu.SMEM)
AN = pl.BlockSpec(memory_space=pl.ANY)
PARAMS = pltpu.CompilerParams(vmem_limit_bytes=67000000)


def here():
    return lax.axis_index("hullx"), lax.axis_index("hully")


def iota(shape, dim):
    return lax.broadcasted_iota(I32, shape, dim)


def split2(x):
    hi = x.astype(BF16)
    lo = (x - hi.astype(F32)).astype(BF16)
    return hi, lo


def split3(x):
    hi = x.astype(BF16)
    rest = x - hi.astype(F32)
    mid = rest.astype(BF16)
    lo = (rest - mid.astype(F32)).astype(BF16)
    return hi, mid, lo


def nt(a, b, precision=None):
    return lax.dot_general(a, b, (((1,), (1,)), ((), ())), precision=precision, preferred_element_type=F32)


def mm(a, b, precision=None):
    return lax.dot_general(a, b, (((1,), (0,)), ((), ())), precision=precision, preferred_element_type=F32)


def lane_row(column, start):
    spot = iota((8, 128), 1) == iota((8, 128), 0) + start
    return jnp.sum(jnp.where(spot, column, 0.0), axis=0, keepdims=True)


def total(x):
    return jnp.sum(jnp.sum(x, axis=1, keepdims=True), axis=0, keepdims=True)


def zdiff_parts(v):
    lane = iota(v.shape, 1)
    before = jnp.where(lane == 0, 0.0, pltpu.roll(v, 1, 1))
    after = jnp.where(lane == CZ - 1, 0.0, pltpu.roll(v, CZ - 1, 1))
    return before, after


def y_parts(v):
    return pltpu.roll(v, 1, 0), pltpu.roll(v, v.shape[0] - 1, 0)


def s_yz(v):
    a, b = y_parts(v)
    c, d = zdiff_parts(v)
    return (a + b) + (c + d)


def wake_kernel(cols, chord, radius, vel, wc_in, ws_in, ww_in, blocks, keep, give, row, ab, v, wc, ws, ww, sem):
    hx, hy = here()
    pairs = [(wc_in, wc), (ws_in, ws), (ww_in, ww), (vel.at[0], v)]
    copies = run(pairs + [(blocks.at[2 * hx + i, 0], ab.at[i]) for i in range(2)], sem)
    finish_all(copies[:3])
    cells = wc[...]
    place = cells >> 7
    spot = (iota((768, 256), 0) == place).astype(BF16)
    picked = jnp.zeros((128, 256), F32)
    copies[3].wait()
    for part in split2(v[...].reshape(768, 128)):
        picked = picked + lax.dot_general(part, spot, (((0,), (0,)), ((), ())), preferred_element_type=F32)
    samples = jnp.sum(jnp.where(iota((128, 256), 0) == (cells & 127), picked, 0.0), axis=0, keepdims=True) * ww[...]
    sec = ws[...]
    high = jnp.where(iota((8, 256), 0) == (sec >> 7), samples, 0.0)
    low = (iota((128, 256), 0) == (sec & 127)).astype(F32)
    row[...] = nt(high, low, HIGH)
    lane = iota((1, 128), 1)
    crow = rrow = jnp.zeros((1, 128), F32)
    for k in range(8):
        crow = jnp.where(lane == 8 * hy + k, chord[k], crow)
        rrow = jnp.where(lane == 8 * hy + k, radius[k], rrow)
    c0 = cols[1, 2 * hx].astype(F32)
    c1 = cols[1, 2 * hx + 1].astype(F32)
    colrow = jnp.where(lane == 0, c0, jnp.where(lane == 1, c1, 0.0))
    eye = iota((128, 128), 0) == iota((128, 128), 1)
    even = (hy & 1) == 0
    first, second = row[0:4, :], row[4:8, :]
    finish_all(copies[4:])
    d0 = jnp.sum(jnp.where(eye, ab[0], 0.0), axis=0, keepdims=True)
    d1 = jnp.sum(jnp.where(eye, ab[1], 0.0), axis=0, keepdims=True)
    keep[...] = jnp.concatenate([jnp.where(even, first, second), jnp.where(even, crow, rrow), d0, d1, colrow], axis=0)
    give[...] = jnp.concatenate(
        [jnp.where(even, second, first), jnp.where(even, rrow, crow), jnp.zeros((3, 128), F32)], axis=0
    )


def join_kernel(keep, got, out):
    out[...] = jnp.broadcast_to((keep[...] + got[...])[None], out.shape)


def trim1_kernel(recv, infl, out, state, table, grouped):
    hx, hy = here()
    by_core = recv[...].reshape(HX, HY // 2, 2, 8, 128)
    for core in range(2):
        grouped[core] = jnp.sum(by_core[:, :, core], axis=1)
    wake = jnp.concatenate([jnp.sum(grouped[0], axis=0)[0:4], jnp.sum(grouped[1], axis=0)[0:4]], axis=0)
    chord = grouped[0, :, 4, :]
    radius = grouped[1, :, 4, :]
    table[0] = recv[:, 7, :]
    table[1] = recv[:, 5, :]
    table[2] = recv[:, 6, :]
    state[0] = wake
    state[1] = chord
    state[2] = radius
    circ = chord * (radius - wake)
    acc = infl[:, 0:128] * circ[0:1, :]
    for c in range(1, 8):
        acc = acc + infl[:, c * 128 : (c + 1) * 128] * circ[c : c + 1, :]
    row = lane_row(jnp.sum(acc, axis=1, keepdims=True), 8 * hy)
    out[...] = jnp.broadcast_to(row[None], out.shape)


def trim2_kernel(res, recv, state, infl, out, force):
    hx, hy = here()
    induced = jnp.sum(recv[:, 0, :].reshape(HX, HY, 128), axis=1)
    wake, chord, radius = state[0], state[1], state[2]
    circ = chord * (radius - wake)
    omega = 1.0 + 0.5 * (res[0] - total(circ * radius) * (1.0 / NSEC))
    circ = chord * (omega * radius - wake - induced)
    omega = omega + 0.5 * (res[0] - total(circ * radius) * (1.0 / NSEC))
    acc = infl[:, 0:128] * circ[0:1, :]
    for c in range(1, 8):
        acc = acc + infl[:, c * 128 : (c + 1) * 128] * circ[c : c + 1, :]
    induced2 = lane_row(jnp.sum(acc, axis=1, keepdims=True), 8 * hy)
    mine = (iota((8, 128), 0) == hx) & ((iota((8, 128), 1) >> 3) == hy)
    full = chord * (omega * radius - wake - induced2) * omega * radius
    row = jnp.sum(jnp.where(mine, full, 0.0), axis=0, keepdims=True)
    force[...] = pltpu.roll(row, lax.rem(128 - 8 * hy, 128), 1)[:, 0:8]
    out[...] = jnp.broadcast_to(row[None], out.shape)


MID = slice(8, 8 + CY)


def run(pairs, sems):
    copies = [pltpu.make_async_copy(src, dst, sems.at[i]) for i, (src, dst) in enumerate(pairs)]
    for c in copies:
        c.start()
    return copies


def finish_all(copies):
    for c in copies:
        c.wait()


def codes_of(agg, hx, hy, y0):
    rows = agg.shape[1]
    plane = iota(agg.shape, 0) + CX * hx
    group = lax.div(iota((1, rows, 128), 1) + y0, 3) + 16 * hy
    return (agg - plane * 256 - group + 4).astype(F32)


def widen(low, middle, high):
    return jnp.concatenate([low, middle, high], axis=0)


HALO = 17


def packx_kernel(vel, src, pres, mdiag, pdiag, bc, bs, bw, tail, head, ints, sems):
    ends = ((1, tail), (0, head))
    pairs = []
    for last, out in ends:
        end = lambda w: pl.ds(last * (CX - w), w)
        pairs += [(mdiag.at[end(4)], out.at[11:15]), (pdiag.at[end(2)], out.at[15:17])]
    pairs += [(bc, ints.at[0]), (bs, ints.at[1])]
    first = len(pairs)
    for last, out in ends:
        end = lambda w: pl.ds(last * (CX - w), w)
        pairs.append((bw, out.at[HALO, 8:12]))
        pairs.append((pres.at[end(2)], out.at[9:11]))
        for c in range(3):
            pairs.append((vel.at[c, end(2)], out.at[2 * c : 2 * c + 2]))
            pairs.append((src.at[c, end(1)], out.at[6 + c : 7 + c]))
    copies = run(pairs, sems)
    finish_all(copies[:first])
    for out in (tail, head):
        out[11:17] = 1.0 / (6.0 + out[11:17])
        out[HALO, 0:4] = ints[0].astype(F32)
        out[HALO, 4:8] = ints[1].astype(F32)
        out[HALO, 12:16] = jnp.zeros((4, 128), F32)
        out[HALO, 16:48] = jnp.zeros((32, 128), F32)
    finish_all(copies[first:])


def packy_kernel(
    vel, src, pres, mdiag, pdiag, agg, lists, xlo, xhi, token,
    near_a, far_a, near_b, far_b,
    edge, aedge, sems,
):
    hx, hy = here()
    odd = hy & 1
    ends = []
    for at, a, out in ((1 - odd, near_a, near_b), (odd, far_a, far_b)):
        row = pl.multiple_of((CY - 8) * at, 8)
        ends.append((pl.ds(row, 8), row, a, out))
    pairs = []
    for n, (rows, _, a, out) in enumerate(ends):
        pairs += [(mdiag.at[:, rows], edge.at[n, 0]), (pdiag.at[:, rows], edge.at[n, 1]), (agg.at[:, rows], aedge.at[n])]
    for rows, _, a, out in ends:
        for c in range(3):
            pairs.append((vel.at[c, :, rows], a.at[CX * c : CX * c + CX]))
            pairs.append((src.at[c, :, rows], a.at[48 + CX * c : 64 + CX * c]))
        pairs.append((pres.at[:, rows], out.at[0:CX]))
        for k, side in ((0, xlo), (1, xhi)):
            pairs.append((side.at[0:HALO, rows], out.at[pl.ds(64 + HALO * k, HALO)]))
            for j in range(2):
                pairs.append((side.at[HALO, slice(8 * j, 8 * j + 8)], out.at[100 + 2 * k + j]))
        for j in range(2):
            pairs.append((lists.at[HALO, slice(8 * j, 8 * j + 8)], out.at[98 + j]))
    copies = run(pairs, sems)
    finish_all(copies[:6])
    for n, (_, row, a, out) in enumerate(ends):
        out[16:32] = 1.0 / (6.0 + edge[n, 0])
        out[32:48] = 1.0 / (6.0 + edge[n, 1])
        out[48:64] = codes_of(aedge[n], hx, hy, row)
    finish_all(copies[6:])


def sweeps_kernel(
    vel_in, src_in, pres_in, mdiag_in, pdiag_in, agg_in, near_a, far_a, near_b, far_b, xlo, xhi, token,
    free_out, invd_out, invp_out, codes_out, near, far,
    v, s, q, invd, invp, codes, ya, yb, xb, vel, src, pres, mdiag, pdiag, agg, free, sems,
):
    hx, hy = here()
    odd = hy & 1
    finish_all(
        run(
            [(near_a, ya.at[1 - odd]), (far_a, ya.at[odd]), (near_b, yb.at[1 - odd]), (far_b, yb.at[odd])]
            + [(xlo.at[0:HALO], xb.at[0]), (xhi.at[0:HALO], xb.at[1])]
            + [(vel_in, vel), (src_in, src), (pres_in, pres), (mdiag_in, mdiag), (pdiag_in, pdiag), (agg_in, agg)],
            sems,
        )
    )
    yalo, yahi, ylo, yhi = ya.at[0], ya.at[1], yb.at[0], yb.at[1]
    for n in range(2):
        grown = lambda k: widen(ylo[64 + HALO * n + k], xb[n, k], yhi[64 + HALO * n + k])
        for k in range(2):
            for c in range(3):
                v[c, 18 * n + k] = grown(2 * c + k)
            v[3, 18 * n + k] = grown(9 + k)
            invp[18 * n + k] = grown(15 + k)
        for c in range(3):
            s[c, 17 * n] = grown(6 + c)
        for k in range(4):
            invd[20 * n + k] = grown(11 + k)

    def grow(x, carry):
        for c in range(3):
            v[c, x + 2] = widen(yalo[CX * c + x], vel[c, x], yahi[CX * c + x])
            s[c, x + 1] = widen(yalo[48 + CX * c + x], src[c, x], yahi[48 + CX * c + x])
        v[3, x + 2] = widen(ylo[x], pres[x], yhi[x])
        invd[x + 4] = widen(ylo[16 + x], 1.0 / (6.0 + mdiag[x]), yhi[16 + x])
        invp[x + 2] = widen(ylo[32 + x], 1.0 / (6.0 + pdiag[x]), yhi[32 + x])
        base = (CX * hx + x) * 256 + 16 * hy + lax.div(iota((CY, 128), 0), 3)
        codes[x] = widen(ylo[48 + x], (agg[x] - base + 4).astype(F32), yhi[48 + x])
        return carry

    lax.fori_loop(0, CX, grow, 0, unroll=4)

    copies = run([(invd, invd_out), (invp, invp_out), (codes, codes_out)], sems)

    def first(i, carry):
        inv = invd[i + 3]
        p = v[3, i + 1]
        ya, yb = y_parts(p)
        za, zb = zdiff_parts(p)
        for c, grad in enumerate((v[3, i + 2] - v[3, i], yb - ya, zb - za)):
            sc = s[c, i] - 0.5 * grad
            s[c, i] = sc
            q[c, i] = (sc + v[c, i] + v[c, i + 2] + s_yz(v[c, i + 1])) * inv
        return carry

    lax.fori_loop(0, CX + 2, first, 0, unroll=3)

    def second(x, carry):
        inv = invd[x + 4]
        for c in range(3):
            free[c, x] = (s[c, x + 1] + q[c, x] + q[c, x + 2] + s_yz(q[c, x + 1])) * inv
        return carry

    for k in range(4):
        lax.fori_loop(4 * k, 4 * k + 4, second, 0, unroll=4)
        part = slice(4 * k, 4 * k + 4)
        copy = pltpu.make_async_copy(free.at[:, part], free_out.at[:, part], sems.at[3 + k])
        copy.start()
        copies.append(copy)
    to = 0
    for c, w in enumerate((3, 2, 2)):
        near[to : to + w] = free[c, pl.ds((1 - (hx & 1)) * (CX - w), w)]
        far[to : to + w] = free[c, pl.ds((hx & 1) * (CX - w), w)]
        to += w
    finish_all(copies)


def body_parts():
    return [(sx, sy) for sy in (0, -1, 1) for sx in (0, -1, 1)]


def three(n, w, fn):
    for i in range(w):
        fn(i, 0, i)

    def own(j, carry):
        fn(j + w, 1, j)
        return carry

    lax.fori_loop(0, CX, own, 0, unroll=8)
    for i in range(n - CX - w):
        fn(CX + w + i, 2, i)


def body_kernel(
    recv, lists, ynear, yfar, xlo, xhi, unear, ufar, free_in, invd_in, invp_in, codes_in, table_in, gfold,
    pr0_out, target_out, corr1_out, near, far, send,
    pr0, target, corr1, b, listed, dp, corr0, acc, x3, free, invd, invp, codes, table, early_sems, sems,
):
    hx, hy = here()
    early = [(lists.at[HALO, 0:16], listed.at[0:16])]
    early += [(xlo.at[HALO, 0:16], listed.at[16:32]), (xhi.at[HALO, 0:16], listed.at[32:48])]
    for n, buf in ((1 - (hy & 1), ynear), (hy & 1, yfar)):
        for j in range(6):
            at = pl.multiple_of(48 + 48 * n + 8 * j, 8)
            early.append((buf.at[98 + j], listed.at[pl.ds(at, 8)]))
    early = run(early, early_sems)
    copies = run(
        [(invd_in, invd), (unear, x3.at[1 - (hx & 1)]), (ufar, x3.at[hx & 1]), (free_in, free), (invp_in, invp), (codes_in, codes), (table_in, table)],
        sems,
    )
    finish_all(early)
    force = jnp.sum(recv[:, 0, :].reshape(HX, HY, 128), axis=1)

    def entries(j):
        rows = [listed[16 * k + 4 * j + i : 16 * k + 4 * j + i + 1, :] for k in range(9) for i in range(4)]
        return jnp.concatenate(rows, axis=1)

    ecell, esec, ewt = entries(0), entries(1), entries(2)
    sec = esec.astype(I32)
    low = (iota((128, EN), 0) == (sec & 127)).astype(BF16)
    got = mm(jnp.concatenate(split3(force), axis=0), low)
    got = got[0:8] + got[8:16] + got[16:24]
    val = jnp.sum(jnp.where(iota((8, EN), 0) == (sec >> 7), got, 0.0), axis=0, keepdims=True) * ewt
    cell = ecell.astype(I32)
    cz = cell & 127
    place = cell >> 7
    cx = (place * 43691) >> 21
    cy = place - 48 * cx
    vh = val.astype(BF16).astype(F32)
    at_z = iota((128, EN), 0) == cz
    zh = jnp.where(at_z, vh, 0.0).astype(BF16)
    zl = jnp.where(at_z, val - vh, 0.0).astype(BF16)
    for k, (sx, sy) in enumerate(body_parts()):
        lanes = slice(k * 512, (k + 1) * 512)
        x, y = cx[:, lanes], cy[:, lanes]
        planes = CX if sx == 0 else 4
        first = {0: 4, -1: 0, 1: 20}[sx]
        x = x - 12 if sx < 0 else x
        inside = (x >= 0) & (x < planes)
        if sy == 0:
            r = jnp.where(inside, x * YE + y + 8, -1)
            rows = planes * YE
        else:
            y = y - 40 if sy < 0 else y
            inside = inside & (y >= 0) & (y < 8)
            r = jnp.where(inside, x * 8 + y, -1)
            rows = planes * 8
        spot = (iota((rows, 512), 0) == r).astype(BF16)
        part = nt(spot, zh[:, lanes]) + nt(spot, zl[:, lanes])
        if sy == 0:
            b[first : first + planes] = part.reshape(planes, YE, 128)
        else:
            at = 0 if sy < 0 else 56
            b[first : first + planes, at : at + 8] = b[first : first + planes, at : at + 8] + part.reshape(planes, 8, 128)

    finish_all(copies[:4])
    u = lambda c, at, part, j: x3[part // 2, at + j] if part != 1 else free[c, j]

    def s1(p, part, j):
        dp[p] = b[p] * invd[p]

    def s2(i, part, j):
        p = i + 1
        pr0[i] = u(0, 0, part, j) + (b[p] + dp[p - 1] + dp[p + 1] + s_yz(dp[p])) * invd[p]

    def s3(t, part, j):
        ya, yb = y_parts(u(1, 3, part, j))
        za, zb = zdiff_parts(u(2, 5, part, j))
        tg = -0.5 * ((pr0[t + 2] - pr0[t]) + (yb - ya) + (zb - za))
        target[t] = tg
        corr0[t] = 0.8 * tg * invp[t]

    def s4(c, part, j):
        t = c + 1
        v = corr0[t]
        corr1[c] = 0.2 * v + 0.8 * (target[t] + corr0[t - 1] + corr0[t + 1] + s_yz(v)) * invp[t]

    three(24, 4, s1)
    three(22, 3, s2)
    results = run([(pr0, pr0_out)], early_sems)
    finish_all(copies[4:])
    three(20, 2, s3)
    three(18, 1, s4)
    results += run([(target, target_out), (corr1, corr1_out)], sems)

    def s5(g, carry):
        halves, picks = [], []
        for k in range(4):
            x = 4 * g + k
            v = corr1[x + 1]
            full = target[x + 2] + corr1[x] + corr1[x + 2] + s_yz(v)
            res = full[8:56] - v[8:56] / invp[x + 2, MID, :]
            code = codes[x, MID, :]
            high = res.astype(BF16).astype(F32)
            for half in (high, res - high):
                picked = [jnp.where(code == float(n + 1), half, 0.0) for n in range(7)]
                halves.append(jnp.concatenate(picked, axis=0).astype(BF16))
            picks += [(iota((256, 128), 1) == x).astype(BF16)]
        part = mm(jnp.concatenate(halves, axis=1), jnp.concatenate(picks, axis=0))
        acc[...] = jnp.where(g == 0, part, acc[...] + part)
        return carry

    acc[...] = jnp.zeros(acc.shape, F32)
    lax.fori_loop(0, CX // 4, s5, 0)
    for last, out in ((1 - (hx & 1), near), (hx & 1, far)):
        out[0:3] = corr1[pl.ds(1 + last * (CX - 3), 3)]
        out[3:6] = codes[pl.ds(last * (CX - 3), 3)]
    window = mm(gfold[...], acc[...], HIGH) * float(384.0**-0.5)
    blank = jnp.zeros((32, 128), F32)
    spread = jnp.concatenate(
        [jnp.concatenate([window if j == q else blank for j in range(4)], axis=1) for q in range(4)], axis=0
    )
    m = iota((128, 1), 0)
    plane = 8 * (m & 15) + (m >> 4)
    c0 = table[0, :, 0:1].astype(I32)
    c1 = table[0, :, 1:2].astype(I32)
    lane = iota((128, 128), 1)
    wants = []
    for blk in (2 * plane, 2 * plane + 1, c0, c1):
        half = blk & 1
        pln = blk >> 1
        pln = pln - jnp.where((half == 0) & (hy == HY - 1), 1, 0) + jnp.where((half == 1) & (hy == 0), 1, 0)
        at = pln - CX * hx
        at = jnp.where((at >= 0) & (at < CX), at, -1)
        wants.append((lane == at).astype(F32))
    send[...] = jnp.broadcast_to(nt(jnp.concatenate(wants, axis=1), spread, HIGH)[:, None, :], send.shape)
    finish_all(results)


def coarse_kernel(cols, recv_in, blocks, table_in, out, ab, diag, recv, table, sem):
    hx, hy = here()
    copies = run([(recv_in, recv), (table_in, table), (blocks.at[pl.ds(2 * hx, 2)], ab)], sem)
    c0, c1 = cols[1, 2 * hx], cols[1, 2 * hx + 1]
    half = (0, 1, c0 & 1, c1 & 1)
    m = hx * HY + hy
    diag[...] = jnp.ones((8, 128), F32)
    finish_all(copies[:2])
    diag[0:1, :] = table[1, pl.ds(m, 1), :]
    diag[1:2, :] = table[2, pl.ds(m, 1), :]
    for i, c in enumerate((c0, c1)):
        pln = c >> 1
        diag[2 + i : 3 + i, :] = table[1 + (c & 1), pl.ds((pln & 7) * HY + (pln >> 3), 1), :]
    z = jnp.sum(recv[:, 0, :].reshape(HX, HY, 128), axis=0)
    r, c = iota((128, 1024), 0), iota((128, 1024), 1)
    later = (c >> 7) & 1
    m16 = (c + 4) & 15
    place = ((r >> 5) == (c >> 8)) & ((r & 31) == m16 + 16 * later) & ((later == 0) | (m16 < 8))
    y3 = mm(jnp.concatenate(split3(z), axis=0), place.astype(BF16))
    y = y3[0:16] + y3[16:32] + y3[32:48]
    lane = iota((HY, 128), 1)
    hys = iota((HY, 128), 0)
    rows = []
    for q in range(4):
        slot = (lane + 4 + 128 * half[q] - 16 * hys) & 255
        a = jnp.where(slot < 16, y[:, (2 * q) * 128 : (2 * q + 1) * 128], 0.0)
        b = jnp.where((slot >= 16) & (slot < 24), y[:, (2 * q + 1) * 128 : (2 * q + 2) * 128], 0.0)
        rows.append(jnp.sum(a + b, axis=0, keepdims=True))
    res = jnp.concatenate(rows + [jnp.zeros((4, 128), F32)], axis=0)
    first = 0.8 * res / diag[...]
    seconds = []
    copies[2].wait()
    parts = jnp.concatenate(split3(first), axis=0)

    def product(block, row):
        hi, lo = split2(block)
        both = nt(parts, hi) + nt(parts, lo)
        return both[row : row + 1] + both[8 + row : 9 + row] + both[16 + row : 17 + row]

    for i in range(2):
        applied = product(ab[i, 0], i) + product(ab[i, 1], 2 + i)
        seconds.append(first[i : i + 1] + 0.8 * (res[i : i + 1] - applied) / diag[i : i + 1, :])
    second = jnp.concatenate(seconds, axis=1)
    lane2 = iota((HY, 256), 1)
    slot = (lane2 + 4 - 16 * iota((HY, 256), 0)) & 255
    wide = jnp.broadcast_to(second, (HY, 256))
    d0 = jnp.where(slot < 16, wide, 0.0)
    d1 = jnp.where((slot >= 16) & (slot < 24), wide, 0.0)
    r, c = iota((512, 128), 0), iota((512, 128), 1)
    later = r >> 8
    m16 = (r + 4) & 15
    fold = (c == m16 + 16 * later) & ((later == 0) | (m16 < 8))
    w3 = mm(jnp.concatenate(split3(jnp.concatenate([d0, d1], axis=1)), axis=0), fold.astype(BF16))
    windows = w3[0:16] + w3[16:32] + w3[32:48]
    for i in range(HX):
        out[i * HY : (i + 1) * HY, :] = windows


def last_kernel(
    recv, corr1_in, codes_in, xnear, xfar, target_in, invp_in, pr0_in, free_in, pres_in, glift,
    vel_hbm, pres_hbm,
    vel_out, pres_out, win, c2, s1, s2, corr1, codes, target, invp, pr0, free, pres, xb, sems,
):
    hx, hy = here()
    mid = slice(1, CX + 1)
    copies = run(
        [(corr1_in.at[mid], corr1.at[mid]), (codes_in, codes), (xnear, xb.at[1 - (hx & 1)]), (xfar, xb.at[hx & 1])]
        + [(target_in, target), (invp_in, invp)]
        + [(pr0_in.at[3 : 3 + CX, MID], pr0), (free_in.at[1:3, :, MID], free), (pres_in, pres)],
        sems,
    )
    hx, hy = here()
    for i in range(24):
        p = jnp.clip(CX * hx - 4 + i, 0, 127)
        m = (p & 7) * HY + (p >> 3)
        win[i : i + 1, :] = recv[pl.ds(m, 1), :]
    w = win[0:24, :]
    lane = iota((24, 128), 1)
    w = jnp.where((lane < 4) & (hy == 0), pltpu.roll(w, 1, 0), w)
    w = jnp.where((lane >= 20) & (lane < 24) & (hy == HY - 1), pltpu.roll(w, 23, 0), w)
    win[0:24, :] = w
    win[24:128, :] = jnp.zeros((104, 128), F32)
    wt = win[...].T
    win[...] = wt

    def lift(i, part, j):
        column = jnp.sum(jnp.where(iota((32, 128), 1) == i + 1, win[0:32, :], 0.0), axis=1, keepdims=True)
        wide = jnp.broadcast_to(column, (32, 128))
        v = mm(glift[...], jnp.concatenate(split2(wide), axis=0))
        side = xb.at[part // 2]
        code = codes[j] if part == 1 else side[3 + j]
        lifted = corr1[j + 1] if part == 1 else side[j]
        for n in range(7):
            lifted = jnp.where(code == float(n + 1), lifted + v[n * YE : (n + 1) * YE], lifted)
        c2[i] = lifted

    finish_all(copies[:4])
    three(22, 3, lift)
    finish_all(copies[4:6])

    def sweep1(t, part, j):
        v = c2[t + 1]
        s1[t] = 0.2 * v + 0.8 * (target[t] + c2[t] + c2[t + 2] + s_yz(v)) * invp[t]

    def sweep2(c, part, j):
        v = s1[c + 1]
        s2[c] = 0.2 * v + 0.8 * (target[c + 1] + s1[c] + s1[c + 2] + s_yz(v)) * invp[c + 1]

    three(20, 2, sweep1)
    three(18, 1, sweep2)

    finish_all(copies[6:])

    def finish(x, carry):
        v = s2[x + 1]
        ya, yb = y_parts(v)
        za, zb = zdiff_parts(v)
        vel_out[0, x] = pr0[x] - 0.5 * (s2[x + 2] - s2[x])[8:56]
        vel_out[1, x] = free[0, x] - 0.5 * (yb - ya)[8:56]
        vel_out[2, x] = free[1, x] - 0.5 * (zb - za)[8:56]
        pres_out[x] = pres[x] + 0.7 * v[8:56]
        return carry

    results = []
    for k in range(4):
        lax.fori_loop(4 * k, 4 * k + 4, finish, 0, unroll=4)
        part = slice(4 * k, 4 * k + 4)
        for n, (src, dst) in enumerate(((vel_out.at[:, part], vel_hbm.at[:, part]), (pres_out.at[part], pres_hbm.at[part]))):
            copy = pltpu.make_async_copy(src, dst, sems.at[2 * k + n])
            copy.start()
            results.append(copy)
    finish_all(results)


def tables():
    y = np.arange(CY)
    gfold = np.zeros((32, 7 * CY), np.float32)
    for d in range(7):
        gfold[y // 3 + d + 1, d * CY + y] = 1.0
    glift = np.zeros((7 * YE, 64), np.float32)
    for d in range(7):
        for yy in range(YE):
            slot = (yy - 8) // 3 + d + 1
            if 0 <= slot < 32:
                for part in range(2):
                    glift[d * YE + yy, part * 32 + slot] = 1.0
    return gfold, glift


def to_all(x):
    return lax.all_to_all(x, BOTH, 0, 0, tiled=True)


def pair(x, axis="hully"):
    return lax.ppermute(x, axis, [(i, i ^ 1) for i in range(HX if axis == "hullx" else HY)])


def across(x, axis="hully"):
    n = HX if axis == "hullx" else HY
    return lax.ppermute(x, axis, [(i, j) for k in range(1, n - 1, 2) for i, j in ((k, k + 1), (k + 1, k))])


def shift(x, by):
    return lax.ppermute(x, "hullx", [(i, i + by) for i in range(HX) if 0 <= i + by < HX])


def shp(*dims, dtype=F32):
    return jax.ShapeDtypeStruct(dims, dtype)


def local(
    velocity, pressure, mom_source, mom_diag, press_diag, agglomeration, coarse_blocks, coarse_columns,
    wake_cells, wake_sections, wake_weights, chord, radius, influence, resistance,
    body_cells, body_sections, body_weights,
):
    gfold, glift = (jnp.asarray(t) for t in tables())
    cols = coarse_columns.T
    block = lambda *n: pltpu.VMEM((*n, YE, CZ), F32)
    sems = lambda n: pltpu.SemaphoreType.DMA((n,))

    def call(kernel, name, outs, ins, scratch, args, out_specs=None):
        if out_specs is None:
            out_specs = (VM,) * len(outs) if isinstance(outs, tuple) else VM
        return pl.pallas_call(
            kernel, out_shape=outs, in_specs=ins, out_specs=out_specs,
            scratch_shapes=scratch, compiler_params=PARAMS, name=name,
        )(*args)

    xt, xh = call(
        packx_kernel, "packx", (shp(HALO + 1, CY, CZ),) * 2, [AN] * 8, [pltpu.VMEM((2, 4, 128), I32), sems(22)],
        (velocity, mom_source, pressure, mom_diag, press_diag)
        + tuple(a.reshape(4, 128) for a in (body_cells, body_sections, body_weights)),
    )
    x1lo, x1hi = shift(xt, 1), shift(xh, -1)

    keep, give = call(
        wake_kernel, "wake", (shp(8, 128),) * 2, [SM, SM, SM] + [AN] * 5,
        [pltpu.VMEM((8, 128), F32), pltpu.VMEM((2, 128, 128), F32), pltpu.VMEM((CX, CY, CZ), F32)]
        + [pltpu.VMEM((1, 256), I32)] * 2 + [pltpu.VMEM((1, 256), F32), sems(6)],
        (cols, chord, radius, velocity, wake_cells[None], wake_sections[None], wake_weights[None]) + (coarse_blocks,),
    )
    payload = call(join_kernel, "join", shp(128, 8, 128), [VM, VM], [], (keep, pair(give)))
    recv1 = to_all(payload)
    out1, state, table = call(
        trim1_kernel, "trim1", (shp(128, ROWS[0], 128), shp(3, 8, 128), shp(3, 128, 128)), [VM, VM],
        [pltpu.VMEM((2, 8, 8, 128), F32)], (recv1,) + (influence,),
    )
    recv2 = to_all(out1)

    ya_near, ya_far, yb_near, yb_far = call(
        packy_kernel, "packy", (shp(96, 8, CZ),) * 2 + (shp(104, 8, CZ),) * 2, [AN] * 10,
        [pltpu.VMEM((2, 2, CX, 8, CZ), F32), pltpu.VMEM((2, CX, 8, CZ), I32), sems(36)],
        (velocity, mom_source, pressure, mom_diag, press_diag, agglomeration, xt, x1lo, x1hi, payload),
    )
    ya_near, yb_near = pair(ya_near), pair(yb_near)
    ya_far, yb_far = across(ya_far), across(yb_far)
    free, invd, invp, codes, fxt, fxh = call(
        sweeps_kernel, "sweeps",
        (shp(3, CX, YE, CZ), shp(24, YE, CZ), shp(20, YE, CZ), shp(CX, YE, CZ)) + (shp(7, YE, CZ),) * 2,
        [AN] * 13,
        [block(4, CX + 4), block(3, CX + 2), block(3, CX + 2), block(24), block(20), block(CX)]
        + [pltpu.VMEM((2, 96, 8, CZ), F32), pltpu.VMEM((2, 104, 8, CZ), F32), pltpu.VMEM((2, HALO, CY, CZ), F32)]
        + [pltpu.VMEM((3, CX, CY, CZ), F32)] * 2 + [pltpu.VMEM((CX, CY, CZ), F32)] * 3
        + [pltpu.VMEM((CX, CY, CZ), I32), block(3, CX), sems(12)],
        (velocity, mom_source, pressure, mom_diag, press_diag, agglomeration, ya_near, ya_far, yb_near, yb_far, x1lo, x1hi, state),
        (AN, AN, AN, AN, VM, VM),
    )
    x3near, x3far = pair(fxt, "hullx"), across(fxh, "hullx")

    out2, force = call(
        trim2_kernel, "trim2", (shp(128, ROWS[1], 128), shp(1, 8)), [SM, VM, VM, VM], [],
        (resistance, recv2, state, influence),
    )
    recv3 = to_all(out2)

    pr0, target, corr1, ct, ch, out4 = call(
        body_kernel, "body",
        (shp(22, YE, CZ), shp(20, YE, CZ), shp(18, YE, CZ), shp(6, YE, CZ), shp(6, YE, CZ), shp(128, ROWS[2], 128)),
        [VM] + [AN] * 12 + [VM],
        [block(22), block(20), block(18), block(24), pltpu.VMEM((144, 128), F32), block(24), block(20), pltpu.VMEM((7 * CY, 128), F32)]
        + [block(2, 7), block(3, CX), block(24), block(20), block(CX), pltpu.VMEM((3, 128, 128), F32), sems(15), sems(7)],
        (recv3, xt, yb_near, yb_far, x1lo, x1hi, x3near, x3far, free, invd, invp, codes, table, gfold),
        (AN, AN, AN, VM, VM, VM),
    )
    recv4 = to_all(out4)
    cxnear, cxfar = pair(ct, "hullx"), across(ch, "hullx")
    out5 = call(
        coarse_kernel, "coarse", shp(128, 128), [SM, AN, AN, AN],
        [pltpu.VMEM((2, 2, 128, 128), F32), pltpu.VMEM((8, 128), F32), pltpu.VMEM((128, 4, 128), F32)]
        + [pltpu.VMEM((3, 128, 128), F32), sems(3)],
        (cols, recv4, coarse_blocks, table),
    )
    recv5 = to_all(out5[:, None, :])[:, 0, :]
    vel_new, pres_new = call(
        last_kernel, "last", (shp(3, CX, CY, CZ), shp(CX, CY, CZ)),
        [VM] + [AN] * 9 + [VM],
        [pltpu.VMEM((3, CX, CY, CZ), F32), pltpu.VMEM((CX, CY, CZ), F32)]
        + [pltpu.VMEM((128, 128), F32), block(22), block(20), block(18), block(CX + 2), block(CX), block(20), block(20)]
        + [pltpu.VMEM((CX, CY, CZ), F32), pltpu.VMEM((2, CX, CY, CZ), F32), pltpu.VMEM((CX, CY, CZ), F32), block(2, 6), sems(9)],
        (recv5, corr1, codes, cxnear, cxfar, target, invp, pr0, free, pressure, glift.astype(BF16)),
        (AN, AN),
    )
    section_force = force.reshape(8)
    return vel_new, pres_new, section_force


def solution(mesh):
    fine = P("hullx", "hully", None)
    vector = P(None, "hullx", "hully", None)
    flat = P(BOTH)
    in_specs = (
        vector, fine, vector, fine, fine, fine,
        P("hully", None, None, None), P("hully", None),
        flat, flat, flat, flat, flat, P(BOTH, None), P(), flat, flat, flat,
    )
    return jax.shard_map(local, mesh=mesh, in_specs=in_specs, out_specs=(vector, fine, flat), check_vma=False)
```

```python
import numpy as np
import jax
import jax.numpy as jnp
from jax import lax
from jax.experimental import pallas as pl
from jax.experimental.pallas import tpu as pltpu
from jax.sharding import PartitionSpec as P

HX, HY = 8, 16
CX, CY, CZ = 16, 48, 128
NSEC = 1024
BOTH = ("hullx", "hully")
ROWS = (4, 1, 4)
F32, BF16, I32 = jnp.float32, jnp.bfloat16, jnp.int32
HIGH = lax.Precision.HIGHEST
YE = 64
EN = 9 * 512

VM = pl.BlockSpec(memory_space=pltpu.VMEM)
SM = pl.BlockSpec(memory_space=pltpu.SMEM)
AN = pl.BlockSpec(memory_space=pl.ANY)
PARAMS = pltpu.CompilerParams(vmem_limit_bytes=67000000)


def here():
    return lax.axis_index("hullx"), lax.axis_index("hully")


def iota(shape, dim):
    return lax.broadcasted_iota(I32, shape, dim)


def split2(x):
    hi = x.astype(BF16)
    lo = (x - hi.astype(F32)).astype(BF16)
    return hi, lo


def split3(x):
    hi = x.astype(BF16)
    rest = x - hi.astype(F32)
    mid = rest.astype(BF16)
    lo = (rest - mid.astype(F32)).astype(BF16)
    return hi, mid, lo


def nt(a, b, precision=None):
    return lax.dot_general(a, b, (((1,), (1,)), ((), ())), precision=precision, preferred_element_type=F32)


def mm(a, b, precision=None):
    return lax.dot_general(a, b, (((1,), (0,)), ((), ())), precision=precision, preferred_element_type=F32)


def lane_row(column, start):
    spot = iota((8, 128), 1) == iota((8, 128), 0) + start
    return jnp.sum(jnp.where(spot, column, 0.0), axis=0, keepdims=True)


def total(x):
    return jnp.sum(jnp.sum(x, axis=1, keepdims=True), axis=0, keepdims=True)


def zdiff_parts(v):
    lane = iota(v.shape, 1)
    before = jnp.where(lane == 0, 0.0, pltpu.roll(v, 1, 1))
    after = jnp.where(lane == CZ - 1, 0.0, pltpu.roll(v, CZ - 1, 1))
    return before, after


def y_parts(v):
    return pltpu.roll(v, 1, 0), pltpu.roll(v, v.shape[0] - 1, 0)


def s_yz(v):
    a, b = y_parts(v)
    c, d = zdiff_parts(v)
    return (a + b) + (c + d)


def wake_kernel(cols, chord, radius, vel, wc_in, ws_in, ww_in, blocks, keep, give, row, ab, v, wc, ws, ww, sem):
    hx, hy = here()
    pairs = [(wc_in, wc), (ws_in, ws), (ww_in, ww), (vel.at[0], v)]
    copies = run(pairs + [(blocks.at[2 * hx + i, 0], ab.at[i]) for i in range(2)], sem)
    finish_all(copies[:3])
    cells = wc[...]
    place = cells >> 7
    spot = (iota((768, 256), 0) == place).astype(BF16)
    picked = jnp.zeros((128, 256), F32)
    copies[3].wait()
    for part in split2(v[...].reshape(768, 128)):
        picked = picked + lax.dot_general(part, spot, (((0,), (0,)), ((), ())), preferred_element_type=F32)
    samples = jnp.sum(jnp.where(iota((128, 256), 0) == (cells & 127), picked, 0.0), axis=0, keepdims=True) * ww[...]
    sec = ws[...]
    high = jnp.where(iota((8, 256), 0) == (sec >> 7), samples, 0.0)
    low = (iota((128, 256), 0) == (sec & 127)).astype(F32)
    row[...] = nt(high, low, HIGH)
    lane = iota((1, 128), 1)
    crow = rrow = jnp.zeros((1, 128), F32)
    for k in range(8):
        crow = jnp.where(lane == 8 * hy + k, chord[k], crow)
        rrow = jnp.where(lane == 8 * hy + k, radius[k], rrow)
    c0 = cols[1, 2 * hx].astype(F32)
    c1 = cols[1, 2 * hx + 1].astype(F32)
    colrow = jnp.where(lane == 0, c0, jnp.where(lane == 1, c1, 0.0))
    eye = iota((128, 128), 0) == iota((128, 128), 1)
    even = (hy & 1) == 0
    first, second = row[0:4, :], row[4:8, :]
    finish_all(copies[4:])
    d0 = jnp.sum(jnp.where(eye, ab[0], 0.0), axis=0, keepdims=True)
    d1 = jnp.sum(jnp.where(eye, ab[1], 0.0), axis=0, keepdims=True)
    keep[...] = jnp.concatenate([jnp.where(even, first, second), jnp.where(even, crow, rrow), d0, d1, colrow], axis=0)
    give[...] = jnp.concatenate(
        [jnp.where(even, second, first), jnp.where(even, rrow, crow), jnp.zeros((3, 128), F32)], axis=0
    )


def join_kernel(keep, got, out):
    out[...] = jnp.broadcast_to((keep[...] + got[...])[None], out.shape)


def trim1_kernel(recv, infl, out, state, table, grouped):
    hx, hy = here()
    by_core = recv[...].reshape(HX, HY // 2, 2, 8, 128)
    for core in range(2):
        grouped[core] = jnp.sum(by_core[:, :, core], axis=1)
    wake = jnp.concatenate([jnp.sum(grouped[0], axis=0)[0:4], jnp.sum(grouped[1], axis=0)[0:4]], axis=0)
    chord = grouped[0, :, 4, :]
    radius = grouped[1, :, 4, :]
    table[0] = recv[:, 7, :]
    table[1] = recv[:, 5, :]
    table[2] = recv[:, 6, :]
    state[0] = wake
    state[1] = chord
    state[2] = radius
    circ = chord * (radius - wake)
    acc = infl[:, 0:128] * circ[0:1, :]
    for c in range(1, 8):
        acc = acc + infl[:, c * 128 : (c + 1) * 128] * circ[c : c + 1, :]
    row = lane_row(jnp.sum(acc, axis=1, keepdims=True), 8 * hy)
    out[...] = jnp.broadcast_to(row[None], out.shape)


def trim2_kernel(res, recv, state, infl, out, force):
    hx, hy = here()
    induced = jnp.sum(recv[:, 0, :].reshape(HX, HY, 128), axis=1)
    wake, chord, radius = state[0], state[1], state[2]
    circ = chord * (radius - wake)
    omega = 1.0 + 0.5 * (res[0] - total(circ * radius) * (1.0 / NSEC))
    circ = chord * (omega * radius - wake - induced)
    omega = omega + 0.5 * (res[0] - total(circ * radius) * (1.0 / NSEC))
    acc = infl[:, 0:128] * circ[0:1, :]
    for c in range(1, 8):
        acc = acc + infl[:, c * 128 : (c + 1) * 128] * circ[c : c + 1, :]
    induced2 = lane_row(jnp.sum(acc, axis=1, keepdims=True), 8 * hy)
    mine = (iota((8, 128), 0) == hx) & ((iota((8, 128), 1) >> 3) == hy)
    full = chord * (omega * radius - wake - induced2) * omega * radius
    row = jnp.sum(jnp.where(mine, full, 0.0), axis=0, keepdims=True)
    force[...] = pltpu.roll(row, lax.rem(128 - 8 * hy, 128), 1)[:, 0:8]
    out[...] = jnp.broadcast_to(row[None], out.shape)


MID = slice(8, 8 + CY)


def run(pairs, sems):
    copies = [pltpu.make_async_copy(src, dst, sems.at[i]) for i, (src, dst) in enumerate(pairs)]
    for c in copies:
        c.start()
    return copies


def finish_all(copies):
    for c in copies:
        c.wait()


def codes_of(agg, hx, hy, y0):
    rows = agg.shape[1]
    plane = iota(agg.shape, 0) + CX * hx
    group = lax.div(iota((1, rows, 128), 1) + y0, 3) + 16 * hy
    return (agg - plane * 256 - group + 4).astype(F32)


def widen(low, middle, high):
    return jnp.concatenate([low, middle, high], axis=0)


HALO = 17


def packx_kernel(vel, src, pres, mdiag, pdiag, bc, bs, bw, tail, head, ints, sems):
    ends = ((1, tail), (0, head))
    pairs = []
    for last, out in ends:
        end = lambda w: pl.ds(last * (CX - w), w)
        pairs += [(mdiag.at[end(4)], out.at[11:15]), (pdiag.at[end(2)], out.at[15:17])]
    pairs += [(bc, ints.at[0]), (bs, ints.at[1])]
    first = len(pairs)
    for last, out in ends:
        end = lambda w: pl.ds(last * (CX - w), w)
        pairs.append((bw, out.at[HALO, 8:12]))
        pairs.append((pres.at[end(2)], out.at[9:11]))
        for c in range(3):
            pairs.append((vel.at[c, end(2)], out.at[2 * c : 2 * c + 2]))
            pairs.append((src.at[c, end(1)], out.at[6 + c : 7 + c]))
    copies = run(pairs, sems)
    finish_all(copies[:first])
    for out in (tail, head):
        out[11:17] = 1.0 / (6.0 + out[11:17])
        out[HALO, 0:4] = ints[0].astype(F32)
        out[HALO, 4:8] = ints[1].astype(F32)
        out[HALO, 12:16] = jnp.zeros((4, 128), F32)
        out[HALO, 16:48] = jnp.zeros((32, 128), F32)
    finish_all(copies[first:])


def packy_kernel(
    vel, src, pres, mdiag, pdiag, agg, lists, xlo, xhi, token,
    near_a, far_a, near_b, far_b,
    edge, aedge, sems,
):
    hx, hy = here()
    odd = hy & 1
    ends = []
    for at, a, out in ((1 - odd, near_a, near_b), (odd, far_a, far_b)):
        row = pl.multiple_of((CY - 8) * at, 8)
        ends.append((pl.ds(row, 8), row, a, out))
    pairs = []
    for n, (rows, _, a, out) in enumerate(ends):
        pairs += [(mdiag.at[:, rows], edge.at[n, 0]), (pdiag.at[:, rows], edge.at[n, 1]), (agg.at[:, rows], aedge.at[n])]
    for rows, _, a, out in ends:
        for c in range(3):
            pairs.append((vel.at[c, :, rows], a.at[CX * c : CX * c + CX]))
            pairs.append((src.at[c, :, rows], a.at[48 + CX * c : 64 + CX * c]))
        pairs.append((pres.at[:, rows], out.at[0:CX]))
        for k, side in ((0, xlo), (1, xhi)):
            pairs.append((side.at[0:HALO, rows], out.at[pl.ds(64 + HALO * k, HALO)]))
            for j in range(2):
                pairs.append((side.at[HALO, slice(8 * j, 8 * j + 8)], out.at[100 + 2 * k + j]))
        for j in range(2):
            pairs.append((lists.at[HALO, slice(8 * j, 8 * j + 8)], out.at[98 + j]))
    copies = run(pairs, sems)
    finish_all(copies[:6])
    for n, (_, row, a, out) in enumerate(ends):
        out[16:32] = 1.0 / (6.0 + edge[n, 0])
        out[32:48] = 1.0 / (6.0 + edge[n, 1])
        out[48:64] = codes_of(aedge[n], hx, hy, row)
    finish_all(copies[6:])


def sweeps_kernel(
    vel_in, src_in, pres_in, mdiag_in, pdiag_in, agg_in, near_a, far_a, near_b, far_b, xlo, xhi, token,
    free_out, invd_out, invp_out, codes_out, near, far,
    v, s, q, invd, invp, codes, ya, yb, xb, vel, src, pres, mdiag, pdiag, agg, free, sems,
):
    hx, hy = here()
    odd = hy & 1
    finish_all(
        run(
            [(near_a, ya.at[1 - odd]), (far_a, ya.at[odd]), (near_b, yb.at[1 - odd]), (far_b, yb.at[odd])]
            + [(xlo.at[0:HALO], xb.at[0]), (xhi.at[0:HALO], xb.at[1])]
            + [(vel_in, vel), (src_in, src), (pres_in, pres), (mdiag_in, mdiag), (pdiag_in, pdiag), (agg_in, agg)],
            sems,
        )
    )
    yalo, yahi, ylo, yhi = ya.at[0], ya.at[1], yb.at[0], yb.at[1]
    for n in range(2):
        grown = lambda k: widen(ylo[64 + HALO * n + k], xb[n, k], yhi[64 + HALO * n + k])
        for k in range(2):
            for c in range(3):
                v[c, 18 * n + k] = grown(2 * c + k)
            v[3, 18 * n + k] = grown(9 + k)
            invp[18 * n + k] = grown(15 + k)
        for c in range(3):
            s[c, 17 * n] = grown(6 + c)
        for k in range(4):
            invd[20 * n + k] = grown(11 + k)

    def grow(x, carry):
        for c in range(3):
            v[c, x + 2] = widen(yalo[CX * c + x], vel[c, x], yahi[CX * c + x])
            s[c, x + 1] = widen(yalo[48 + CX * c + x], src[c, x], yahi[48 + CX * c + x])
        v[3, x + 2] = widen(ylo[x], pres[x], yhi[x])
        invd[x + 4] = widen(ylo[16 + x], 1.0 / (6.0 + mdiag[x]), yhi[16 + x])
        invp[x + 2] = widen(ylo[32 + x], 1.0 / (6.0 + pdiag[x]), yhi[32 + x])
        base = (CX * hx + x) * 256 + 16 * hy + lax.div(iota((CY, 128), 0), 3)
        codes[x] = widen(ylo[48 + x], (agg[x] - base + 4).astype(F32), yhi[48 + x])
        return carry

    lax.fori_loop(0, CX, grow, 0, unroll=8)

    copies = run([(invd, invd_out), (invp, invp_out), (codes, codes_out)], sems)

    def first(i, carry):
        inv = invd[i + 3]
        p = v[3, i + 1]
        ya, yb = y_parts(p)
        za, zb = zdiff_parts(p)
        for c, grad in enumerate((v[3, i + 2] - v[3, i], yb - ya, zb - za)):
            sc = s[c, i] - 0.5 * grad
            s[c, i] = sc
            q[c, i] = (sc + v[c, i] + v[c, i + 2] + s_yz(v[c, i + 1])) * inv
        return carry

    lax.fori_loop(0, CX + 2, first, 0, unroll=6)

    def second(x, carry):
        inv = invd[x + 4]
        for c in range(3):
            free[c, x] = (s[c, x + 1] + q[c, x] + q[c, x + 2] + s_yz(q[c, x + 1])) * inv
        return carry

    for k in range(4):
        lax.fori_loop(4 * k, 4 * k + 4, second, 0, unroll=4)
        part = slice(4 * k, 4 * k + 4)
        copy = pltpu.make_async_copy(free.at[:, part], free_out.at[:, part], sems.at[3 + k])
        copy.start()
        copies.append(copy)
    to = 0
    for c, w in enumerate((3, 2, 2)):
        near[to : to + w] = free[c, pl.ds((1 - (hx & 1)) * (CX - w), w)]
        far[to : to + w] = free[c, pl.ds((hx & 1) * (CX - w), w)]
        to += w
    finish_all(copies)


def body_parts():
    return [(sx, sy) for sy in (0, -1, 1) for sx in (0, -1, 1)]


def three(n, w, fn):
    for i in range(w):
        fn(i, 0, i)

    def own(j, carry):
        fn(j + w, 1, j)
        return carry

    lax.fori_loop(0, CX, own, 0, unroll=16)
    for i in range(n - CX - w):
        fn(CX + w + i, 2, i)


def body_kernel(
    recv, lists, ynear, yfar, xlo, xhi, unear, ufar, free_in, invd_in, invp_in, codes_in, table_in, gfold,
    pr0_out, target_out, corr1_out, near, far, send,
    pr0, target, corr1, b, listed, dp, corr0, acc, x3, free, invd, invp, codes, table, early_sems, sems,
):
    hx, hy = here()
    early = [(lists.at[HALO, 0:16], listed.at[0:16])]
    early += [(xlo.at[HALO, 0:16], listed.at[16:32]), (xhi.at[HALO, 0:16], listed.at[32:48])]
    for n, buf in ((1 - (hy & 1), ynear), (hy & 1, yfar)):
        for j in range(6):
            at = pl.multiple_of(48 + 48 * n + 8 * j, 8)
            early.append((buf.at[98 + j], listed.at[pl.ds(at, 8)]))
    early = run(early, early_sems)
    copies = run(
        [(invd_in, invd), (unear, x3.at[1 - (hx & 1)]), (ufar, x3.at[hx & 1]), (free_in, free), (invp_in, invp), (codes_in, codes), (table_in, table)],
        sems,
    )
    finish_all(early)
    force = jnp.sum(recv[:, 0, :].reshape(HX, HY, 128), axis=1)

    def entries(j):
        rows = [listed[16 * k + 4 * j + i : 16 * k + 4 * j + i + 1, :] for k in range(9) for i in range(4)]
        return jnp.concatenate(rows, axis=1)

    ecell, esec, ewt = entries(0), entries(1), entries(2)
    sec = esec.astype(I32)
    low = (iota((128, EN), 0) == (sec & 127)).astype(BF16)
    got = mm(jnp.concatenate(split3(force), axis=0), low)
    got = got[0:8] + got[8:16] + got[16:24]
    val = jnp.sum(jnp.where(iota((8, EN), 0) == (sec >> 7), got, 0.0), axis=0, keepdims=True) * ewt
    cell = ecell.astype(I32)
    cz = cell & 127
    place = cell >> 7
    cx = (place * 43691) >> 21
    cy = place - 48 * cx
    vh = val.astype(BF16).astype(F32)
    at_z = iota((128, EN), 0) == cz
    zh = jnp.where(at_z, vh, 0.0).astype(BF16)
    zl = jnp.where(at_z, val - vh, 0.0).astype(BF16)
    for k, (sx, sy) in enumerate(body_parts()):
        lanes = slice(k * 512, (k + 1) * 512)
        x, y = cx[:, lanes], cy[:, lanes]
        planes = CX if sx == 0 else 4
        first = {0: 4, -1: 0, 1: 20}[sx]
        x = x - 12 if sx < 0 else x
        inside = (x >= 0) & (x < planes)
        if sy == 0:
            r = jnp.where(inside, x * YE + y + 8, -1)
            rows = planes * YE
        else:
            y = y - 40 if sy < 0 else y
            inside = inside & (y >= 0) & (y < 8)
            r = jnp.where(inside, x * 8 + y, -1)
            rows = planes * 8
        spot = (iota((rows, 512), 0) == r).astype(BF16)
        part = nt(spot, zh[:, lanes]) + nt(spot, zl[:, lanes])
        if sy == 0:
            b[first : first + planes] = part.reshape(planes, YE, 128)
        else:
            at = 0 if sy < 0 else 56
            b[first : first + planes, at : at + 8] = b[first : first + planes, at : at + 8] + part.reshape(planes, 8, 128)

    finish_all(copies[:4])
    u = lambda c, at, part, j: x3[part // 2, at + j] if part != 1 else free[c, j]

    def s1(p, part, j):
        dp[p] = b[p] * invd[p]

    def s2(i, part, j):
        p = i + 1
        pr0[i] = u(0, 0, part, j) + (b[p] + dp[p - 1] + dp[p + 1] + s_yz(dp[p])) * invd[p]

    def s3(t, part, j):
        ya, yb = y_parts(u(1, 3, part, j))
        za, zb = zdiff_parts(u(2, 5, part, j))
        tg = -0.5 * ((pr0[t + 2] - pr0[t]) + (yb - ya) + (zb - za))
        target[t] = tg
        corr0[t] = 0.8 * tg * invp[t]

    def s4(c, part, j):
        t = c + 1
        v = corr0[t]
        corr1[c] = 0.2 * v + 0.8 * (target[t] + corr0[t - 1] + corr0[t + 1] + s_yz(v)) * invp[t]

    three(24, 4, s1)
    three(22, 3, s2)
    results = run([(pr0, pr0_out)], early_sems)
    finish_all(copies[4:])
    three(20, 2, s3)
    three(18, 1, s4)
    results += run([(target, target_out), (corr1, corr1_out)], sems)

    def s5(g, carry):
        halves, picks = [], []
        for k in range(4):
            x = 4 * g + k
            v = corr1[x + 1]
            full = target[x + 2] + corr1[x] + corr1[x + 2] + s_yz(v)
            res = full[8:56] - v[8:56] / invp[x + 2, MID, :]
            code = codes[x, MID, :]
            high = res.astype(BF16).astype(F32)
            for half in (high, res - high):
                picked = [jnp.where(code == float(n + 1), half, 0.0) for n in range(7)]
                halves.append(jnp.concatenate(picked, axis=0).astype(BF16))
            picks += [(iota((256, 128), 1) == x).astype(BF16)]
        part = mm(jnp.concatenate(halves, axis=1), jnp.concatenate(picks, axis=0))
        acc[...] = jnp.where(g == 0, part, acc[...] + part)
        return carry

    acc[...] = jnp.zeros(acc.shape, F32)
    lax.fori_loop(0, CX // 4, s5, 0, unroll=4)
    for last, out in ((1 - (hx & 1), near), (hx & 1, far)):
        out[0:3] = corr1[pl.ds(1 + last * (CX - 3), 3)]
        out[3:6] = codes[pl.ds(last * (CX - 3), 3)]
    window = mm(gfold[...], acc[...], HIGH) * float(384.0**-0.5)
    blank = jnp.zeros((32, 128), F32)
    spread = jnp.concatenate(
        [jnp.concatenate([window if j == q else blank for j in range(4)], axis=1) for q in range(4)], axis=0
    )
    m = iota((128, 1), 0)
    plane = 8 * (m & 15) + (m >> 4)
    c0 = table[0, :, 0:1].astype(I32)
    c1 = table[0, :, 1:2].astype(I32)
    lane = iota((128, 128), 1)
    wants = []
    for blk in (2 * plane, 2 * plane + 1, c0, c1):
        half = blk & 1
        pln = blk >> 1
        pln = pln - jnp.where((half == 0) & (hy == HY - 1), 1, 0) + jnp.where((half == 1) & (hy == 0), 1, 0)
        at = pln - CX * hx
        at = jnp.where((at >= 0) & (at < CX), at, -1)
        wants.append((lane == at).astype(F32))
    send[...] = jnp.broadcast_to(nt(jnp.concatenate(wants, axis=1), spread, HIGH)[:, None, :], send.shape)
    finish_all(results)


def coarse_kernel(cols, recv_in, blocks, table_in, out, ab, diag, recv, table, sem):
    hx, hy = here()
    copies = run([(recv_in, recv), (table_in, table), (blocks.at[pl.ds(2 * hx, 2)], ab)], sem)
    c0, c1 = cols[1, 2 * hx], cols[1, 2 * hx + 1]
    half = (0, 1, c0 & 1, c1 & 1)
    m = hx * HY + hy
    diag[...] = jnp.ones((8, 128), F32)
    finish_all(copies[:2])
    diag[0:1, :] = table[1, pl.ds(m, 1), :]
    diag[1:2, :] = table[2, pl.ds(m, 1), :]
    for i, c in enumerate((c0, c1)):
        pln = c >> 1
        diag[2 + i : 3 + i, :] = table[1 + (c & 1), pl.ds((pln & 7) * HY + (pln >> 3), 1), :]
    z = jnp.sum(recv[:, 0, :].reshape(HX, HY, 128), axis=0)
    r, c = iota((128, 1024), 0), iota((128, 1024), 1)
    later = (c >> 7) & 1
    m16 = (c + 4) & 15
    place = ((r >> 5) == (c >> 8)) & ((r & 31) == m16 + 16 * later) & ((later == 0) | (m16 < 8))
    y3 = mm(jnp.concatenate(split3(z), axis=0), place.astype(BF16))
    y = y3[0:16] + y3[16:32] + y3[32:48]
    lane = iota((HY, 128), 1)
    hys = iota((HY, 128), 0)
    rows = []
    for q in range(4):
        slot = (lane + 4 + 128 * half[q] - 16 * hys) & 255
        a = jnp.where(slot < 16, y[:, (2 * q) * 128 : (2 * q + 1) * 128], 0.0)
        b = jnp.where((slot >= 16) & (slot < 24), y[:, (2 * q + 1) * 128 : (2 * q + 2) * 128], 0.0)
        rows.append(jnp.sum(a + b, axis=0, keepdims=True))
    res = jnp.concatenate(rows + [jnp.zeros((4, 128), F32)], axis=0)
    first = 0.8 * res / diag[...]
    seconds = []
    copies[2].wait()
    parts = jnp.concatenate(split3(first), axis=0)

    def product(block, row):
        hi, lo = split2(block)
        both = nt(parts, hi) + nt(parts, lo)
        return both[row : row + 1] + both[8 + row : 9 + row] + both[16 + row : 17 + row]

    for i in range(2):
        applied = product(ab[i, 0], i) + product(ab[i, 1], 2 + i)
        seconds.append(first[i : i + 1] + 0.8 * (res[i : i + 1] - applied) / diag[i : i + 1, :])
    second = jnp.concatenate(seconds, axis=1)
    lane2 = iota((HY, 256), 1)
    slot = (lane2 + 4 - 16 * iota((HY, 256), 0)) & 255
    wide = jnp.broadcast_to(second, (HY, 256))
    d0 = jnp.where(slot < 16, wide, 0.0)
    d1 = jnp.where((slot >= 16) & (slot < 24), wide, 0.0)
    r, c = iota((512, 128), 0), iota((512, 128), 1)
    later = r >> 8
    m16 = (r + 4) & 15
    fold = (c == m16 + 16 * later) & ((later == 0) | (m16 < 8))
    w3 = mm(jnp.concatenate(split3(jnp.concatenate([d0, d1], axis=1)), axis=0), fold.astype(BF16))
    windows = w3[0:16] + w3[16:32] + w3[32:48]
    for i in range(HX):
        out[i * HY : (i + 1) * HY, :] = windows


def last_kernel(
    recv, corr1_in, codes_in, xnear, xfar, target_in, invp_in, pr0_in, free_in, pres_in, glift,
    vel_hbm, pres_hbm,
    vel_out, pres_out, win, c2, s1, s2, corr1, codes, target, invp, pr0, free, pres, xb, sems,
):
    hx, hy = here()
    mid = slice(1, CX + 1)
    copies = run(
        [(corr1_in.at[mid], corr1.at[mid]), (codes_in, codes), (xnear, xb.at[1 - (hx & 1)]), (xfar, xb.at[hx & 1])]
        + [(target_in, target), (invp_in, invp)]
        + [(pr0_in.at[3 : 3 + CX, MID], pr0), (free_in.at[1:3, :, MID], free), (pres_in, pres)],
        sems,
    )
    hx, hy = here()
    for i in range(24):
        p = jnp.clip(CX * hx - 4 + i, 0, 127)
        m = (p & 7) * HY + (p >> 3)
        win[i : i + 1, :] = recv[pl.ds(m, 1), :]
    w = win[0:24, :]
    lane = iota((24, 128), 1)
    w = jnp.where((lane < 4) & (hy == 0), pltpu.roll(w, 1, 0), w)
    w = jnp.where((lane >= 20) & (lane < 24) & (hy == HY - 1), pltpu.roll(w, 23, 0), w)
    win[0:24, :] = w
    win[24:128, :] = jnp.zeros((104, 128), F32)
    wt = win[...].T
    win[...] = wt

    def lift(i, part, j):
        column = jnp.sum(jnp.where(iota((32, 128), 1) == i + 1, win[0:32, :], 0.0), axis=1, keepdims=True)
        wide = jnp.broadcast_to(column, (32, 128))
        v = mm(glift[...], jnp.concatenate(split2(wide), axis=0))
        side = xb.at[part // 2]
        code = codes[j] if part == 1 else side[3 + j]
        lifted = corr1[j + 1] if part == 1 else side[j]
        for n in range(7):
            lifted = jnp.where(code == float(n + 1), lifted + v[n * YE : (n + 1) * YE], lifted)
        c2[i] = lifted

    finish_all(copies[:4])
    three(22, 3, lift)
    finish_all(copies[4:6])

    def sweep1(t, part, j):
        v = c2[t + 1]
        s1[t] = 0.2 * v + 0.8 * (target[t] + c2[t] + c2[t + 2] + s_yz(v)) * invp[t]

    def sweep2(c, part, j):
        v = s1[c + 1]
        s2[c] = 0.2 * v + 0.8 * (target[c + 1] + s1[c] + s1[c + 2] + s_yz(v)) * invp[c + 1]

    three(20, 2, sweep1)
    three(18, 1, sweep2)

    finish_all(copies[6:])

    def finish(x, carry):
        v = s2[x + 1]
        ya, yb = y_parts(v)
        za, zb = zdiff_parts(v)
        vel_out[0, x] = pr0[x] - 0.5 * (s2[x + 2] - s2[x])[8:56]
        vel_out[1, x] = free[0, x] - 0.5 * (yb - ya)[8:56]
        vel_out[2, x] = free[1, x] - 0.5 * (zb - za)[8:56]
        pres_out[x] = pres[x] + 0.7 * v[8:56]
        return carry

    results = []
    for k in range(4):
        lax.fori_loop(4 * k, 4 * k + 4, finish, 0, unroll=4)
        part = slice(4 * k, 4 * k + 4)
        for n, (src, dst) in enumerate(((vel_out.at[:, part], vel_hbm.at[:, part]), (pres_out.at[part], pres_hbm.at[part]))):
            copy = pltpu.make_async_copy(src, dst, sems.at[2 * k + n])
            copy.start()
            results.append(copy)
    finish_all(results)


def tables():
    y = np.arange(CY)
    gfold = np.zeros((32, 7 * CY), np.float32)
    for d in range(7):
        gfold[y // 3 + d + 1, d * CY + y] = 1.0
    glift = np.zeros((7 * YE, 64), np.float32)
    for d in range(7):
        for yy in range(YE):
            slot = (yy - 8) // 3 + d + 1
            if 0 <= slot < 32:
                for part in range(2):
                    glift[d * YE + yy, part * 32 + slot] = 1.0
    return gfold, glift


def to_all(x):
    return lax.all_to_all(x, BOTH, 0, 0, tiled=True)


def pair(x, axis="hully"):
    return lax.ppermute(x, axis, [(i, i ^ 1) for i in range(HX if axis == "hullx" else HY)])


def across(x, axis="hully"):
    n = HX if axis == "hullx" else HY
    return lax.ppermute(x, axis, [(i, j) for k in range(1, n - 1, 2) for i, j in ((k, k + 1), (k + 1, k))])


def shift(x, by):
    return lax.ppermute(x, "hullx", [(i, i + by) for i in range(HX) if 0 <= i + by < HX])


def shp(*dims, dtype=F32):
    return jax.ShapeDtypeStruct(dims, dtype)


def local(
    velocity, pressure, mom_source, mom_diag, press_diag, agglomeration, coarse_blocks, coarse_columns,
    wake_cells, wake_sections, wake_weights, chord, radius, influence, resistance,
    body_cells, body_sections, body_weights,
):
    gfold, glift = (jnp.asarray(t) for t in tables())
    cols = coarse_columns.T
    block = lambda *n: pltpu.VMEM((*n, YE, CZ), F32)
    sems = lambda n: pltpu.SemaphoreType.DMA((n,))

    def call(kernel, name, outs, ins, scratch, args, out_specs=None):
        if out_specs is None:
            out_specs = (VM,) * len(outs) if isinstance(outs, tuple) else VM
        return pl.pallas_call(
            kernel, out_shape=outs, in_specs=ins, out_specs=out_specs,
            scratch_shapes=scratch, compiler_params=PARAMS, name=name,
        )(*args)

    xt, xh = call(
        packx_kernel, "packx", (shp(HALO + 1, CY, CZ),) * 2, [AN] * 8, [pltpu.VMEM((2, 4, 128), I32), sems(22)],
        (velocity, mom_source, pressure, mom_diag, press_diag)
        + tuple(a.reshape(4, 128) for a in (body_cells, body_sections, body_weights)),
    )
    x1lo, x1hi = shift(xt, 1), shift(xh, -1)

    keep, give = call(
        wake_kernel, "wake", (shp(8, 128),) * 2, [SM, SM, SM] + [AN] * 5,
        [pltpu.VMEM((8, 128), F32), pltpu.VMEM((2, 128, 128), F32), pltpu.VMEM((CX, CY, CZ), F32)]
        + [pltpu.VMEM((1, 256), I32)] * 2 + [pltpu.VMEM((1, 256), F32), sems(6)],
        (cols, chord, radius, velocity, wake_cells[None], wake_sections[None], wake_weights[None]) + (coarse_blocks,),
    )
    payload = call(join_kernel, "join", shp(128, 8, 128), [VM, VM], [], (keep, pair(give)))
    recv1 = to_all(payload)
    out1, state, table = call(
        trim1_kernel, "trim1", (shp(128, ROWS[0], 128), shp(3, 8, 128), shp(3, 128, 128)), [VM, VM],
        [pltpu.VMEM((2, 8, 8, 128), F32)], (recv1,) + (influence,),
    )
    recv2 = to_all(out1)

    ya_near, ya_far, yb_near, yb_far = call(
        packy_kernel, "packy", (shp(96, 8, CZ),) * 2 + (shp(104, 8, CZ),) * 2, [AN] * 10,
        [pltpu.VMEM((2, 2, CX, 8, CZ), F32), pltpu.VMEM((2, CX, 8, CZ), I32), sems(36)],
        (velocity, mom_source, pressure, mom_diag, press_diag, agglomeration, xt, x1lo, x1hi, payload),
    )
    ya_near, yb_near = pair(ya_near), pair(yb_near)
    ya_far, yb_far = across(ya_far), across(yb_far)
    free, invd, invp, codes, fxt, fxh = call(
        sweeps_kernel, "sweeps",
        (shp(3, CX, YE, CZ), shp(24, YE, CZ), shp(20, YE, CZ), shp(CX, YE, CZ)) + (shp(7, YE, CZ),) * 2,
        [AN] * 13,
        [block(4, CX + 4), block(3, CX + 2), block(3, CX + 2), block(24), block(20), block(CX)]
        + [pltpu.VMEM((2, 96, 8, CZ), F32), pltpu.VMEM((2, 104, 8, CZ), F32), pltpu.VMEM((2, HALO, CY, CZ), F32)]
        + [pltpu.VMEM((3, CX, CY, CZ), F32)] * 2 + [pltpu.VMEM((CX, CY, CZ), F32)] * 3
        + [pltpu.VMEM((CX, CY, CZ), I32), block(3, CX), sems(12)],
        (velocity, mom_source, pressure, mom_diag, press_diag, agglomeration, ya_near, ya_far, yb_near, yb_far, x1lo, x1hi, state),
        (AN, AN, AN, AN, VM, VM),
    )
    x3near, x3far = pair(fxt, "hullx"), across(fxh, "hullx")

    out2, force = call(
        trim2_kernel, "trim2", (shp(128, ROWS[1], 128), shp(1, 8)), [SM, VM, VM, VM], [],
        (resistance, recv2, state, influence),
    )
    recv3 = to_all(out2)

    pr0, target, corr1, ct, ch, out4 = call(
        body_kernel, "body",
        (shp(22, YE, CZ), shp(20, YE, CZ), shp(18, YE, CZ), shp(6, YE, CZ), shp(6, YE, CZ), shp(128, ROWS[2], 128)),
        [VM] + [AN] * 12 + [VM],
        [block(22), block(20), block(18), block(24), pltpu.VMEM((144, 128), F32), block(24), block(20), pltpu.VMEM((7 * CY, 128), F32)]
        + [block(2, 7), block(3, CX), block(24), block(20), block(CX), pltpu.VMEM((3, 128, 128), F32), sems(15), sems(7)],
        (recv3, xt, yb_near, yb_far, x1lo, x1hi, x3near, x3far, free, invd, invp, codes, table, gfold),
        (AN, AN, AN, VM, VM, VM),
    )
    recv4 = to_all(out4)
    cxnear, cxfar = pair(ct, "hullx"), across(ch, "hullx")
    out5 = call(
        coarse_kernel, "coarse", shp(128, 128), [SM, AN, AN, AN],
        [pltpu.VMEM((2, 2, 128, 128), F32), pltpu.VMEM((8, 128), F32), pltpu.VMEM((128, 4, 128), F32)]
        + [pltpu.VMEM((3, 128, 128), F32), sems(3)],
        (cols, recv4, coarse_blocks, table),
    )
    recv5 = to_all(out5[:, None, :])[:, 0, :]
    vel_new, pres_new = call(
        last_kernel, "last", (shp(3, CX, CY, CZ), shp(CX, CY, CZ)),
        [VM] + [AN] * 9 + [VM],
        [pltpu.VMEM((3, CX, CY, CZ), F32), pltpu.VMEM((CX, CY, CZ), F32)]
        + [pltpu.VMEM((128, 128), F32), block(22), block(20), block(18), block(CX + 2), block(CX), block(20), block(20)]
        + [pltpu.VMEM((CX, CY, CZ), F32), pltpu.VMEM((2, CX, CY, CZ), F32), pltpu.VMEM((CX, CY, CZ), F32), block(2, 6), sems(9)],
        (recv5, corr1, codes, cxnear, cxfar, target, invp, pr0, free, pressure, glift.astype(BF16)),
        (AN, AN),
    )
    section_force = force.reshape(8)
    return vel_new, pres_new, section_force


def solution(mesh):
    fine = P("hullx", "hully", None)
    vector = P(None, "hullx", "hully", None)
    flat = P(BOTH)
    in_specs = (
        vector, fine, vector, fine, fine, fine,
        P("hully", None, None, None), P("hully", None),
        flat, flat, flat, flat, flat, P(BOTH, None), P(), flat, flat, flat,
    )
    return jax.shard_map(local, mesh=mesh, in_specs=in_specs, out_specs=(vector, fine, flat), check_vma=False)
```
